32 devices in a mesh: side: 2 (over x), row: 4 (over z), col: 4 (over y, core).
Axes of the slice: x: 2, y: 2, z: 4, core: 2. Of those that a mesh axis runs over, the one named last changes fastest.
Arguments:
- query: bfloat16 [2, 8, 4096], P(None, 'row'), may hold values from -32 to 32
- new_keys: bfloat16 [2, 8, 512], P(None, 'row'), may hold values from -6 to 6
- new_values: bfloat16 [2, 8, 512], P(None, 'row'), may hold values from -12 to 12
- key_cache: bfloat16 [8, 1536, 512], P('row', 'col'), may hold values from -4 to 4
- value_cache: bfloat16 [8, 1536, 512], P('row', 'col'), may hold values from -12 to 12
- lengths: int32 [8], P('row'), may hold values from 256 to 1536, as said below
- residual: bfloat16 [2, 8, 8192], P(None, None, 'row'), may hold values from -32 to 32
- out_weight: bfloat16 [4096, 8192], P('col', 'row'), may hold values from -0.5 to 0.5
- norm_gain: bfloat16 [8192], P('row'), may hold values from 0.099609375 to 1.8984375
- gate_weight: bfloat16 [8192, 14336], P('row', 'col'), may hold values from -0.0625 to 0.0625
- up_weight: bfloat16 [8192, 14336], P('row', 'col'), may hold values from -0.0625 to 0.0625
- down_weight: bfloat16 [14336, 8192], P('col', 'row'), may hold values from -0.046875 to 0.046875
Outputs:
- hidden_out: bfloat16 [2, 8, 8192], P(None, None, 'row')
The draws below stay inside these ranges and needn't reach their ends.
Inputs may be any that keep to these rules, and one draw needn't show every extreme that they name: `lengths`: every value from 256 to 1536 can occur; in every draw some row has exactly 1536 and some row exactly 256.
All inputs are finite; a program needn't handle non-finite values.
Results may differ from the reference program's by a relative error of at most 0.0059.
Values may be sent and summed in bfloat16 or wider, within the bound.
No kernel may reach another device: no remote copies, remote signals or barrier semaphores. Data moves between devices by JAX's collectives and lax.ppermute only.
A program may use at most 128 MiB of HBM per device.

```python
import math
import jax
import jax.numpy as jnp
from jax import lax

D = 8192
FF = 14336
HEADS = 32
KV_HEADS = 4
HD = 128
ROWS = 8
CAP = 1536
MINLEN = 256


def draw_lengths(key, part):
    key = jax.random.fold_in(key, 5)
    first, second = jax.random.split(key)
    drawn = jax.random.randint(first, (ROWS,), MINLEN, CAP + 1)
    order = jax.random.permutation(second, ROWS)
    drawn = drawn.at[order[0]].set(CAP)
    drawn = drawn.at[order[1]].set(MINLEN)
    return drawn.astype(jnp.int32)


def draw_key_cache(key, part):
    own = jax.random.fold_in(key, 11)
    base = jax.random.truncated_normal(own, -4.0, 4.0, (ROWS, CAP, KV_HEADS * HD), jnp.float32)
    return base.astype(jnp.bfloat16)


def draw_query(key, part):
    own = jax.random.fold_in(key, 12)
    base = jax.random.truncated_normal(own, -4.0, 4.0, (2, ROWS, HEADS * HD), jnp.float32)
    return base.astype(jnp.bfloat16)


def draw_residual(key, part):
    key = jax.random.fold_in(key, 7)
    first, second, third = jax.random.split(key, 3)
    ramp = jnp.arange(D, dtype=jnp.float32) / D
    rough = jnp.exp(jax.random.uniform(second, (D,), jnp.float32, -0.35, 0.35))
    values = jax.random.truncated_normal(first, -4.0, 4.0, (2, ROWS, D), jnp.float32)
    columns = 0.5 * jnp.exp(ramp * math.log(3.0)) * rough
    rows = 0.3 * jnp.exp(jax.random.uniform(third, (2, ROWS), jnp.float32, 0.0, math.log(10.0)))
    return (values * rows[:, :, None] * columns[None, None, :]).astype(jnp.bfloat16)


def shard_levels(stream_key, extent, cuts, least, high):
    gain = 1.0
    for axis_at, parts in cuts:
        heights = jax.random.uniform(jax.random.fold_in(jax.random.fold_in(stream_key, 6), axis_at), (parts,), jnp.float32, least / len(cuts), high / len(cuts))
        gain = gain * jnp.repeat(jnp.exp(heights), extent[axis_at] // parts).reshape((-1,) + (1,) * (len(extent) - 1 - axis_at))
    return gain


def gaussian(own_key, extent, width, limit, cuts=(), kind=jnp.bfloat16):
    array = width * jax.random.normal(own_key, extent, jnp.float32)
    if cuts:
        array = array * shard_levels(own_key, extent, cuts, -0.22, 0.18)
    return jnp.clip(array, -limit, limit).astype(kind)


def setup_inputs(seed: int = 0) -> dict:
    key_list = jax.random.split(jax.random.key(seed), 13)
    query = draw_query(jax.random.fold_in(key_list[12], 71), 0)
    new_keys = gaussian(key_list[1], (2, ROWS, KV_HEADS * HD), 1.0, 6.0, ((1, 4),))
    new_values = gaussian(key_list[2], (2, ROWS, KV_HEADS * HD), 2.0, 12.0, ((1, 4),))
    key_cache = draw_key_cache(jax.random.fold_in(key_list[12], 71), 0)
    value_cache = gaussian(key_list[4], (ROWS, CAP, KV_HEADS * HD), 2.0, 12.0, ((0, 4), (1, 4)))
    lengths = draw_lengths(jax.random.fold_in(key_list[12], 71), 0)
    residual = draw_residual(jax.random.fold_in(key_list[12], 71), 0)
    out_weight = gaussian(key_list[7], (HEADS * HD, D), HD ** -0.5, 0.5, ((0, 4), (1, 4)))
    norm_gain = jnp.clip(1.0 + 0.18 * jax.random.normal(key_list[8], (D,), jnp.float32), 0.099609375, 1.8984375).astype(jnp.bfloat16)
    gate_weight = gaussian(key_list[9], (D, FF), D ** -0.5, 0.0625, ((0, 4), (1, 4)))
    up_weight = gaussian(key_list[10], (D, FF), D ** -0.5, 0.0625, ((0, 4), (1, 4)))
    down_weight = gaussian(key_list[11], (FF, D), FF ** -0.5, 0.046875, ((0, 4), (1, 4)))
    return {"query": query, "new_keys": new_keys, "new_values": new_values, "key_cache": key_cache, "value_cache": value_cache, "lengths": lengths, "residual": residual, "out_weight": out_weight, "norm_gain": norm_gain, "gate_weight": gate_weight, "up_weight": up_weight, "down_weight": down_weight}


def reference(query, new_keys, new_values, key_cache, value_cache, lengths, residual, out_weight, norm_gain, gate_weight, up_weight, down_weight):
    group = HEADS // KV_HEADS
    inv_root = 1.0 / math.sqrt(HD)
    positions = jnp.arange(CAP, dtype=jnp.int32)
    live = positions[None, :] < lengths.astype(jnp.int32)[:, None]
    cached_keys = key_cache.astype(jnp.float32).reshape(ROWS, CAP, KV_HEADS, HD)
    cached_values = value_cache.astype(jnp.float32).reshape(ROWS, CAP, KV_HEADS, HD)
    finished = []
    for step in range(2):
        queries = query[step].astype(jnp.float32).reshape(ROWS, KV_HEADS, group, HD)
        cache_scores = jnp.einsum('bkgd,bpkd->bkgp', queries, cached_keys, precision=lax.Precision.HIGHEST) * inv_root
        cache_scores = jnp.where(live[:, None, None, :], cache_scores, -jnp.inf)
        fresh_keys = new_keys[:step + 1].astype(jnp.float32).reshape(step + 1, ROWS, KV_HEADS, HD)
        fresh_values = new_values[:step + 1].astype(jnp.float32).reshape(step + 1, ROWS, KV_HEADS, HD)
        fresh_scores = jnp.einsum('bkgd,tbkd->bkgt', queries, fresh_keys, precision=lax.Precision.HIGHEST) * inv_root
        top = jnp.maximum(lax.optimization_barrier(jnp.max(cache_scores, axis=-1)), lax.optimization_barrier(jnp.max(fresh_scores, axis=-1)))
        cache_weights = jnp.exp(cache_scores - top[..., None])
        fresh_weights = jnp.exp(fresh_scores - top[..., None])
        total = lax.optimization_barrier(jnp.sum(cache_weights, axis=-1)) + lax.optimization_barrier(jnp.sum(fresh_weights, axis=-1))
        summed = jnp.einsum('bkgp,bpkd->bkgd', cache_weights, cached_values, precision=lax.Precision.HIGHEST)
        summed = summed + jnp.einsum('bkgt,tbkd->bkgd', fresh_weights, fresh_values, precision=lax.Precision.HIGHEST)
        attended = (summed / total[..., None]).reshape(ROWS, HEADS * HD).astype(jnp.bfloat16)
        mid = residual[step].astype(jnp.float32) + jnp.dot(attended, out_weight, preferred_element_type=jnp.float32)
        inv = lax.rsqrt(lax.optimization_barrier(jnp.mean(mid * mid, axis=1, keepdims=True)) + 1e-05)
        lifted = (mid * norm_gain.astype(jnp.float32)).astype(jnp.bfloat16)
        gate = jnp.dot(lifted, gate_weight, preferred_element_type=jnp.float32) * inv
        up = jnp.dot(lifted, up_weight, preferred_element_type=jnp.float32) * inv
        act = (jax.nn.silu(gate) * up).astype(jnp.bfloat16)
        finished.append((mid + jnp.dot(act, down_weight, preferred_element_type=jnp.float32)).astype(jnp.bfloat16))
    return jnp.stack(finished)
```

```python
import functools
import math

import jax
import jax.numpy as jnp
from jax import lax
from jax.experimental import pallas as pl
from jax.experimental.pallas import tpu as pltpu
from jax.sharding import PartitionSpec as P

HEADS = 32
KV_HEADS = 4
HD = 128
GROUP = HEADS // KV_HEADS
TOKENS = 2
very_low = -1e30
MIB = 1024 * 1024
WIRE = jnp.bfloat16
VMEM_SPEC = pl.BlockSpec(memory_space=pltpu.VMEM)
ANY_SPEC = pl.BlockSpec(memory_space=pl.ANY)


def partner(value, axis, k):
    return lax.ppermute(value, axis, [(i, i ^ k) for i in range(lax.axis_size(axis))])


def spread(piece, axis):
    return [piece] + [partner(piece, axis, k) for k in range(1, lax.axis_size(axis))]


def dot(a, b):
    return jnp.dot(a, b, preferred_element_type=jnp.float32)


def dot_t(a, b):
    return lax.dot_general(a, b, (((1,), (1,)), ((), ())), preferred_element_type=jnp.float32)


def call(kernel, out_shape, in_specs, scratch=(), limit=4, name=None, flops=None):
    cost = None
    if flops is not None:
        cost = pl.CostEstimate(flops=flops, bytes_accessed=1024, transcendentals=0)
    return pl.pallas_call(
        kernel,
        out_shape=out_shape,
        in_specs=in_specs,
        out_specs=jax.tree.map(lambda _: VMEM_SPEC, out_shape),
        scratch_shapes=list(scratch),
        compiler_params=pltpu.CompilerParams(vmem_limit_bytes=limit * MIB),
        cost_estimate=cost,
        name=name,
    )


def in_hbm(value):
    return pltpu.with_memory_space_constraint(value, pltpu.HBM)


def in_vmem(value):
    return pltpu.with_memory_space_constraint(value, pltpu.VMEM)


def divide(blocks, bit, keep, send):
    for i in range(keep.shape[0]):
        keep[i] = blocks[2 * i + bit]
        send[i] = blocks[2 * i + 1 - bit]


def attention_kernel(cols, lengths, *rest):
    sources, (keep, send), held, (sized_ref, packed, sems) = rest[:5], rest[5:7], rest[7:12], rest[12:]
    sized = pltpu.make_async_copy(lengths, sized_ref, sems.at[5])
    sized.start()
    lengths = sized_ref
    copies = [
        pltpu.make_async_copy(source, target, sems.at[i])
        for i, (source, target) in enumerate(zip(sources, held))
    ]
    for copy in copies:
        copy.start()
    query, new_keys, new_values, keys, values = held
    column = lax.axis_index("col")
    rows, span, _ = keys.shape
    hb = HEADS // cols
    inv_root = 1.0 / math.sqrt(HD)
    n = TOKENS * GROUP
    pairs = [(b, g) for b in range(rows) for g in range(KV_HEADS)]
    for copy in [sized] + copies[:4]:
        copy.wait()
    q32 = query[...].astype(jnp.float32)
    nk, nv = new_keys[...].astype(jnp.float32), new_values[...].astype(jnp.float32)
    zeros = jnp.zeros((8 - TOKENS, HD), jnp.float32)

    def fresh(block, b, g):
        lanes = slice(g * HD, (g + 1) * HD)
        return jnp.concatenate([block[t, b : b + 1, lanes] for t in range(TOKENS)] + [zeros], axis=0)

    scores, fresh_scores = [], []
    for b, g in pairs:
        q = jnp.concatenate(
            [
                q32[t, b : b + 1, (g * GROUP + h) * HD : (g * GROUP + h + 1) * HD]
                for t in range(TOKENS)
                for h in range(GROUP)
            ],
            axis=0,
        ).astype(jnp.bfloat16)
        s = dot_t(q, keys[b, :, g * HD : (g + 1) * HD]) * inv_root
        position = column * span + lax.broadcasted_iota(jnp.int32, (n, span), 1)
        scores.append(jnp.where(position < lengths[b], s, very_low))
        f = dot_t(q, fresh(nk, b, g).astype(jnp.bfloat16)) * inv_root
        token = lax.broadcasted_iota(jnp.int32, (n, 8), 0) // GROUP
        slot = lax.broadcasted_iota(jnp.int32, (n, 8), 1)
        seen = jnp.logical_and(slot <= token, column == 0)
        fresh_scores.append(jnp.where(seen, f, very_low))
    scores = jnp.concatenate(scores, axis=0)
    fresh_scores = jnp.concatenate(fresh_scores, axis=0)
    peak = jnp.maximum(
        jnp.max(scores, axis=1, keepdims=True), jnp.max(fresh_scores, axis=1, keepdims=True)
    )
    weights = jnp.where(scores > 0.5 * very_low, jnp.exp(scores - peak), 0.0)
    fresh_weights = jnp.where(fresh_scores > 0.5 * very_low, jnp.exp(fresh_scores - peak), 0.0)
    total = jnp.sum(weights, axis=1, keepdims=True) + jnp.sum(fresh_weights, axis=1, keepdims=True)

    def halves(w):
        high = w.astype(jnp.bfloat16)
        low = (w - high.astype(jnp.float32)).astype(jnp.bfloat16)
        return jnp.concatenate([high, low], axis=0)

    lane = lax.broadcasted_iota(jnp.int32, (GROUP, HD), 1)
    stats = [jnp.zeros((GROUP, HD), jnp.float32) for _ in range(KV_HEADS)]
    copies[4].wait()
    for i, (b, g) in enumerate(pairs):
        here = slice(i * n, (i + 1) * n)
        s = dot(halves(weights[here]), values[b, :, g * HD : (g + 1) * HD])
        s = s + dot(halves(fresh_weights[here]), fresh(nv, b, g).astype(jnp.bfloat16))
        s = s[:n] + s[n:]
        for t in range(TOKENS):
            tb = t * rows + b
            part = slice(i * n + t * GROUP, i * n + (t + 1) * GROUP)
            stats[g] = jnp.where(lane == 2 * tb, peak[part], stats[g])
            stats[g] = jnp.where(lane == 2 * tb + 1, total[part], stats[g])
            block = s[t * GROUP : (t + 1) * GROUP]
            if hb >= GROUP:
                at = g * GROUP
                packed[at // hb, tb, at % hb : at % hb + GROUP] = block
            else:
                for j in range(GROUP // hb):
                    packed[g * (GROUP // hb) + j, tb] = block[j * hb : (j + 1) * hb]
    for g in range(KV_HEADS):
        if hb >= GROUP:
            at = g * GROUP
            packed[at // hb, TOKENS * rows, at % hb : at % hb + GROUP] = stats[g]
        else:
            for j in range(GROUP // hb):
                packed[g * (GROUP // hb) + j, TOKENS * rows] = stats[g][j * hb : (j + 1) * hb]
    divide(packed, column & 1, keep, send)


def joined(first, second, i):
    cells = first.shape[1] - 1
    result = []
    for tb in range(cells):
        stats = [p[i, cells] for p in (first, second)]
        peak_a, peak_b = (s[:, 2 * tb : 2 * tb + 1] for s in stats)
        total_a, total_b = (s[:, 2 * tb + 1 : 2 * tb + 2] for s in stats)
        peak = jnp.maximum(peak_a, peak_b)
        scale_a, scale_b = jnp.exp(peak_a - peak), jnp.exp(peak_b - peak)
        total = total_a * scale_a + total_b * scale_b
        result.append((first[i, tb] * scale_a + second[i, tb] * scale_b, total, peak))
    return result


def merge_kernel(level, kept, received, keep, send, packed):
    lane = lax.broadcasted_iota(jnp.int32, kept.shape[2:], 1)
    for i in range(kept.shape[0]):
        stats = jnp.zeros(kept.shape[2:], jnp.float32)
        result = joined(kept, received, i)
        for tb, (summed, total, peak) in enumerate(result):
            packed[i, tb] = summed
            stats = jnp.where(lane == 2 * tb, peak, stats)
            stats = jnp.where(lane == 2 * tb + 1, total, stats)
        packed[i, len(result)] = stats
    divide(packed, (lax.axis_index("col") >> level) & 1, keep, send)


def attended_kernel(kept, received, out):
    attended = [summed / total for summed, total, _ in joined(kept, received, 0)]
    rows = [
        jnp.concatenate([a[h : h + 1] for a in attended], axis=0) for h in range(kept.shape[2])
    ]
    out[...] = jnp.concatenate(rows, axis=1).astype(out.dtype)


def add_kernel(first, second, out):
    out[...] = (first[...].astype(jnp.float32) + second[...].astype(jnp.float32)).astype(out.dtype)


def group_order(value, groups):
    here = value.shape[1] // groups
    return jnp.concatenate(
        [value[t, r * here : (r + 1) * here] for r in range(groups) for t in range(TOKENS)], axis=0
    )


def canonical(parts, canon, me):
    cells = parts[0].shape[0]
    for k, part in enumerate(parts):
        canon[jnp.bitwise_xor(me, k), :cells] = part[...].astype(jnp.float32)
    rows = [canon[r, :cells] for r in range(len(parts))]
    return jnp.concatenate(rows, axis=0).astype(jnp.bfloat16)


def over_columns(width, body):
    size = width // 2 if width % 256 == 0 else width

    def step(j, carry):
        body(pl.multiple_of(j * size, 128), size)
        return carry

    lax.fori_loop(0, width // size, step, 0)


def out_kernel(groups, *refs):
    parts, (weight, out, canon, attended) = refs[:groups], refs[groups:]
    attended[...] = canonical(parts, canon, lax.axis_index("row"))

    def body(at, size):
        out[:, pl.ds(at, size)] = dot(attended[...], weight[:, pl.ds(at, size)]).astype(out.dtype)

    over_columns(out.shape[1], body)


def in_pieces(squares):
    first = squares.astype(WIRE).astype(jnp.float32)
    second = (squares - first).astype(WIRE).astype(jnp.float32)
    third = squares - first - second
    lane = lax.broadcasted_iota(jnp.int32, (squares.shape[0], HD), 1)
    return jnp.where(
        lane == 0, first, jnp.where(lane == 1, second, jnp.where(lane == 2, third, 0.0))
    )


def lift_kernel(groups, split, residual, gains, gate_weight, up_weight, first, second, *refs):
    mid_out, keep, send, lifted, packed = refs
    hidden = gate_weight.shape[1] // split
    start = lax.axis_index("side") * hidden if split > 1 else 0
    half = packed.shape[1] // 2
    mid = first[...].astype(jnp.float32) + second[...].astype(jnp.float32)
    mid = group_order(residual[...].astype(jnp.float32), groups) + mid
    mid_out[...] = mid
    sent = in_pieces(jnp.sum(mid * mid, axis=1, keepdims=True))
    lifted[...] = (mid * gains[...].astype(jnp.float32).reshape(1, mid.shape[1])).astype(jnp.bfloat16)
    for i in range(2):
        piece = sent[i * half : (i + 1) * half]
        packed[i, :, hidden:] = jnp.concatenate([piece, piece], axis=0)

    def body(at, size):
        block = pl.ds(pl.multiple_of(start + at, 128), size)
        gate = dot(lifted[...], gate_weight[:, block])
        up = dot(lifted[...], up_weight[:, block])
        for i in range(2):
            rows = slice(i * half, (i + 1) * half)
            packed[i, :, pl.ds(at, size)] = jnp.concatenate([gate[rows], up[rows]], axis=0)

    over_columns(hidden, body)
    bit = lax.axis_index("row") & 1
    keep[...] = packed[bit].astype(keep.dtype)
    send[...] = packed[1 - bit].astype(send.dtype)


def sum_kernel(first, second, out):
    hidden = out.shape[1] - HD
    total = first[...].astype(jnp.float32) + second[...].astype(jnp.float32)
    out[:, :hidden] = total[:, :hidden].astype(out.dtype)
    squares = jnp.sum(total[:, hidden:], axis=1, keepdims=True)
    out[:, hidden:] = in_pieces(squares).astype(out.dtype)


def act_kernel(model, first, second, out):
    hidden = first.shape[1] - HD
    cells = first.shape[0] // 2
    total = first[...].astype(jnp.float32) + second[...].astype(jnp.float32)
    squares = jnp.sum(total[:cells, hidden:], axis=1, keepdims=True)
    inv = lax.rsqrt(squares / model + 1e-05)
    gate = total[:cells, :hidden] * inv
    up = total[cells:, :hidden] * inv
    out[...] = (gate / (1.0 + jnp.exp(-gate)) * up).astype(out.dtype)


def gather_kernel(own, received, out, packed):
    bit = lax.axis_index("row") & 1
    packed[bit] = own[...].astype(jnp.float32)
    packed[1 - bit] = received[...].astype(jnp.float32)
    out[...] = jnp.concatenate([packed[0], packed[1]], axis=0).astype(out.dtype)


def down_kernel(other, act, weight, *refs):
    out = refs[-1]
    hidden = act.shape[1]
    start = 0
    if weight.shape[0] > hidden:
        start = pl.multiple_of(jnp.bitwise_xor(lax.axis_index("side"), other) * hidden, 128)

    def body(at, size):
        product = dot(act[...], weight[pl.ds(start, hidden), pl.ds(at, size)])
        if len(refs) > 1:
            product = product + refs[0][:, pl.ds(at, size)]
        out[:, pl.ds(at, size)] = product.astype(out.dtype)

    over_columns(out.shape[1], body)


def final_kernel(groups, mid, first, second, out):
    total = first[...].astype(jnp.float32) + second[...].astype(jnp.float32)
    total = mid[...] + total
    here = out.shape[1] // groups
    for t in range(TOKENS):
        block = [
            total[(r * TOKENS + t) * here : (r * TOKENS + t + 1) * here] for r in range(groups)
        ]
        out[t] = jnp.concatenate(block, axis=0).astype(out.dtype)


def shards(
    query,
    new_keys,
    new_values,
    key_cache,
    value_cache,
    lengths,
    residual,
    out_weight,
    norm_gain,
    gate_weight,
    up_weight,
    down_weight,
):
    sides, groups, cols = (lax.axis_size(a) for a in ("side", "row", "col"))
    rows_here = key_cache.shape[0]
    total_rows = residual.shape[1]
    width_share = residual.shape[2]
    hidden_share = gate_weight.shape[1]
    features = out_weight.shape[0]
    model = width_share * groups
    m = TOKENS * total_rows
    cells = TOKENS * rows_here
    hb = HEADS // cols
    split = 2 if sides == 2 and (hidden_share // 2) % 128 == 0 else 1
    hidden = hidden_share // split
    f32, bf16 = jnp.float32, jnp.bfloat16
    shape = jax.ShapeDtypeStruct
    pad = -(-cells // 8) * 8

    def halves(n):
        return [shape((n // 2, cells + 1, hb, HD), f32)] * 2

    sources = [query, new_keys, new_values, key_cache, value_cache]
    keep, send = call(
        functools.partial(attention_kernel, cols),
        halves(cols),
        [ANY_SPEC] * 6,
        [pltpu.VMEM(a.shape, a.dtype) for a in sources]
        + [pltpu.SMEM(lengths.shape, lengths.dtype)]
        + [pltpu.VMEM((cols, cells + 1, hb, HD), f32), pltpu.SemaphoreType.DMA((6,))],
        flops=40 * 10**9,
        name="attention",
    )(*[in_hbm(a) for a in [lengths, *sources]])
    for level in range(1, cols.bit_length() - 1):
        received = partner(send, "col", 1 << (level - 1))
        n = cols >> level
        keep, send = call(
            functools.partial(merge_kernel, level),
            halves(n),
            [VMEM_SPEC] * 2,
            [pltpu.VMEM((n, cells + 1, hb, HD), f32)],
            name="merge",
        )(keep, received)
    attended = call(
        attended_kernel,
        shape((cells, features), bf16),
        [VMEM_SPEC] * 2,
        name="attended",
    )(keep, partner(send, "col", cols // 2))
    gathered = spread(attended, "row")
    partial = call(
        functools.partial(out_kernel, groups),
        shape((m, width_share), WIRE),
        [VMEM_SPEC] * (groups + 1),
        [pltpu.VMEM((groups, pad, features), f32), pltpu.VMEM((m, features), bf16)],
        name="out_projection",
    )(*gathered, in_vmem(out_weight))

    def sum_of_columns(value):
        for level in range(cols.bit_length() - 2):
            value = call(
                add_kernel,
                shape(value.shape, WIRE),
                [VMEM_SPEC] * 2,
                name="add",
            )(value, partner(value, "col", 1 << level))
        return value, partner(value, "col", cols // 2)

    mid, keep, send = call(
        functools.partial(lift_kernel, groups, split),
        [shape((m, width_share), f32)] + [shape((m, hidden + HD), WIRE)] * 2,
        [VMEM_SPEC] * 6,
        [pltpu.VMEM((m, width_share), bf16), pltpu.VMEM((2, m, hidden + HD), f32)],
        name="gate_up",
    )(
        in_vmem(residual), in_vmem(norm_gain), in_vmem(gate_weight), in_vmem(up_weight),
        *sum_of_columns(partial),
    )
    received = partner(send, "row", 1)
    for level in range(1, groups.bit_length() - 1):
        keep = call(
            sum_kernel,
            shape(keep.shape, WIRE),
            [VMEM_SPEC] * 2,
            name="gate_up_sum",
        )(keep, received)
        received = partner(keep, "row", 1 << level)
    act = call(
        functools.partial(act_kernel, model),
        shape((m // 2, hidden), bf16),
        [VMEM_SPEC] * 2,
        name="activation",
    )(keep, received)
    own = call(
        gather_kernel,
        shape((m, hidden), bf16),
        [VMEM_SPEC] * 2,
        [pltpu.VMEM((2, m // 2, hidden), f32)],
        name="gather_act",
    )(act, partner(act, "row", 1))
    down_weight = in_vmem(down_weight)
    first = call(
        functools.partial(down_kernel, 0),
        shape((m, width_share), f32 if split > 1 else WIRE),
        [VMEM_SPEC] * 2,
        name="down_first",
    )(own, down_weight)
    down = first
    if split > 1:
        crossed = partner(own, "side", 1)
        down = call(
            functools.partial(down_kernel, 1),
            shape((m, width_share), WIRE),
            [VMEM_SPEC] * 3,
            name="down_second",
        )(crossed, down_weight, first)
    return call(
        functools.partial(final_kernel, groups),
        shape((TOKENS, total_rows, width_share), bf16),
        [VMEM_SPEC] * 3,
        name="final",
    )(mid, *sum_of_columns(down))


def solution(mesh):
    in_specs = (
        P(None, "row", None),
        P(None, "row", None),
        P(None, "row", None),
        P("row", "col", None),
        P("row", "col", None),
        P("row"),
        P(None, None, "row"),
        P("col", "row"),
        P("row"),
        P("row", "col"),
        P("row", "col"),
        P("col", "row"),
    )
    out_specs = P(None, None, "row")
    return jax.shard_map(shards, mesh=mesh, in_specs=in_specs, out_specs=out_specs, check_vma=False)
```

```python
import functools
import math

import jax
import jax.numpy as jnp
from jax import lax
from jax.experimental import pallas as pl
from jax.experimental.pallas import tpu as pltpu
from jax.sharding import PartitionSpec as P

HEADS = 32
KV_HEADS = 4
HD = 128
GROUP = HEADS // KV_HEADS
TOKENS = 2
very_low = -1e30
MIB = 1024 * 1024
WIRE = jnp.bfloat16
VMEM_SPEC = pl.BlockSpec(memory_space=pltpu.VMEM)
ANY_SPEC = pl.BlockSpec(memory_space=pl.ANY)


def partner(value, axis, k):
    return lax.ppermute(value, axis, [(i, i ^ k) for i in range(lax.axis_size(axis))])


def spread(piece, axis):
    return [piece] + [partner(piece, axis, k) for k in reversed(range(1, lax.axis_size(axis)))]


def by_distance(pieces):
    return pieces[:1] + pieces[:0:-1]


def tree_sum(values):
    while len(values) > 1:
        values = [values[i] + values[i + 1] for i in range(0, len(values), 2)]
    return values[0]


def dot(a, b):
    return jnp.dot(a, b, preferred_element_type=jnp.float32)


def dot_t(a, b):
    return lax.dot_general(a, b, (((1,), (1,)), ((), ())), preferred_element_type=jnp.float32)


def call(kernel, out_shape, in_specs, scratch=(), limit=4, name=None, flops=None):
    cost = None
    if flops is not None:
        cost = pl.CostEstimate(flops=flops, bytes_accessed=1024, transcendentals=0)
    return pl.pallas_call(
        kernel,
        out_shape=out_shape,
        in_specs=in_specs,
        out_specs=jax.tree.map(lambda _: VMEM_SPEC, out_shape),
        scratch_shapes=list(scratch),
        compiler_params=pltpu.CompilerParams(vmem_limit_bytes=limit * MIB),
        cost_estimate=cost,
        name=name,
    )


def in_hbm(value):
    return pltpu.with_memory_space_constraint(value, pltpu.HBM)


def in_vmem(value):
    return pltpu.with_memory_space_constraint(value, pltpu.VMEM)


def attention_kernel(cols, lengths, *rest):
    sources, outs = rest[:5], rest[5 : 5 + cols]
    held, (sized_ref, packed, sems) = rest[5 + cols : 10 + cols], rest[10 + cols :]
    sized = pltpu.make_async_copy(lengths, sized_ref, sems.at[5])
    sized.start()
    lengths = sized_ref
    copies = [
        pltpu.make_async_copy(source, target, sems.at[i])
        for i, (source, target) in enumerate(zip(sources, held))
    ]
    for copy in copies:
        copy.start()
    query, new_keys, new_values, keys, values = held
    column = lax.axis_index("col")
    rows, span, _ = keys.shape
    hb = HEADS // cols
    inv_root = 1.0 / math.sqrt(HD)
    n = TOKENS * GROUP
    pairs = [(b, g) for b in range(rows) for g in range(KV_HEADS)]
    for copy in [sized] + copies[:4]:
        copy.wait()
    q32 = query[...].astype(jnp.float32)
    nk, nv = new_keys[...].astype(jnp.float32), new_values[...].astype(jnp.float32)
    zeros = jnp.zeros((8 - TOKENS, HD), jnp.float32)

    def fresh(block, b, g):
        lanes = slice(g * HD, (g + 1) * HD)
        return jnp.concatenate([block[t, b : b + 1, lanes] for t in range(TOKENS)] + [zeros], axis=0)

    scores, fresh_scores = [], []
    for b, g in pairs:
        q = jnp.concatenate(
            [
                q32[t, b : b + 1, (g * GROUP + h) * HD : (g * GROUP + h + 1) * HD]
                for t in range(TOKENS)
                for h in range(GROUP)
            ],
            axis=0,
        ).astype(jnp.bfloat16)
        s = dot_t(q, keys[b, :, g * HD : (g + 1) * HD]) * inv_root
        position = column * span + lax.broadcasted_iota(jnp.int32, (n, span), 1)
        scores.append(jnp.where(position < lengths[b], s, very_low))
        f = dot_t(q, fresh(nk, b, g).astype(jnp.bfloat16)) * inv_root
        token = lax.broadcasted_iota(jnp.int32, (n, 8), 0) // GROUP
        slot = lax.broadcasted_iota(jnp.int32, (n, 8), 1)
        seen = jnp.logical_and(slot <= token, column == 0)
        fresh_scores.append(jnp.where(seen, f, very_low))
    scores = jnp.concatenate(scores, axis=0)
    fresh_scores = jnp.concatenate(fresh_scores, axis=0)
    peak = jnp.maximum(
        jnp.max(scores, axis=1, keepdims=True), jnp.max(fresh_scores, axis=1, keepdims=True)
    )
    weights = jnp.where(scores > 0.5 * very_low, jnp.exp(scores - peak), 0.0)
    fresh_weights = jnp.where(fresh_scores > 0.5 * very_low, jnp.exp(fresh_scores - peak), 0.0)
    total = jnp.sum(weights, axis=1, keepdims=True) + jnp.sum(fresh_weights, axis=1, keepdims=True)

    def halves(w):
        high = w.astype(jnp.bfloat16)
        low = (w - high.astype(jnp.float32)).astype(jnp.bfloat16)
        return jnp.concatenate([high, low], axis=0)

    lane = lax.broadcasted_iota(jnp.int32, (GROUP, HD), 1)
    stats = [jnp.zeros((GROUP, HD), jnp.float32) for _ in range(KV_HEADS)]
    copies[4].wait()
    for i, (b, g) in enumerate(pairs):
        here = slice(i * n, (i + 1) * n)
        s = dot(halves(weights[here]), values[b, :, g * HD : (g + 1) * HD])
        s = s + dot(halves(fresh_weights[here]), fresh(nv, b, g).astype(jnp.bfloat16))
        s = s[:n] + s[n:]
        for t in range(TOKENS):
            tb = t * rows + b
            part = slice(i * n + t * GROUP, i * n + (t + 1) * GROUP)
            stats[g] = jnp.where(lane == 2 * tb, peak[part], stats[g])
            stats[g] = jnp.where(lane == 2 * tb + 1, total[part], stats[g])
            block = s[t * GROUP : (t + 1) * GROUP]
            if hb >= GROUP:
                at = g * GROUP
                packed[at // hb, tb, at % hb : at % hb + GROUP] = block
            else:
                for j in range(GROUP // hb):
                    packed[g * (GROUP // hb) + j, tb] = block[j * hb : (j + 1) * hb]
    for g in range(KV_HEADS):
        if hb >= GROUP:
            at = g * GROUP
            packed[at // hb, TOKENS * rows, at % hb : at % hb + GROUP] = stats[g]
        else:
            for j in range(GROUP // hb):
                packed[g * (GROUP // hb) + j, TOKENS * rows] = stats[g][j * hb : (j + 1) * hb]
    for k in range(cols):
        outs[k][...] = packed[jnp.bitwise_xor(column, k)]


def combine_kernel(cols, *refs):
    parts, out = refs[:cols], refs[cols]
    cells = parts[0].shape[0] - 1
    hb = parts[0].shape[1]
    stats = [p[cells] for p in parts]
    attended = []
    for tb in range(cells):
        peaks = [s[:, 2 * tb : 2 * tb + 1] for s in stats]
        totals = [s[:, 2 * tb + 1 : 2 * tb + 2] for s in stats]
        top = functools.reduce(jnp.maximum, peaks)
        scales = [jnp.exp(p - top) for p in peaks]
        total = tree_sum([t * s for t, s in zip(totals, scales)])
        summed = tree_sum([p[tb] * s for p, s in zip(parts, scales)])
        attended.append(summed / total)
    rows = [
        jnp.concatenate([attended[tb][h : h + 1] for tb in range(cells)], axis=0) for h in range(hb)
    ]
    out[...] = jnp.concatenate(rows, axis=1).astype(out.dtype)


def group_order(value, groups):
    here = value.shape[1] // groups
    return jnp.concatenate(
        [value[t, r * here : (r + 1) * here] for r in range(groups) for t in range(TOKENS)], axis=0
    )


def canonical(parts, canon, me):
    cells = parts[0].shape[0]
    for k, part in enumerate(parts):
        canon[jnp.bitwise_xor(me, k), :cells] = part[...].astype(jnp.float32)
    rows = [canon[r, :cells] for r in range(len(parts))]
    return jnp.concatenate(rows, axis=0).astype(jnp.bfloat16)


def over_columns(width, body):
    size = width // 2 if width % 256 == 0 else width

    def step(j, carry):
        body(pl.multiple_of(j * size, 128), size)
        return carry

    lax.fori_loop(0, width // size, step, 0)


def out_kernel(groups, *refs):
    parts, (weight, out, canon, attended) = by_distance(refs[:groups]), refs[groups:]
    attended[...] = canonical(parts, canon, lax.axis_index("row"))

    def body(at, size):
        out[:, pl.ds(at, size)] = dot(attended[...], weight[:, pl.ds(at, size)]).astype(out.dtype)

    over_columns(out.shape[1], body)


def in_pieces(squares):
    first = squares.astype(WIRE).astype(jnp.float32)
    second = (squares - first).astype(WIRE).astype(jnp.float32)
    third = squares - first - second
    lane = lax.broadcasted_iota(jnp.int32, (squares.shape[0], HD), 1)
    return jnp.where(
        lane == 0, first, jnp.where(lane == 1, second, jnp.where(lane == 2, third, 0.0))
    )


def lift_kernel(groups, split, residual, gains, gate_weight, up_weight, *refs):
    parts, (mid_out, out, lifted) = by_distance(refs[:-3]), refs[-3:]
    hidden = gate_weight.shape[1] // split
    start = lax.axis_index("side") * hidden if split > 1 else 0
    mid = tree_sum([p[...].astype(jnp.float32) for p in parts])
    mid = group_order(residual[...].astype(jnp.float32), groups) + mid
    mid_out[...] = mid
    sent = in_pieces(jnp.sum(mid * mid, axis=1, keepdims=True))
    lifted[...] = (mid * gains[...].astype(jnp.float32).reshape(1, mid.shape[1])).astype(jnp.bfloat16)
    out[:, hidden:] = jnp.concatenate([sent, sent], axis=0).astype(out.dtype)

    def body(at, size):
        block = pl.ds(pl.multiple_of(start + at, 128), size)
        gate = dot(lifted[...], gate_weight[:, block])
        up = dot(lifted[...], up_weight[:, block])
        both = jnp.concatenate([gate, up], axis=0)
        out[:, pl.ds(at, size)] = both.astype(out.dtype)

    over_columns(hidden, body)


def sum_kernel(first, second, out):
    hidden = out.shape[1] - HD
    total = first[...].astype(jnp.float32) + second[...].astype(jnp.float32)
    out[:, :hidden] = total[:, :hidden].astype(out.dtype)
    squares = jnp.sum(total[:, hidden:], axis=1, keepdims=True)
    out[:, hidden:] = in_pieces(squares).astype(out.dtype)


def act_kernel(model, first, second, out):
    hidden = first.shape[1] - HD
    cells = first.shape[0] // 2
    total = first[...].astype(jnp.float32) + second[...].astype(jnp.float32)
    squares = jnp.sum(total[:cells, hidden:], axis=1, keepdims=True)
    inv = lax.rsqrt(squares / model + 1e-05)
    gate = total[:cells, :hidden] * inv
    up = total[cells:, :hidden] * inv
    out[...] = (gate / (1.0 + jnp.exp(-gate)) * up).astype(out.dtype)


def down_kernel(other, act, weight, *refs):
    out = refs[-1]
    hidden = act.shape[1]
    start = 0
    if weight.shape[0] > hidden:
        start = pl.multiple_of(jnp.bitwise_xor(lax.axis_index("side"), other) * hidden, 128)

    def body(at, size):
        product = dot(act[...], weight[pl.ds(start, hidden), pl.ds(at, size)])
        if len(refs) > 1:
            product = product + refs[0][:, pl.ds(at, size)]
        out[:, pl.ds(at, size)] = product.astype(out.dtype)

    over_columns(out.shape[1], body)


def final_kernel(groups, mid, *refs):
    parts, out = by_distance(refs[:-1]), refs[-1]
    total = mid[...] + tree_sum([p[...].astype(jnp.float32) for p in parts])
    here = out.shape[1] // groups
    for t in range(TOKENS):
        block = [
            total[(r * TOKENS + t) * here : (r * TOKENS + t + 1) * here] for r in range(groups)
        ]
        out[t] = jnp.concatenate(block, axis=0).astype(out.dtype)


def shards(
    query,
    new_keys,
    new_values,
    key_cache,
    value_cache,
    lengths,
    residual,
    out_weight,
    norm_gain,
    gate_weight,
    up_weight,
    down_weight,
):
    sides, groups, cols = (lax.axis_size(a) for a in ("side", "row", "col"))
    rows_here = key_cache.shape[0]
    total_rows = residual.shape[1]
    width_share = residual.shape[2]
    hidden_share = gate_weight.shape[1]
    features = out_weight.shape[0]
    model = width_share * groups
    m = TOKENS * total_rows
    cells = TOKENS * rows_here
    hb = HEADS // cols
    split = 2 if sides == 2 and (hidden_share // 2) % 128 == 0 else 1
    hidden = hidden_share // split
    f32, bf16 = jnp.float32, jnp.bfloat16
    shape = jax.ShapeDtypeStruct
    pad = -(-cells // 8) * 8

    sources = [query, new_keys, new_values, key_cache, value_cache]
    message = shape((cells + 1, hb, HD), f32)
    parts = call(
        functools.partial(attention_kernel, cols),
        [message] * cols,
        [ANY_SPEC] * 6,
        [pltpu.VMEM(a.shape, a.dtype) for a in sources]
        + [pltpu.SMEM(lengths.shape, lengths.dtype)]
        + [pltpu.VMEM((cols, cells + 1, hb, HD), f32), pltpu.SemaphoreType.DMA((6,))],
        flops=40 * 10**9,
        name="attention",
    )(*[in_hbm(a) for a in [lengths, *sources]])
    parts = [parts[0]] + [partner(parts[k], "col", k) for k in range(1, cols)]
    attended = call(
        functools.partial(combine_kernel, cols),
        shape((cells, features), bf16),
        [VMEM_SPEC] * cols,
        name="combine",
    )(*parts)
    gathered = spread(attended, "row")
    partial = call(
        functools.partial(out_kernel, groups),
        shape((m, width_share), WIRE),
        [VMEM_SPEC] * (groups + 1),
        [pltpu.VMEM((groups, pad, features), f32), pltpu.VMEM((m, features), bf16)],
        name="out_projection",
    )(*gathered, in_vmem(out_weight))
    mid, value = call(
        functools.partial(lift_kernel, groups, split),
        [shape((m, width_share), f32), shape((2 * m, hidden + HD), WIRE)],
        [VMEM_SPEC] * (cols + 4),
        [pltpu.VMEM((m, width_share), bf16)],
        name="gate_up",
    )(
        in_vmem(residual), in_vmem(norm_gain), in_vmem(gate_weight), in_vmem(up_weight),
        *spread(partial, "col"),
    )
    last = groups // 2
    for level in range(groups.bit_length() - 2):
        value = call(
            sum_kernel,
            shape(value.shape, WIRE),
            [VMEM_SPEC] * 2,
            name="gate_up_sum",
        )(value, partner(value, "row", 1 << level))

    def activation(first, second):
        return call(
            functools.partial(act_kernel, model),
            shape((m, hidden), bf16),
            [VMEM_SPEC] * 2,
            name="activation",
        )(first, second)

    own = activation(value, partner(value, "row", last))
    down_weight = in_vmem(down_weight)
    first = call(
        functools.partial(down_kernel, 0),
        shape((m, width_share), f32 if split > 1 else WIRE),
        [VMEM_SPEC] * 2,
        name="down_first",
    )(own, down_weight)
    down = first
    if split > 1:
        crossed = activation(
            partner(value, "side", 1), partner(value, ("side", "row"), groups + last)
        )
        down = call(
            functools.partial(down_kernel, 1),
            shape((m, width_share), WIRE),
            [VMEM_SPEC] * 3,
            name="down_second",
        )(crossed, down_weight, first)
    return call(
        functools.partial(final_kernel, groups),
        shape((TOKENS, total_rows, width_share), bf16),
        [VMEM_SPEC] * (cols + 1),
        name="final",
    )(mid, *spread(down, "col"))


def solution(mesh):
    in_specs = (
        P(None, "row", None),
        P(None, "row", None),
        P(None, "row", None),
        P("row", "col", None),
        P("row", "col", None),
        P("row"),
        P(None, None, "row"),
        P("col", "row"),
        P("row"),
        P("row", "col"),
        P("row", "col"),
        P("col", "row"),
    )
    out_specs = P(None, None, "row")
    return jax.shard_map(shards, mesh=mesh, in_specs=in_specs, out_specs=out_specs, check_vma=False)
```

```python
import functools
import math

import jax
import jax.numpy as jnp
from jax import lax
from jax.experimental import pallas as pl
from jax.experimental.pallas import tpu as pltpu
from jax.sharding import PartitionSpec as P

HEADS = 32
KV_HEADS = 4
HD = 128
GROUP = HEADS // KV_HEADS
TOKENS = 2
very_low = -1e30
MIB = 1024 * 1024
WIRE = jnp.bfloat16
VMEM_SPEC = pl.BlockSpec(memory_space=pltpu.VMEM)
ANY_SPEC = pl.BlockSpec(memory_space=pl.ANY)


def partner(value, axis, k):
    return lax.ppermute(value, axis, [(i, i ^ k) for i in range(lax.axis_size(axis))])


def spread(piece, axis):
    return [piece] + [partner(piece, axis, k) for k in range(1, lax.axis_size(axis))]


def tree_sum(values):
    while len(values) > 1:
        values = [values[i] + values[i + 1] for i in range(0, len(values), 2)]
    return values[0]


def dot(a, b):
    return jnp.dot(a, b, preferred_element_type=jnp.float32)


def dot_t(a, b):
    return lax.dot_general(a, b, (((1,), (1,)), ((), ())), preferred_element_type=jnp.float32)


def call(kernel, out_shape, in_specs, scratch=(), limit=4, name=None, flops=None):
    cost = None
    if flops is not None:
        cost = pl.CostEstimate(flops=flops, bytes_accessed=1024, transcendentals=0)
    return pl.pallas_call(
        kernel,
        out_shape=out_shape,
        in_specs=in_specs,
        out_specs=jax.tree.map(lambda _: VMEM_SPEC, out_shape),
        scratch_shapes=list(scratch),
        compiler_params=pltpu.CompilerParams(vmem_limit_bytes=limit * MIB),
        cost_estimate=cost,
        name=name,
    )


def in_hbm(value):
    return pltpu.with_memory_space_constraint(value, pltpu.HBM)


def in_vmem(value):
    return pltpu.with_memory_space_constraint(value, pltpu.VMEM)


def attention_kernel(cols, lengths, *rest):
    sources, outs = rest[:5], rest[5 : 5 + cols]
    held, (sized_ref, packed, sems) = rest[5 + cols : 10 + cols], rest[10 + cols :]
    sized = pltpu.make_async_copy(lengths, sized_ref, sems.at[5])
    sized.start()
    lengths = sized_ref
    copies = [
        pltpu.make_async_copy(source, target, sems.at[i])
        for i, (source, target) in enumerate(zip(sources, held))
    ]
    for copy in copies:
        copy.start()
    query, new_keys, new_values, keys, values = held
    column = lax.axis_index("col")
    rows, span, _ = keys.shape
    hb = HEADS // cols
    inv_root = 1.0 / math.sqrt(HD)
    n = TOKENS * GROUP
    pairs = [(b, g) for b in range(rows) for g in range(KV_HEADS)]
    for copy in [sized] + copies[:4]:
        copy.wait()
    q32 = query[...].astype(jnp.float32)
    nk, nv = new_keys[...].astype(jnp.float32), new_values[...].astype(jnp.float32)
    zeros = jnp.zeros((8 - TOKENS, HD), jnp.float32)

    def fresh(block, b, g):
        lanes = slice(g * HD, (g + 1) * HD)
        return jnp.concatenate([block[t, b : b + 1, lanes] for t in range(TOKENS)] + [zeros], axis=0)

    scores, fresh_scores = [], []
    for b, g in pairs:
        q = jnp.concatenate(
            [
                q32[t, b : b + 1, (g * GROUP + h) * HD : (g * GROUP + h + 1) * HD]
                for t in range(TOKENS)
                for h in range(GROUP)
            ],
            axis=0,
        ).astype(jnp.bfloat16)
        s = dot_t(q, keys[b, :, g * HD : (g + 1) * HD]) * inv_root
        position = column * span + lax.broadcasted_iota(jnp.int32, (n, span), 1)
        scores.append(jnp.where(position < lengths[b], s, very_low))
        f = dot_t(q, fresh(nk, b, g).astype(jnp.bfloat16)) * inv_root
        token = lax.broadcasted_iota(jnp.int32, (n, 8), 0) // GROUP
        slot = lax.broadcasted_iota(jnp.int32, (n, 8), 1)
        seen = jnp.logical_and(slot <= token, column == 0)
        fresh_scores.append(jnp.where(seen, f, very_low))
    scores = jnp.concatenate(scores, axis=0)
    fresh_scores = jnp.concatenate(fresh_scores, axis=0)
    peak = jnp.maximum(
        jnp.max(scores, axis=1, keepdims=True), jnp.max(fresh_scores, axis=1, keepdims=True)
    )
    weights = jnp.where(scores > 0.5 * very_low, jnp.exp(scores - peak), 0.0)
    fresh_weights = jnp.where(fresh_scores > 0.5 * very_low, jnp.exp(fresh_scores - peak), 0.0)
    total = jnp.sum(weights, axis=1, keepdims=True) + jnp.sum(fresh_weights, axis=1, keepdims=True)

    def halves(w):
        high = w.astype(jnp.bfloat16)
        low = (w - high.astype(jnp.float32)).astype(jnp.bfloat16)
        return jnp.concatenate([high, low], axis=0)

    lane = lax.broadcasted_iota(jnp.int32, (GROUP, HD), 1)
    stats = [jnp.zeros((GROUP, HD), jnp.float32) for _ in range(KV_HEADS)]
    copies[4].wait()
    for i, (b, g) in enumerate(pairs):
        here = slice(i * n, (i + 1) * n)
        s = dot(halves(weights[here]), values[b, :, g * HD : (g + 1) * HD])
        s = s + dot(halves(fresh_weights[here]), fresh(nv, b, g).astype(jnp.bfloat16))
        s = s[:n] + s[n:]
        for t in range(TOKENS):
            tb = t * rows + b
            part = slice(i * n + t * GROUP, i * n + (t + 1) * GROUP)
            stats[g] = jnp.where(lane == 2 * tb, peak[part], stats[g])
            stats[g] = jnp.where(lane == 2 * tb + 1, total[part], stats[g])
            block = s[t * GROUP : (t + 1) * GROUP]
            if hb >= GROUP:
                at = g * GROUP
                packed[at // hb, tb, at % hb : at % hb + GROUP] = block
            else:
                for j in range(GROUP // hb):
                    packed[g * (GROUP // hb) + j, tb] = block[j * hb : (j + 1) * hb]
    for g in range(KV_HEADS):
        if hb >= GROUP:
            at = g * GROUP
            packed[at // hb, TOKENS * rows, at % hb : at % hb + GROUP] = stats[g]
        else:
            for j in range(GROUP // hb):
                packed[g * (GROUP // hb) + j, TOKENS * rows] = stats[g][j * hb : (j + 1) * hb]
    for k in range(cols):
        outs[k][...] = packed[jnp.bitwise_xor(column, k)]


def combine_kernel(cols, *refs):
    parts, out = refs[:cols], refs[cols]
    cells = parts[0].shape[0] - 1
    hb = parts[0].shape[1]
    stats = [p[cells] for p in parts]
    attended = []
    for tb in range(cells):
        peaks = [s[:, 2 * tb : 2 * tb + 1] for s in stats]
        totals = [s[:, 2 * tb + 1 : 2 * tb + 2] for s in stats]
        top = functools.reduce(jnp.maximum, peaks)
        scales = [jnp.exp(p - top) for p in peaks]
        total = tree_sum([t * s for t, s in zip(totals, scales)])
        summed = tree_sum([p[tb] * s for p, s in zip(parts, scales)])
        attended.append(summed / total)
    rows = [
        jnp.concatenate([attended[tb][h : h + 1] for tb in range(cells)], axis=0) for h in range(hb)
    ]
    out[...] = jnp.concatenate(rows, axis=1).astype(out.dtype)


def group_order(value, groups):
    here = value.shape[1] // groups
    return jnp.concatenate(
        [value[t, r * here : (r + 1) * here] for r in range(groups) for t in range(TOKENS)], axis=0
    )


def canonical(parts, canon, me):
    cells = parts[0].shape[0]
    for k, part in enumerate(parts):
        canon[jnp.bitwise_xor(me, k), :cells] = part[...].astype(jnp.float32)
    rows = [canon[r, :cells] for r in range(len(parts))]
    return jnp.concatenate(rows, axis=0).astype(jnp.bfloat16)


def over_columns(width, body):
    size = width // 2 if width % 256 == 0 else width

    def step(j, carry):
        body(pl.multiple_of(j * size, 128), size)
        return carry

    lax.fori_loop(0, width // size, step, 0)


def out_kernel(groups, *refs):
    parts, (weight, out, canon, attended) = refs[:groups], refs[groups:]
    attended[...] = canonical(parts, canon, lax.axis_index("row"))

    def body(at, size):
        out[:, pl.ds(at, size)] = dot(attended[...], weight[:, pl.ds(at, size)]).astype(out.dtype)

    over_columns(out.shape[1], body)


def in_pieces(squares):
    first = squares.astype(WIRE).astype(jnp.float32)
    second = (squares - first).astype(WIRE).astype(jnp.float32)
    third = squares - first - second
    lane = lax.broadcasted_iota(jnp.int32, (squares.shape[0], HD), 1)
    return jnp.where(
        lane == 0, first, jnp.where(lane == 1, second, jnp.where(lane == 2, third, 0.0))
    )


def lift_kernel(groups, split, residual, gains, gate_weight, up_weight, *refs):
    parts, (mid_out, keep, send, lifted, packed) = refs[:-5], refs[-5:]
    hidden = gate_weight.shape[1] // split
    start = lax.axis_index("side") * hidden if split > 1 else 0
    half = packed.shape[1] // 2
    mid = tree_sum([p[...].astype(jnp.float32) for p in parts])
    mid = group_order(residual[...].astype(jnp.float32), groups) + mid
    mid_out[...] = mid
    sent = in_pieces(jnp.sum(mid * mid, axis=1, keepdims=True))
    lifted[...] = (mid * gains[...].astype(jnp.float32).reshape(1, mid.shape[1])).astype(jnp.bfloat16)
    for i in range(2):
        piece = sent[i * half : (i + 1) * half]
        packed[i, :, hidden:] = jnp.concatenate([piece, piece], axis=0)

    def body(at, size):
        block = pl.ds(pl.multiple_of(start + at, 128), size)
        gate = dot(lifted[...], gate_weight[:, block])
        up = dot(lifted[...], up_weight[:, block])
        for i in range(2):
            rows = slice(i * half, (i + 1) * half)
            packed[i, :, pl.ds(at, size)] = jnp.concatenate([gate[rows], up[rows]], axis=0)

    over_columns(hidden, body)
    bit = lax.axis_index("row") & 1
    keep[...] = packed[bit].astype(keep.dtype)
    send[...] = packed[1 - bit].astype(send.dtype)


def sum_kernel(first, second, out):
    hidden = out.shape[1] - HD
    total = first[...].astype(jnp.float32) + second[...].astype(jnp.float32)
    out[:, :hidden] = total[:, :hidden].astype(out.dtype)
    squares = jnp.sum(total[:, hidden:], axis=1, keepdims=True)
    out[:, hidden:] = in_pieces(squares).astype(out.dtype)


def act_kernel(model, first, second, out):
    hidden = first.shape[1] - HD
    cells = first.shape[0] // 2
    total = first[...].astype(jnp.float32) + second[...].astype(jnp.float32)
    squares = jnp.sum(total[:cells, hidden:], axis=1, keepdims=True)
    inv = lax.rsqrt(squares / model + 1e-05)
    gate = total[:cells, :hidden] * inv
    up = total[cells:, :hidden] * inv
    out[...] = (gate / (1.0 + jnp.exp(-gate)) * up).astype(out.dtype)


def gather_kernel(own, received, out, packed):
    bit = lax.axis_index("row") & 1
    packed[bit] = own[...].astype(jnp.float32)
    packed[1 - bit] = received[...].astype(jnp.float32)
    out[...] = jnp.concatenate([packed[0], packed[1]], axis=0).astype(out.dtype)


def down_kernel(other, act, weight, *refs):
    out = refs[-1]
    hidden = act.shape[1]
    start = 0
    if weight.shape[0] > hidden:
        start = pl.multiple_of(jnp.bitwise_xor(lax.axis_index("side"), other) * hidden, 128)

    def body(at, size):
        product = dot(act[...], weight[pl.ds(start, hidden), pl.ds(at, size)])
        if len(refs) > 1:
            product = product + refs[0][:, pl.ds(at, size)]
        out[:, pl.ds(at, size)] = product.astype(out.dtype)

    over_columns(out.shape[1], body)


def final_kernel(groups, mid, *refs):
    parts, out = refs[:-1], refs[-1]
    total = mid[...] + tree_sum([p[...].astype(jnp.float32) for p in parts])
    here = out.shape[1] // groups
    for t in range(TOKENS):
        block = [
            total[(r * TOKENS + t) * here : (r * TOKENS + t + 1) * here] for r in range(groups)
        ]
        out[t] = jnp.concatenate(block, axis=0).astype(out.dtype)


def shards(
    query,
    new_keys,
    new_values,
    key_cache,
    value_cache,
    lengths,
    residual,
    out_weight,
    norm_gain,
    gate_weight,
    up_weight,
    down_weight,
):
    sides, groups, cols = (lax.axis_size(a) for a in ("side", "row", "col"))
    rows_here = key_cache.shape[0]
    total_rows = residual.shape[1]
    width_share = residual.shape[2]
    hidden_share = gate_weight.shape[1]
    features = out_weight.shape[0]
    model = width_share * groups
    m = TOKENS * total_rows
    cells = TOKENS * rows_here
    hb = HEADS // cols
    split = 2 if sides == 2 and (hidden_share // 2) % 128 == 0 else 1
    hidden = hidden_share // split
    f32, bf16 = jnp.float32, jnp.bfloat16
    shape = jax.ShapeDtypeStruct
    pad = -(-cells // 8) * 8

    sources = [query, new_keys, new_values, key_cache, value_cache]
    message = shape((cells + 1, hb, HD), f32)
    parts = call(
        functools.partial(attention_kernel, cols),
        [message] * cols,
        [ANY_SPEC] * 6,
        [pltpu.VMEM(a.shape, a.dtype) for a in sources]
        + [pltpu.SMEM(lengths.shape, lengths.dtype)]
        + [pltpu.VMEM((cols, cells + 1, hb, HD), f32), pltpu.SemaphoreType.DMA((6,))],
        flops=40 * 10**9,
        name="attention",
    )(*[in_hbm(a) for a in [lengths, *sources]])
    parts = [parts[0]] + [partner(parts[k], "col", k) for k in range(1, cols)]
    attended = call(
        functools.partial(combine_kernel, cols),
        shape((cells, features), bf16),
        [VMEM_SPEC] * cols,
        name="combine",
    )(*parts)
    gathered = spread(attended, "row")
    partial = call(
        functools.partial(out_kernel, groups),
        shape((m, width_share), WIRE),
        [VMEM_SPEC] * (groups + 1),
        [pltpu.VMEM((groups, pad, features), f32), pltpu.VMEM((m, features), bf16)],
        name="out_projection",
    )(*gathered, in_vmem(out_weight))
    mid, keep, send = call(
        functools.partial(lift_kernel, groups, split),
        [shape((m, width_share), f32)] + [shape((m, hidden + HD), WIRE)] * 2,
        [VMEM_SPEC] * (cols + 4),
        [pltpu.VMEM((m, width_share), bf16), pltpu.VMEM((2, m, hidden + HD), f32)],
        name="gate_up",
    )(
        in_vmem(residual), in_vmem(norm_gain), in_vmem(gate_weight), in_vmem(up_weight),
        *spread(partial, "col"),
    )
    received = partner(send, "row", 1)
    for level in range(1, groups.bit_length() - 1):
        keep = call(
            sum_kernel,
            shape(keep.shape, WIRE),
            [VMEM_SPEC] * 2,
            name="gate_up_sum",
        )(keep, received)
        received = partner(keep, "row", 1 << level)
    act = call(
        functools.partial(act_kernel, model),
        shape((m // 2, hidden), bf16),
        [VMEM_SPEC] * 2,
        name="activation",
    )(keep, received)
    down_weight = in_vmem(down_weight)

    def down_part(same, from_row, other, before, result):
        rows = call(
            gather_kernel,
            shape((m, hidden), bf16),
            [VMEM_SPEC] * 2,
            [pltpu.VMEM((2, m // 2, hidden), f32)],
            name="gather_act",
        )(same, from_row)
        return call(
            functools.partial(down_kernel, other),
            shape((m, width_share), result),
            [VMEM_SPEC] * (2 + len(before)),
            name="down",
        )(rows, down_weight, *before)

    before = []
    if split > 1:
        far = partner(act, ("side", "row"), groups + 1)
        before = [down_part(partner(act, "side", 1), far, 1, before, f32)]
    down = down_part(act, partner(act, "row", 1), 0, before, WIRE)
    return call(
        functools.partial(final_kernel, groups),
        shape((TOKENS, total_rows, width_share), bf16),
        [VMEM_SPEC] * (cols + 1),
        name="final",
    )(mid, *spread(down, "col"))


def solution(mesh):
    in_specs = (
        P(None, "row", None),
        P(None, "row", None),
        P(None, "row", None),
        P("row", "col", None),
        P("row", "col", None),
        P("row"),
        P(None, None, "row"),
        P("col", "row"),
        P("row"),
        P("row", "col"),
        P("row", "col"),
        P("col", "row"),
    )
    out_specs = P(None, None, "row")
    return jax.shard_map(shards, mesh=mesh, in_specs=in_specs, out_specs=out_specs, check_vma=False)
```

```python
import functools
import math

import jax
import jax.numpy as jnp
from jax import lax
from jax.experimental import pallas as pl
from jax.experimental.pallas import tpu as pltpu
from jax.sharding import PartitionSpec as P

HEADS = 32
KV_HEADS = 4
HD = 128
GROUP = HEADS // KV_HEADS
TOKENS = 2
very_low = -1e30
MIB = 1024 * 1024
WIRE = jnp.bfloat16
VMEM_SPEC = pl.BlockSpec(memory_space=pltpu.VMEM)
ANY_SPEC = pl.BlockSpec(memory_space=pl.ANY)


def partner(value, axis, k):
    return lax.ppermute(value, axis, [(i, i ^ k) for i in range(lax.axis_size(axis))])


def spread(piece, axis):
    return [piece] + [partner(piece, axis, k) for k in range(1, lax.axis_size(axis))]


def tree_sum(values):
    while len(values) > 1:
        values = [values[i] + values[i + 1] for i in range(0, len(values), 2)]
    return values[0]


def dot(a, b):
    return jnp.dot(a, b, preferred_element_type=jnp.float32)


def dot_t(a, b):
    return lax.dot_general(a, b, (((1,), (1,)), ((), ())), preferred_element_type=jnp.float32)


def call(kernel, out_shape, in_specs, scratch=(), limit=4, name=None, flops=None):
    cost = None
    if flops is not None:
        cost = pl.CostEstimate(flops=flops, bytes_accessed=1024, transcendentals=0)
    return pl.pallas_call(
        kernel,
        out_shape=out_shape,
        in_specs=in_specs,
        out_specs=jax.tree.map(lambda _: VMEM_SPEC, out_shape),
        scratch_shapes=list(scratch),
        compiler_params=pltpu.CompilerParams(vmem_limit_bytes=limit * MIB),
        cost_estimate=cost,
        name=name,
    )


def in_hbm(value):
    return pltpu.with_memory_space_constraint(value, pltpu.HBM)


def in_vmem(value):
    return pltpu.with_memory_space_constraint(value, pltpu.VMEM)


def attention_kernel(cols, lengths, *rest):
    sources, outs = rest[:5], rest[5 : 5 + cols]
    held, (sized_ref, packed, sems) = rest[5 + cols : 10 + cols], rest[10 + cols :]
    sized = pltpu.make_async_copy(lengths, sized_ref, sems.at[5])
    sized.start()
    lengths = sized_ref
    copies = [
        pltpu.make_async_copy(source, target, sems.at[i])
        for i, (source, target) in enumerate(zip(sources, held))
    ]
    for copy in copies:
        copy.start()
    query, new_keys, new_values, keys, values = held
    column = lax.axis_index("col")
    rows, span, _ = keys.shape
    hb = HEADS // cols
    inv_root = 1.0 / math.sqrt(HD)
    n = TOKENS * GROUP
    pairs = [(b, g) for b in range(rows) for g in range(KV_HEADS)]
    for copy in [sized] + copies[:4]:
        copy.wait()
    q32 = query[...].astype(jnp.float32)
    nk, nv = new_keys[...].astype(jnp.float32), new_values[...].astype(jnp.float32)
    zeros = jnp.zeros((8 - TOKENS, HD), jnp.float32)

    def fresh(block, b, g):
        lanes = slice(g * HD, (g + 1) * HD)
        return jnp.concatenate([block[t, b : b + 1, lanes] for t in range(TOKENS)] + [zeros], axis=0)

    scores, fresh_scores = [], []
    for b, g in pairs:
        q = jnp.concatenate(
            [
                q32[t, b : b + 1, (g * GROUP + h) * HD : (g * GROUP + h + 1) * HD]
                for t in range(TOKENS)
                for h in range(GROUP)
            ],
            axis=0,
        ).astype(jnp.bfloat16)
        s = dot_t(q, keys[b, :, g * HD : (g + 1) * HD]) * inv_root
        position = column * span + lax.broadcasted_iota(jnp.int32, (n, span), 1)
        scores.append(jnp.where(position < lengths[b], s, very_low))
        f = dot_t(q, fresh(nk, b, g).astype(jnp.bfloat16)) * inv_root
        token = lax.broadcasted_iota(jnp.int32, (n, 8), 0) // GROUP
        slot = lax.broadcasted_iota(jnp.int32, (n, 8), 1)
        seen = jnp.logical_and(slot <= token, column == 0)
        fresh_scores.append(jnp.where(seen, f, very_low))
    scores = jnp.concatenate(scores, axis=0)
    fresh_scores = jnp.concatenate(fresh_scores, axis=0)
    peak = jnp.maximum(
        jnp.max(scores, axis=1, keepdims=True), jnp.max(fresh_scores, axis=1, keepdims=True)
    )
    weights = jnp.where(scores > 0.5 * very_low, jnp.exp(scores - peak), 0.0)
    fresh_weights = jnp.where(fresh_scores > 0.5 * very_low, jnp.exp(fresh_scores - peak), 0.0)
    total = jnp.sum(weights, axis=1, keepdims=True) + jnp.sum(fresh_weights, axis=1, keepdims=True)

    def halves(w):
        high = w.astype(jnp.bfloat16)
        low = (w - high.astype(jnp.float32)).astype(jnp.bfloat16)
        return jnp.concatenate([high, low], axis=0)

    lane = lax.broadcasted_iota(jnp.int32, (GROUP, HD), 1)
    stats = [jnp.zeros((GROUP, HD), jnp.float32) for _ in range(KV_HEADS)]
    copies[4].wait()
    for i, (b, g) in enumerate(pairs):
        here = slice(i * n, (i + 1) * n)
        s = dot(halves(weights[here]), values[b, :, g * HD : (g + 1) * HD])
        s = s + dot(halves(fresh_weights[here]), fresh(nv, b, g).astype(jnp.bfloat16))
        s = s[:n] + s[n:]
        for t in range(TOKENS):
            tb = t * rows + b
            part = slice(i * n + t * GROUP, i * n + (t + 1) * GROUP)
            stats[g] = jnp.where(lane == 2 * tb, peak[part], stats[g])
            stats[g] = jnp.where(lane == 2 * tb + 1, total[part], stats[g])
            block = s[t * GROUP : (t + 1) * GROUP]
            if hb >= GROUP:
                at = g * GROUP
                packed[at // hb, tb, at % hb : at % hb + GROUP] = block
            else:
                for j in range(GROUP // hb):
                    packed[g * (GROUP // hb) + j, tb] = block[j * hb : (j + 1) * hb]
    for g in range(KV_HEADS):
        if hb >= GROUP:
            at = g * GROUP
            packed[at // hb, TOKENS * rows, at % hb : at % hb + GROUP] = stats[g]
        else:
            for j in range(GROUP // hb):
                packed[g * (GROUP // hb) + j, TOKENS * rows] = stats[g][j * hb : (j + 1) * hb]
    for k in range(cols):
        outs[k][...] = packed[jnp.bitwise_xor(column, k)]


def combine_kernel(cols, *refs):
    parts, out = refs[:cols], refs[cols]
    cells = parts[0].shape[0] - 1
    hb = parts[0].shape[1]
    stats = [p[cells] for p in parts]
    attended = []
    for tb in range(cells):
        peaks = [s[:, 2 * tb : 2 * tb + 1] for s in stats]
        totals = [s[:, 2 * tb + 1 : 2 * tb + 2] for s in stats]
        top = functools.reduce(jnp.maximum, peaks)
        scales = [jnp.exp(p - top) for p in peaks]
        total = tree_sum([t * s for t, s in zip(totals, scales)])
        summed = tree_sum([p[tb] * s for p, s in zip(parts, scales)])
        attended.append(summed / total)
    rows = [
        jnp.concatenate([attended[tb][h : h + 1] for tb in range(cells)], axis=0) for h in range(hb)
    ]
    out[...] = jnp.concatenate(rows, axis=1).astype(out.dtype)


def group_order(value, groups):
    here = value.shape[1] // groups
    return jnp.concatenate(
        [value[t, r * here : (r + 1) * here] for r in range(groups) for t in range(TOKENS)], axis=0
    )


def canonical(parts, canon, me):
    cells = parts[0].shape[0]
    for k, part in enumerate(parts):
        canon[jnp.bitwise_xor(me, k), :cells] = part[...].astype(jnp.float32)
    rows = [canon[r, :cells] for r in range(len(parts))]
    return jnp.concatenate(rows, axis=0).astype(jnp.bfloat16)


def over_columns(width, body):
    size = width // 2 if width % 256 == 0 else width

    def step(j, carry):
        body(pl.multiple_of(j * size, 128), size)
        return carry

    lax.fori_loop(0, width // size, step, 0)


def out_kernel(groups, *refs):
    parts, (weight, out, canon, attended) = refs[:groups], refs[groups:]
    attended[...] = canonical(parts, canon, lax.axis_index("row"))

    def body(at, size):
        out[:, pl.ds(at, size)] = dot(attended[...], weight[:, pl.ds(at, size)]).astype(out.dtype)

    over_columns(out.shape[1], body)


def in_pieces(squares):
    first = squares.astype(WIRE).astype(jnp.float32)
    second = (squares - first).astype(WIRE).astype(jnp.float32)
    third = squares - first - second
    lane = lax.broadcasted_iota(jnp.int32, (squares.shape[0], HD), 1)
    return jnp.where(
        lane == 0, first, jnp.where(lane == 1, second, jnp.where(lane == 2, third, 0.0))
    )


def lift_kernel(groups, split, residual, gains, gate_weight, up_weight, *refs):
    parts, (mid_out, keep, send, lifted, packed) = refs[:-5], refs[-5:]
    hidden = gate_weight.shape[1] // split
    start = lax.axis_index("side") * hidden if split > 1 else 0
    half = packed.shape[1] // 2
    mid = tree_sum([p[...].astype(jnp.float32) for p in parts])
    mid = group_order(residual[...].astype(jnp.float32), groups) + mid
    mid_out[...] = mid
    sent = in_pieces(jnp.sum(mid * mid, axis=1, keepdims=True))
    lifted[...] = (mid * gains[...].astype(jnp.float32).reshape(1, mid.shape[1])).astype(jnp.bfloat16)
    for i in range(2):
        piece = sent[i * half : (i + 1) * half]
        packed[i, :, hidden:] = jnp.concatenate([piece, piece], axis=0)

    def body(at, size):
        block = pl.ds(pl.multiple_of(start + at, 128), size)
        gate = dot(lifted[...], gate_weight[:, block])
        up = dot(lifted[...], up_weight[:, block])
        for i in range(2):
            rows = slice(i * half, (i + 1) * half)
            packed[i, :, pl.ds(at, size)] = jnp.concatenate([gate[rows], up[rows]], axis=0)

    over_columns(hidden, body)
    bit = lax.axis_index("row") & 1
    keep[...] = packed[bit].astype(keep.dtype)
    send[...] = packed[1 - bit].astype(send.dtype)


def act_kernel(model, *refs):
    parts, out = refs[:-1], refs[-1]
    hidden = parts[0].shape[1] - HD
    cells = parts[0].shape[0] // 2
    values = [p[...].astype(jnp.float32) for p in parts]
    total = tree_sum(values[0::2]) + tree_sum(values[1::2])
    squares = jnp.sum(total[:cells, hidden:], axis=1, keepdims=True)
    inv = lax.rsqrt(squares / model + 1e-05)
    gate = total[:cells, :hidden] * inv
    up = total[cells:, :hidden] * inv
    out[...] = (gate / (1.0 + jnp.exp(-gate)) * up).astype(out.dtype)


def gather_kernel(own, received, out, packed):
    bit = lax.axis_index("row") & 1
    packed[bit] = own[...].astype(jnp.float32)
    packed[1 - bit] = received[...].astype(jnp.float32)
    out[...] = jnp.concatenate([packed[0], packed[1]], axis=0).astype(out.dtype)


def down_kernel(other, act, weight, *refs):
    out = refs[-1]
    hidden = act.shape[1]
    start = 0
    if weight.shape[0] > hidden:
        start = pl.multiple_of(jnp.bitwise_xor(lax.axis_index("side"), other) * hidden, 128)

    def body(at, size):
        product = dot(act[...], weight[pl.ds(start, hidden), pl.ds(at, size)])
        if len(refs) > 1:
            product = product + refs[0][:, pl.ds(at, size)]
        out[:, pl.ds(at, size)] = product.astype(out.dtype)

    over_columns(out.shape[1], body)


def final_kernel(groups, mid, *refs):
    parts, out = refs[:-1], refs[-1]
    total = mid[...] + tree_sum([p[...].astype(jnp.float32) for p in parts])
    here = out.shape[1] // groups
    for t in range(TOKENS):
        block = [
            total[(r * TOKENS + t) * here : (r * TOKENS + t + 1) * here] for r in range(groups)
        ]
        out[t] = jnp.concatenate(block, axis=0).astype(out.dtype)


def shards(
    query,
    new_keys,
    new_values,
    key_cache,
    value_cache,
    lengths,
    residual,
    out_weight,
    norm_gain,
    gate_weight,
    up_weight,
    down_weight,
):
    sides, groups, cols = (lax.axis_size(a) for a in ("side", "row", "col"))
    rows_here = key_cache.shape[0]
    total_rows = residual.shape[1]
    width_share = residual.shape[2]
    hidden_share = gate_weight.shape[1]
    features = out_weight.shape[0]
    model = width_share * groups
    m = TOKENS * total_rows
    cells = TOKENS * rows_here
    hb = HEADS // cols
    split = 2 if sides == 2 and (hidden_share // 2) % 128 == 0 else 1
    hidden = hidden_share // split
    f32, bf16 = jnp.float32, jnp.bfloat16
    shape = jax.ShapeDtypeStruct
    pad = -(-cells // 8) * 8

    sources = [query, new_keys, new_values, key_cache, value_cache]
    message = shape((cells + 1, hb, HD), f32)
    parts = call(
        functools.partial(attention_kernel, cols),
        [message] * cols,
        [ANY_SPEC] * 6,
        [pltpu.VMEM(a.shape, a.dtype) for a in sources]
        + [pltpu.SMEM(lengths.shape, lengths.dtype)]
        + [pltpu.VMEM((cols, cells + 1, hb, HD), f32), pltpu.SemaphoreType.DMA((6,))],
        flops=40 * 10**9,
        name="attention",
    )(*[in_hbm(a) for a in [lengths, *sources]])
    parts = [parts[0]] + [partner(parts[k], "col", k) for k in range(1, cols)]
    attended = call(
        functools.partial(combine_kernel, cols),
        shape((cells, features), bf16),
        [VMEM_SPEC] * cols,
        name="combine",
    )(*parts)
    gathered = spread(attended, "row")
    partial = call(
        functools.partial(out_kernel, groups),
        shape((m, width_share), WIRE),
        [VMEM_SPEC] * (groups + 1),
        [pltpu.VMEM((groups, pad, features), f32), pltpu.VMEM((m, features), bf16)],
        name="out_projection",
    )(*gathered, in_vmem(out_weight))
    mid, keep, send = call(
        functools.partial(lift_kernel, groups, split),
        [shape((m, width_share), f32)] + [shape((m, hidden + HD), WIRE)] * 2,
        [VMEM_SPEC] * (cols + 4),
        [pltpu.VMEM((m, width_share), bf16), pltpu.VMEM((2, m, hidden + HD), f32)],
        name="gate_up",
    )(
        in_vmem(residual), in_vmem(norm_gain), in_vmem(gate_weight), in_vmem(up_weight),
        *spread(partial, "col"),
    )
    sums = [keep] + [partner((keep, send)[k % 2], "row", k) for k in range(1, groups)]
    act = call(
        functools.partial(act_kernel, model),
        shape((m // 2, hidden), bf16),
        [VMEM_SPEC] * groups,
        name="activation",
    )(*sums)
    down_weight = in_vmem(down_weight)

    def down_part(same, from_row, other, before, result):
        rows = call(
            gather_kernel,
            shape((m, hidden), bf16),
            [VMEM_SPEC] * 2,
            [pltpu.VMEM((2, m // 2, hidden), f32)],
            name="gather_act",
        )(same, from_row)
        return call(
            functools.partial(down_kernel, other),
            shape((m, width_share), result),
            [VMEM_SPEC] * (2 + len(before)),
            name="down",
        )(rows, down_weight, *before)

    near = partner(act, "row", 1)
    if split > 1:
        first = down_part(act, near, 0, [], f32)
        far = partner(act, ("side", "row"), groups + 1)
        down = down_part(partner(act, "side", 1), far, 1, [first], WIRE)
    else:
        down = down_part(act, near, 0, [], WIRE)
    return call(
        functools.partial(final_kernel, groups),
        shape((TOKENS, total_rows, width_share), bf16),
        [VMEM_SPEC] * (cols + 1),
        name="final",
    )(mid, *spread(down, "col"))


def solution(mesh):
    in_specs = (
        P(None, "row", None),
        P(None, "row", None),
        P(None, "row", None),
        P("row", "col", None),
        P("row", "col", None),
        P("row"),
        P(None, None, "row"),
        P("col", "row"),
        P("row"),
        P("row", "col"),
        P("row", "col"),
        P("col", "row"),
    )
    out_specs = P(None, None, "row")
    return jax.shard_map(shards, mesh=mesh, in_specs=in_specs, out_specs=out_specs, check_vma=False)
```

```python
import functools
import math

import jax
import jax.numpy as jnp
from jax import lax
from jax.experimental import pallas as pl
from jax.experimental.pallas import tpu as pltpu
from jax.sharding import PartitionSpec as P

HEADS = 32
KV_HEADS = 4
HD = 128
GROUP = HEADS // KV_HEADS
TOKENS = 2
very_low = -1e30
MIB = 1024 * 1024
WIRE = jnp.bfloat16
VMEM_SPEC = pl.BlockSpec(memory_space=pltpu.VMEM)
ANY_SPEC = pl.BlockSpec(memory_space=pl.ANY)


def partner(value, axis, k):
    return lax.ppermute(value, axis, [(i, i ^ k) for i in range(lax.axis_size(axis))])


def spread(piece, axis):
    return [piece] + [partner(piece, axis, k) for k in range(1, lax.axis_size(axis))]


def tree_sum(values):
    while len(values) > 1:
        values = [values[i] + values[i + 1] for i in range(0, len(values), 2)]
    return values[0]


def dot(a, b):
    return jnp.dot(a, b, preferred_element_type=jnp.float32)


def dot_t(a, b):
    return lax.dot_general(a, b, (((1,), (1,)), ((), ())), preferred_element_type=jnp.float32)


def call(kernel, out_shape, in_specs, scratch=(), limit=4, name=None, flops=None):
    cost = None
    if flops is not None:
        cost = pl.CostEstimate(flops=flops, bytes_accessed=1024, transcendentals=0)
    return pl.pallas_call(
        kernel,
        out_shape=out_shape,
        in_specs=in_specs,
        out_specs=jax.tree.map(lambda _: VMEM_SPEC, out_shape),
        scratch_shapes=list(scratch),
        compiler_params=pltpu.CompilerParams(vmem_limit_bytes=limit * MIB),
        cost_estimate=cost,
        name=name,
    )


def in_hbm(value):
    return pltpu.with_memory_space_constraint(value, pltpu.HBM)


def in_vmem(value):
    return pltpu.with_memory_space_constraint(value, pltpu.VMEM)


def attention_kernel(cols, far, lengths, *rest):
    half = cols // 2
    sources, outs = rest[:5], rest[5 : 5 + half]
    held, (sized, packed, sems) = rest[5 + half : 10 + half], rest[10 + half :]
    column = lax.axis_index("col")
    heads = KV_HEADS // 2
    part = jnp.bitwise_xor(column // half, far)

    def lanes(source):
        width = source.shape[2] // 2
        return source.at[:, :, pl.ds(pl.multiple_of(part * width, 128), width)]

    copies = [
        pltpu.make_async_copy(lanes(source), target, sems.at[i])
        for i, (source, target) in enumerate(zip(sources, held))
    ]
    copies.append(pltpu.make_async_copy(lengths, sized, sems.at[5]))
    for copy in copies:
        copy.start()
    query, new_keys, new_values, keys, values = held
    rows, span, _ = keys.shape
    hb = HEADS // cols
    inv_root = 1.0 / math.sqrt(HD)
    n = TOKENS * GROUP
    pairs = [(b, g) for b in range(rows) for g in range(heads)]
    for i in (0, 1, 2, 5, 3):
        copies[i].wait()
    q32 = query[...].astype(jnp.float32)
    nk, nv = new_keys[...].astype(jnp.float32), new_values[...].astype(jnp.float32)
    zeros = jnp.zeros((8 - TOKENS, HD), jnp.float32)

    def fresh(block, b, g):
        lanes = slice(g * HD, (g + 1) * HD)
        return jnp.concatenate([block[t, b : b + 1, lanes] for t in range(TOKENS)] + [zeros], axis=0)

    scores, fresh_scores = [], []
    for b, g in pairs:
        q = jnp.concatenate(
            [
                q32[t, b : b + 1, (g * GROUP + h) * HD : (g * GROUP + h + 1) * HD]
                for t in range(TOKENS)
                for h in range(GROUP)
            ],
            axis=0,
        ).astype(jnp.bfloat16)
        s = dot_t(q, keys[b, :, g * HD : (g + 1) * HD]) * inv_root
        position = column * span + lax.broadcasted_iota(jnp.int32, (n, span), 1)
        scores.append(jnp.where(position < sized[b], s, very_low))
        f = dot_t(q, fresh(nk, b, g).astype(jnp.bfloat16)) * inv_root
        token = lax.broadcasted_iota(jnp.int32, (n, 8), 0) // GROUP
        slot = lax.broadcasted_iota(jnp.int32, (n, 8), 1)
        seen = jnp.logical_and(slot <= token, column == 0)
        fresh_scores.append(jnp.where(seen, f, very_low))
    scores = jnp.concatenate(scores, axis=0)
    fresh_scores = jnp.concatenate(fresh_scores, axis=0)
    peak = jnp.maximum(
        jnp.max(scores, axis=1, keepdims=True), jnp.max(fresh_scores, axis=1, keepdims=True)
    )
    weights = jnp.where(scores > 0.5 * very_low, jnp.exp(scores - peak), 0.0)
    fresh_weights = jnp.where(fresh_scores > 0.5 * very_low, jnp.exp(fresh_scores - peak), 0.0)
    total = jnp.sum(weights, axis=1, keepdims=True) + jnp.sum(fresh_weights, axis=1, keepdims=True)

    def halves(w):
        high = w.astype(jnp.bfloat16)
        low = (w - high.astype(jnp.float32)).astype(jnp.bfloat16)
        return jnp.concatenate([high, low], axis=0)

    lane = lax.broadcasted_iota(jnp.int32, (GROUP, HD), 1)
    stats = [jnp.zeros((GROUP, HD), jnp.float32) for _ in range(heads)]
    copies[4].wait()
    for i, (b, g) in enumerate(pairs):
        here = slice(i * n, (i + 1) * n)
        s = dot(halves(weights[here]), values[b, :, g * HD : (g + 1) * HD])
        s = s + dot(halves(fresh_weights[here]), fresh(nv, b, g).astype(jnp.bfloat16))
        s = s[:n] + s[n:]
        for t in range(TOKENS):
            tb = t * rows + b
            part = slice(i * n + t * GROUP, i * n + (t + 1) * GROUP)
            stats[g] = jnp.where(lane == 2 * tb, peak[part], stats[g])
            stats[g] = jnp.where(lane == 2 * tb + 1, total[part], stats[g])
            block = s[t * GROUP : (t + 1) * GROUP]
            if hb >= GROUP:
                at = g * GROUP
                packed[at // hb, tb, at % hb : at % hb + GROUP] = block
            else:
                for j in range(GROUP // hb):
                    packed[g * (GROUP // hb) + j, tb] = block[j * hb : (j + 1) * hb]
    for g in range(heads):
        if hb >= GROUP:
            at = g * GROUP
            packed[at // hb, TOKENS * rows, at % hb : at % hb + GROUP] = stats[g]
        else:
            for j in range(GROUP // hb):
                packed[g * (GROUP // hb) + j, TOKENS * rows] = stats[g][j * hb : (j + 1) * hb]
    for k in range(half):
        outs[k][...] = packed[jnp.bitwise_xor(column % half, k)]


def combine_kernel(cols, *refs):
    parts, out = refs[:cols], refs[cols]
    cells = parts[0].shape[0] - 1
    hb = parts[0].shape[1]
    stats = [p[cells] for p in parts]
    attended = []
    for tb in range(cells):
        peaks = [s[:, 2 * tb : 2 * tb + 1] for s in stats]
        totals = [s[:, 2 * tb + 1 : 2 * tb + 2] for s in stats]
        top = functools.reduce(jnp.maximum, peaks)
        scales = [jnp.exp(p - top) for p in peaks]
        total = tree_sum([t * s for t, s in zip(totals, scales)])
        summed = tree_sum([p[tb] * s for p, s in zip(parts, scales)])
        attended.append(summed / total)
    rows = [
        jnp.concatenate([attended[tb][h : h + 1] for tb in range(cells)], axis=0) for h in range(hb)
    ]
    out[...] = jnp.concatenate(rows, axis=1).astype(out.dtype)


def group_order(value, groups):
    here = value.shape[1] // groups
    return jnp.concatenate(
        [value[t, r * here : (r + 1) * here] for r in range(groups) for t in range(TOKENS)], axis=0
    )


def canonical(parts, canon, me):
    cells = parts[0].shape[0]
    for k, part in enumerate(parts):
        canon[jnp.bitwise_xor(me, k), :cells] = part[...].astype(jnp.float32)
    rows = [canon[r, :cells] for r in range(len(parts))]
    return jnp.concatenate(rows, axis=0).astype(jnp.bfloat16)


def over_columns(width, body):
    size = width // 2 if width % 256 == 0 else width

    def step(j, carry):
        body(pl.multiple_of(j * size, 128), size)
        return carry

    lax.fori_loop(0, width // size, step, 0)


def out_kernel(groups, *refs):
    parts, (weight, out, canon, attended) = refs[:groups], refs[groups:]
    attended[...] = canonical(parts, canon, lax.axis_index("row"))

    def body(at, size):
        out[:, pl.ds(at, size)] = dot(attended[...], weight[:, pl.ds(at, size)]).astype(out.dtype)

    over_columns(out.shape[1], body)


def in_pieces(squares):
    first = squares.astype(WIRE).astype(jnp.float32)
    second = (squares - first).astype(WIRE).astype(jnp.float32)
    third = squares - first - second
    lane = lax.broadcasted_iota(jnp.int32, (squares.shape[0], HD), 1)
    return jnp.where(
        lane == 0, first, jnp.where(lane == 1, second, jnp.where(lane == 2, third, 0.0))
    )


def lift_kernel(groups, split, residual, gains, gate_weight, up_weight, *refs):
    parts, (mid_out, keep, send, lifted, packed) = refs[:-5], refs[-5:]
    hidden = gate_weight.shape[1] // split
    start = lax.axis_index("side") * hidden if split > 1 else 0
    half = packed.shape[1] // 2
    mid = tree_sum([p[...].astype(jnp.float32) for p in parts])
    mid = group_order(residual[...].astype(jnp.float32), groups) + mid
    mid_out[...] = mid
    sent = in_pieces(jnp.sum(mid * mid, axis=1, keepdims=True))
    lifted[...] = (mid * gains[...].astype(jnp.float32).reshape(1, mid.shape[1])).astype(jnp.bfloat16)
    for i in range(2):
        piece = sent[i * half : (i + 1) * half]
        packed[i, :, hidden:] = jnp.concatenate([piece, piece], axis=0)

    def body(at, size):
        block = pl.ds(pl.multiple_of(start + at, 128), size)
        gate = dot(lifted[...], gate_weight[:, block])
        up = dot(lifted[...], up_weight[:, block])
        for i in range(2):
            rows = slice(i * half, (i + 1) * half)
            packed[i, :, pl.ds(at, size)] = jnp.concatenate([gate[rows], up[rows]], axis=0)

    over_columns(hidden, body)
    bit = lax.axis_index("row") & 1
    keep[...] = packed[bit].astype(keep.dtype)
    send[...] = packed[1 - bit].astype(send.dtype)


def act_kernel(model, *refs):
    parts, out = refs[:-1], refs[-1]
    hidden = parts[0].shape[1] - HD
    cells = parts[0].shape[0] // 2
    values = [p[...].astype(jnp.float32) for p in parts]
    total = tree_sum(values[0::2]) + tree_sum(values[1::2])
    squares = jnp.sum(total[:cells, hidden:], axis=1, keepdims=True)
    inv = lax.rsqrt(squares / model + 1e-05)
    gate = total[:cells, :hidden] * inv
    up = total[cells:, :hidden] * inv
    out[...] = (gate / (1.0 + jnp.exp(-gate)) * up).astype(out.dtype)


def gather_kernel(own, received, out, packed):
    bit = lax.axis_index("row") & 1
    packed[bit] = own[...].astype(jnp.float32)
    packed[1 - bit] = received[...].astype(jnp.float32)
    out[...] = jnp.concatenate([packed[0], packed[1]], axis=0).astype(out.dtype)


def down_kernel(other, act, weight, *refs):
    out = refs[-1]
    hidden = act.shape[1]
    start = 0
    if weight.shape[0] > hidden:
        start = pl.multiple_of(jnp.bitwise_xor(lax.axis_index("side"), other) * hidden, 128)

    def body(at, size):
        product = dot(act[...], weight[pl.ds(start, hidden), pl.ds(at, size)])
        if len(refs) > 1:
            product = product + refs[0][:, pl.ds(at, size)]
        out[:, pl.ds(at, size)] = product.astype(out.dtype)

    over_columns(out.shape[1], body)


def final_kernel(groups, mid, *refs):
    parts, out = refs[:-1], refs[-1]
    total = mid[...] + tree_sum([p[...].astype(jnp.float32) for p in parts])
    here = out.shape[1] // groups
    for t in range(TOKENS):
        block = [
            total[(r * TOKENS + t) * here : (r * TOKENS + t + 1) * here] for r in range(groups)
        ]
        out[t] = jnp.concatenate(block, axis=0).astype(out.dtype)


def shards(
    query,
    new_keys,
    new_values,
    key_cache,
    value_cache,
    lengths,
    residual,
    out_weight,
    norm_gain,
    gate_weight,
    up_weight,
    down_weight,
):
    sides, groups, cols = (lax.axis_size(a) for a in ("side", "row", "col"))
    rows_here = key_cache.shape[0]
    total_rows = residual.shape[1]
    width_share = residual.shape[2]
    hidden_share = gate_weight.shape[1]
    features = out_weight.shape[0]
    model = width_share * groups
    m = TOKENS * total_rows
    cells = TOKENS * rows_here
    hb = HEADS // cols
    split = 2 if sides == 2 and (hidden_share // 2) % 128 == 0 else 1
    hidden = hidden_share // split
    f32, bf16 = jnp.float32, jnp.bfloat16
    shape = jax.ShapeDtypeStruct
    pad = -(-cells // 8) * 8

    sources = [query, new_keys, new_values, key_cache, value_cache]
    message = shape((cells + 1, hb, HD), f32)
    sources = [query, new_keys, new_values, key_cache, value_cache]

    def messages(far):
        return call(
            functools.partial(attention_kernel, cols, far),
            [message] * (cols // 2),
            [ANY_SPEC] * 6,
            [pltpu.VMEM((*a.shape[:2], a.shape[2] // 2), a.dtype) for a in sources]
            + [pltpu.SMEM(lengths.shape, lengths.dtype)]
            + [pltpu.VMEM((cols // 2, *message.shape), f32), pltpu.SemaphoreType.DMA((6,))],
            flops=40 * 10**9 if far else None,
            name="attention_far" if far else "attention_near",
        )(*[in_hbm(a) for a in [lengths, *sources]])

    parts = messages(1)
    parts = [partner(parts[k], "col", cols // 2 + k) for k in range(cols // 2)]
    near = messages(0)
    parts = [near[0]] + [partner(near[k], "col", k) for k in range(1, cols // 2)] + parts
    attended = call(
        functools.partial(combine_kernel, cols),
        shape((cells, features), bf16),
        [VMEM_SPEC] * cols,
        name="combine",
    )(*parts)
    gathered = spread(attended, "row")
    partial = call(
        functools.partial(out_kernel, groups),
        shape((m, width_share), WIRE),
        [VMEM_SPEC] * (groups + 1),
        [pltpu.VMEM((groups, pad, features), f32), pltpu.VMEM((m, features), bf16)],
        name="out_projection",
    )(*gathered, in_vmem(out_weight))
    mid, keep, send = call(
        functools.partial(lift_kernel, groups, split),
        [shape((m, width_share), f32)] + [shape((m, hidden + HD), WIRE)] * 2,
        [VMEM_SPEC] * (cols + 4),
        [pltpu.VMEM((m, width_share), bf16), pltpu.VMEM((2, m, hidden + HD), f32)],
        name="gate_up",
    )(
        in_vmem(residual), in_vmem(norm_gain), in_vmem(gate_weight), in_vmem(up_weight),
        *spread(partial, "col"),
    )
    sums = [keep] + [partner((keep, send)[k % 2], "row", k) for k in range(1, groups)]
    act = call(
        functools.partial(act_kernel, model),
        shape((m // 2, hidden), bf16),
        [VMEM_SPEC] * groups,
        name="activation",
    )(*sums)
    down_weight = in_vmem(down_weight)

    def down_part(same, from_row, other, before, result):
        rows = call(
            gather_kernel,
            shape((m, hidden), bf16),
            [VMEM_SPEC] * 2,
            [pltpu.VMEM((2, m // 2, hidden), f32)],
            name="gather_act",
        )(same, from_row)
        return call(
            functools.partial(down_kernel, other),
            shape((m, width_share), result),
            [VMEM_SPEC] * (2 + len(before)),
            name="down",
        )(rows, down_weight, *before)

    near = partner(act, "row", 1)
    if split > 1:
        first = down_part(act, near, 0, [], f32)
        far = partner(act, ("side", "row"), groups + 1)
        down = down_part(partner(act, "side", 1), far, 1, [first], WIRE)
    else:
        down = down_part(act, near, 0, [], WIRE)
    return call(
        functools.partial(final_kernel, groups),
        shape((TOKENS, total_rows, width_share), bf16),
        [VMEM_SPEC] * (cols + 1),
        name="final",
    )(mid, *spread(down, "col"))


def solution(mesh):
    in_specs = (
        P(None, "row", None),
        P(None, "row", None),
        P(None, "row", None),
        P("row", "col", None),
        P("row", "col", None),
        P("row"),
        P(None, None, "row"),
        P("col", "row"),
        P("row"),
        P("row", "col"),
        P("row", "col"),
        P("col", "row"),
    )
    out_specs = P(None, None, "row")
    return jax.shard_map(shards, mesh=mesh, in_specs=in_specs, out_specs=out_specs, check_vma=False)
```

```python
import functools
import math

import jax
import jax.numpy as jnp
from jax import lax
from jax.experimental import pallas as pl
from jax.experimental.pallas import tpu as pltpu
from jax.sharding import PartitionSpec as P

HEADS = 32
KV_HEADS = 4
HD = 128
GROUP = HEADS // KV_HEADS
TOKENS = 2
very_low = -1e30
MIB = 1024 * 1024
WIRE = jnp.bfloat16
VMEM_SPEC = pl.BlockSpec(memory_space=pltpu.VMEM)
ANY_SPEC = pl.BlockSpec(memory_space=pl.ANY)


def partner(value, axis, k):
    return lax.ppermute(value, axis, [(i, i ^ k) for i in range(lax.axis_size(axis))])


def spread(piece, axis):
    return [piece] + [partner(piece, axis, k) for k in range(1, lax.axis_size(axis))]


def tree_sum(values):
    while len(values) > 1:
        values = [values[i] + values[i + 1] for i in range(0, len(values), 2)]
    return values[0]


def dot(a, b):
    return jnp.dot(a, b, preferred_element_type=jnp.float32)


def dot_t(a, b):
    return lax.dot_general(a, b, (((1,), (1,)), ((), ())), preferred_element_type=jnp.float32)


def call(kernel, out_shape, in_specs, scratch=(), limit=4, name=None, flops=None):
    cost = None
    if flops is not None:
        cost = pl.CostEstimate(flops=flops, bytes_accessed=1024, transcendentals=0)
    return pl.pallas_call(
        kernel,
        out_shape=out_shape,
        in_specs=in_specs,
        out_specs=jax.tree.map(lambda _: VMEM_SPEC, out_shape),
        scratch_shapes=list(scratch),
        compiler_params=pltpu.CompilerParams(vmem_limit_bytes=limit * MIB),
        cost_estimate=cost,
        name=name,
    )


def in_hbm(value):
    return pltpu.with_memory_space_constraint(value, pltpu.HBM)


def in_vmem(value):
    return pltpu.with_memory_space_constraint(value, pltpu.VMEM)


def attention_kernel(cols, far, lengths, *rest):
    half = cols // 2
    sources, outs = rest[:5], rest[5 : 5 + half]
    held, (sized, packed, sems) = rest[5 + half : 10 + half], rest[10 + half :]
    column = lax.axis_index("col")
    heads = KV_HEADS // 2
    part = jnp.bitwise_xor(column // half, far)

    def lanes(source):
        width = source.shape[2] // 2
        return source.at[:, :, pl.ds(pl.multiple_of(part * width, 128), width)]

    copies = [
        pltpu.make_async_copy(lanes(source), target, sems.at[i])
        for i, (source, target) in enumerate(zip(sources, held))
    ]
    copies.append(pltpu.make_async_copy(lengths, sized, sems.at[5]))
    for copy in copies:
        copy.start()
    query, new_keys, new_values, keys, values = held
    rows, span, _ = keys.shape
    hb = HEADS // cols
    inv_root = 1.0 / math.sqrt(HD)
    n = TOKENS * GROUP
    pairs = [(b, g) for b in range(rows) for g in range(heads)]
    for i in (0, 1, 2, 5, 3):
        copies[i].wait()
    q32 = query[...].astype(jnp.float32)
    nk, nv = new_keys[...].astype(jnp.float32), new_values[...].astype(jnp.float32)
    zeros = jnp.zeros((8 - TOKENS, HD), jnp.float32)

    def fresh(block, b, g):
        lanes = slice(g * HD, (g + 1) * HD)
        return jnp.concatenate([block[t, b : b + 1, lanes] for t in range(TOKENS)] + [zeros], axis=0)

    scores, fresh_scores = [], []
    for b, g in pairs:
        q = jnp.concatenate(
            [
                q32[t, b : b + 1, (g * GROUP + h) * HD : (g * GROUP + h + 1) * HD]
                for t in range(TOKENS)
                for h in range(GROUP)
            ],
            axis=0,
        ).astype(jnp.bfloat16)
        s = dot_t(q, keys[b, :, g * HD : (g + 1) * HD]) * inv_root
        position = column * span + lax.broadcasted_iota(jnp.int32, (n, span), 1)
        scores.append(jnp.where(position < sized[b], s, very_low))
        f = dot_t(q, fresh(nk, b, g).astype(jnp.bfloat16)) * inv_root
        token = lax.broadcasted_iota(jnp.int32, (n, 8), 0) // GROUP
        slot = lax.broadcasted_iota(jnp.int32, (n, 8), 1)
        seen = jnp.logical_and(slot <= token, column == 0)
        fresh_scores.append(jnp.where(seen, f, very_low))
    scores = jnp.concatenate(scores, axis=0)
    fresh_scores = jnp.concatenate(fresh_scores, axis=0)
    peak = jnp.maximum(
        jnp.max(scores, axis=1, keepdims=True), jnp.max(fresh_scores, axis=1, keepdims=True)
    )
    weights = jnp.where(scores > 0.5 * very_low, jnp.exp(scores - peak), 0.0)
    fresh_weights = jnp.where(fresh_scores > 0.5 * very_low, jnp.exp(fresh_scores - peak), 0.0)
    total = jnp.sum(weights, axis=1, keepdims=True) + jnp.sum(fresh_weights, axis=1, keepdims=True)

    def halves(w):
        high = w.astype(jnp.bfloat16)
        low = (w - high.astype(jnp.float32)).astype(jnp.bfloat16)
        return jnp.concatenate([high, low], axis=0)

    lane = lax.broadcasted_iota(jnp.int32, (GROUP, HD), 1)
    stats = [jnp.zeros((GROUP, HD), jnp.float32) for _ in range(heads)]
    copies[4].wait()
    for i, (b, g) in enumerate(pairs):
        here = slice(i * n, (i + 1) * n)
        s = dot(halves(weights[here]), values[b, :, g * HD : (g + 1) * HD])
        s = s + dot(halves(fresh_weights[here]), fresh(nv, b, g).astype(jnp.bfloat16))
        s = s[:n] + s[n:]
        for t in range(TOKENS):
            tb = t * rows + b
            part = slice(i * n + t * GROUP, i * n + (t + 1) * GROUP)
            stats[g] = jnp.where(lane == 2 * tb, peak[part], stats[g])
            stats[g] = jnp.where(lane == 2 * tb + 1, total[part], stats[g])
            block = s[t * GROUP : (t + 1) * GROUP]
            if hb >= GROUP:
                at = g * GROUP
                packed[at // hb, tb, at % hb : at % hb + GROUP] = block
            else:
                for j in range(GROUP // hb):
                    packed[g * (GROUP // hb) + j, tb] = block[j * hb : (j + 1) * hb]
    for g in range(heads):
        if hb >= GROUP:
            at = g * GROUP
            packed[at // hb, TOKENS * rows, at % hb : at % hb + GROUP] = stats[g]
        else:
            for j in range(GROUP // hb):
                packed[g * (GROUP // hb) + j, TOKENS * rows] = stats[g][j * hb : (j + 1) * hb]
    for k in range(half):
        outs[k][...] = packed[jnp.bitwise_xor(column % half, k)]


def combine_kernel(cols, *refs):
    parts, out = refs[:cols], refs[cols]
    cells = parts[0].shape[0] - 1
    hb = parts[0].shape[1]
    stats = [p[cells] for p in parts]
    attended = []
    for tb in range(cells):
        peaks = [s[:, 2 * tb : 2 * tb + 1] for s in stats]
        totals = [s[:, 2 * tb + 1 : 2 * tb + 2] for s in stats]
        top = functools.reduce(jnp.maximum, peaks)
        scales = [jnp.exp(p - top) for p in peaks]
        total = tree_sum([t * s for t, s in zip(totals, scales)])
        summed = tree_sum([p[tb] * s for p, s in zip(parts, scales)])
        attended.append(summed / total)
    rows = [
        jnp.concatenate([attended[tb][h : h + 1] for tb in range(cells)], axis=0) for h in range(hb)
    ]
    out[...] = jnp.concatenate(rows, axis=1).astype(out.dtype)


def group_order(value, groups):
    here = value.shape[1] // groups
    return jnp.concatenate(
        [value[t, r * here : (r + 1) * here] for r in range(groups) for t in range(TOKENS)], axis=0
    )


def canonical(parts, canon, me):
    cells = parts[0].shape[0]
    for k, part in enumerate(parts):
        canon[jnp.bitwise_xor(me, k), :cells] = part[...].astype(jnp.float32)
    rows = [canon[r, :cells] for r in range(len(parts))]
    return jnp.concatenate(rows, axis=0).astype(jnp.bfloat16)


def over_columns(width, body):
    size = width // 2 if width % 256 == 0 else width

    def step(j, carry):
        body(pl.multiple_of(j * size, 128), size)
        return carry

    lax.fori_loop(0, width // size, step, 0)


def out_kernel(groups, *refs):
    parts, (weight, out, canon, attended) = refs[:groups], refs[groups:]
    attended[...] = canonical(parts, canon, lax.axis_index("row"))

    def body(at, size):
        out[:, pl.ds(at, size)] = dot(attended[...], weight[:, pl.ds(at, size)]).astype(out.dtype)

    over_columns(out.shape[1], body)


def in_pieces(squares):
    first = squares.astype(WIRE).astype(jnp.float32)
    second = (squares - first).astype(WIRE).astype(jnp.float32)
    third = squares - first - second
    lane = lax.broadcasted_iota(jnp.int32, (squares.shape[0], HD), 1)
    return jnp.where(
        lane == 0, first, jnp.where(lane == 1, second, jnp.where(lane == 2, third, 0.0))
    )


def lift_kernel(groups, split, residual, gains, gate_weight, up_weight, *refs):
    parts, (mid_out, keep, send, lifted, packed) = refs[:-5], refs[-5:]
    hidden = gate_weight.shape[1] // split
    start = lax.axis_index("side") * hidden if split > 1 else 0
    half = packed.shape[1] // 2
    mid = tree_sum([p[...].astype(jnp.float32) for p in parts])
    mid = group_order(residual[...].astype(jnp.float32), groups) + mid
    mid_out[...] = mid
    sent = in_pieces(jnp.sum(mid * mid, axis=1, keepdims=True))
    lifted[...] = (mid * gains[...].astype(jnp.float32).reshape(1, mid.shape[1])).astype(jnp.bfloat16)
    for i in range(2):
        piece = sent[i * half : (i + 1) * half]
        packed[i, :, hidden:] = jnp.concatenate([piece, piece], axis=0)

    def body(at, size):
        block = pl.ds(pl.multiple_of(start + at, 128), size)
        gate = dot(lifted[...], gate_weight[:, block])
        up = dot(lifted[...], up_weight[:, block])
        for i in range(2):
            rows = slice(i * half, (i + 1) * half)
            packed[i, :, pl.ds(at, size)] = jnp.concatenate([gate[rows], up[rows]], axis=0)

    over_columns(hidden, body)
    bit = lax.axis_index("row") & 1
    keep[...] = packed[bit].astype(keep.dtype)
    send[...] = packed[1 - bit].astype(send.dtype)


def act_kernel(model, *refs):
    parts, out = refs[:-1], refs[-1]
    hidden = parts[0].shape[1] - HD
    cells = parts[0].shape[0] // 2
    values = [p[...].astype(jnp.float32) for p in parts]
    total = tree_sum(values[0::2]) + tree_sum(values[1::2])
    squares = jnp.sum(total[:cells, hidden:], axis=1, keepdims=True)
    inv = lax.rsqrt(squares / model + 1e-05)
    gate = total[:cells, :hidden] * inv
    up = total[cells:, :hidden] * inv
    out[...] = (gate / (1.0 + jnp.exp(-gate)) * up).astype(out.dtype)


def gather_kernel(own, received, out, packed):
    bit = lax.axis_index("row") & 1
    packed[bit] = own[...].astype(jnp.float32)
    packed[1 - bit] = received[...].astype(jnp.float32)
    out[...] = jnp.concatenate([packed[0], packed[1]], axis=0).astype(out.dtype)


def down_kernel(other, act, weight, *refs):
    out = refs[-1]
    hidden = act.shape[1]
    start = 0
    if weight.shape[0] > hidden:
        start = pl.multiple_of(jnp.bitwise_xor(lax.axis_index("side"), other) * hidden, 128)

    def body(at, size):
        product = dot(act[...], weight[pl.ds(start, hidden), pl.ds(at, size)])
        if len(refs) > 1:
            product = product + refs[0][:, pl.ds(at, size)]
        out[:, pl.ds(at, size)] = product.astype(out.dtype)

    over_columns(out.shape[1], body)


def final_kernel(groups, mid, *refs):
    parts, out = refs[:-1], refs[-1]
    total = mid[...] + tree_sum([p[...].astype(jnp.float32) for p in parts])
    here = out.shape[1] // groups
    for t in range(TOKENS):
        block = [
            total[(r * TOKENS + t) * here : (r * TOKENS + t + 1) * here] for r in range(groups)
        ]
        out[t] = jnp.concatenate(block, axis=0).astype(out.dtype)


def shards(
    query,
    new_keys,
    new_values,
    key_cache,
    value_cache,
    lengths,
    residual,
    out_weight,
    norm_gain,
    gate_weight,
    up_weight,
    down_weight,
):
    sides, groups, cols = (lax.axis_size(a) for a in ("side", "row", "col"))
    rows_here = key_cache.shape[0]
    total_rows = residual.shape[1]
    width_share = residual.shape[2]
    hidden_share = gate_weight.shape[1]
    features = out_weight.shape[0]
    model = width_share * groups
    m = TOKENS * total_rows
    cells = TOKENS * rows_here
    hb = HEADS // cols
    split = 2 if sides == 2 and (hidden_share // 2) % 128 == 0 else 1
    hidden = hidden_share // split
    f32, bf16 = jnp.float32, jnp.bfloat16
    shape = jax.ShapeDtypeStruct
    pad = -(-cells // 8) * 8

    sources = [query, new_keys, new_values, key_cache, value_cache]
    message = shape((cells + 1, hb, HD), f32)
    sources = [query, new_keys, new_values, key_cache, value_cache]

    def messages(far):
        return call(
            functools.partial(attention_kernel, cols, far),
            [message] * (cols // 2),
            [ANY_SPEC] * 6,
            [pltpu.VMEM((*a.shape[:2], a.shape[2] // 2), a.dtype) for a in sources]
            + [pltpu.SMEM(lengths.shape, lengths.dtype)]
            + [pltpu.VMEM((cols // 2, *message.shape), f32), pltpu.SemaphoreType.DMA((6,))],
            name="attention_far" if far else "attention_near",
        )(*[in_hbm(a) for a in [lengths, *sources]])

    parts = messages(1)
    parts = [partner(parts[k], "col", cols // 2 + k) for k in range(cols // 2)]
    near = messages(0)
    parts = [near[0]] + [partner(near[k], "col", k) for k in range(1, cols // 2)] + parts
    attended = call(
        functools.partial(combine_kernel, cols),
        shape((cells, features), bf16),
        [VMEM_SPEC] * cols,
        flops=40 * 10**9,
        name="combine",
    )(*parts)
    gathered = spread(attended, "row")
    partial = call(
        functools.partial(out_kernel, groups),
        shape((m, width_share), WIRE),
        [VMEM_SPEC] * (groups + 1),
        [pltpu.VMEM((groups, pad, features), f32), pltpu.VMEM((m, features), bf16)],
        name="out_projection",
    )(*gathered, in_vmem(out_weight))
    mid, keep, send = call(
        functools.partial(lift_kernel, groups, split),
        [shape((m, width_share), f32)] + [shape((m, hidden + HD), WIRE)] * 2,
        [VMEM_SPEC] * (cols + 4),
        [pltpu.VMEM((m, width_share), bf16), pltpu.VMEM((2, m, hidden + HD), f32)],
        name="gate_up",
    )(
        in_vmem(residual), in_vmem(norm_gain), in_vmem(gate_weight), in_vmem(up_weight),
        *spread(partial, "col"),
    )
    sums = [keep] + [partner((keep, send)[k % 2], "row", k) for k in range(1, groups)]
    act = call(
        functools.partial(act_kernel, model),
        shape((m // 2, hidden), bf16),
        [VMEM_SPEC] * groups,
        name="activation",
    )(*sums)
    down_weight = in_vmem(down_weight)

    def down_part(same, from_row, other, before, result):
        rows = call(
            gather_kernel,
            shape((m, hidden), bf16),
            [VMEM_SPEC] * 2,
            [pltpu.VMEM((2, m // 2, hidden), f32)],
            name="gather_act",
        )(same, from_row)
        return call(
            functools.partial(down_kernel, other),
            shape((m, width_share), result),
            [VMEM_SPEC] * (2 + len(before)),
            name="down",
        )(rows, down_weight, *before)

    near = partner(act, "row", 1)
    if split > 1:
        first = down_part(act, near, 0, [], f32)
        far = partner(act, ("side", "row"), groups + 1)
        down = down_part(partner(act, "side", 1), far, 1, [first], WIRE)
    else:
        down = down_part(act, near, 0, [], WIRE)
    return call(
        functools.partial(final_kernel, groups),
        shape((TOKENS, total_rows, width_share), bf16),
        [VMEM_SPEC] * (cols + 1),
        name="final",
    )(mid, *spread(down, "col"))


def solution(mesh):
    in_specs = (
        P(None, "row", None),
        P(None, "row", None),
        P(None, "row", None),
        P("row", "col", None),
        P("row", "col", None),
        P("row"),
        P(None, None, "row"),
        P("col", "row"),
        P("row"),
        P("row", "col"),
        P("row", "col"),
        P("col", "row"),
    )
    out_specs = P(None, None, "row")
    return jax.shard_map(shards, mesh=mesh, in_specs=in_specs, out_specs=out_specs, check_vma=False)
```

```python
import functools
import math

import jax
import jax.numpy as jnp
from jax import lax
from jax.experimental import pallas as pl
from jax.experimental.pallas import tpu as pltpu
from jax.sharding import PartitionSpec as P

HEADS = 32
KV_HEADS = 4
HD = 128
GROUP = HEADS // KV_HEADS
TOKENS = 2
very_low = -1e30
MIB = 1024 * 1024
WIRE = jnp.bfloat16
VMEM_SPEC = pl.BlockSpec(memory_space=pltpu.VMEM)
ANY_SPEC = pl.BlockSpec(memory_space=pl.ANY)


def partner(value, axis, k):
    return lax.ppermute(value, axis, [(i, i ^ k) for i in range(lax.axis_size(axis))])


def spread(piece, axis):
    return [piece] + [partner(piece, axis, k) for k in range(1, lax.axis_size(axis))]


def tree_sum(values):
    while len(values) > 1:
        values = [values[i] + values[i + 1] for i in range(0, len(values), 2)]
    return values[0]


def dot(a, b):
    return jnp.dot(a, b, preferred_element_type=jnp.float32)


def dot_t(a, b):
    return lax.dot_general(a, b, (((1,), (1,)), ((), ())), preferred_element_type=jnp.float32)


def pieces(value):
    first = value.astype(WIRE).astype(jnp.float32)
    second = (value - first).astype(WIRE).astype(jnp.float32)
    return first, second, value - first - second


def call(kernel, out_shape, in_specs, scratch=(), limit=4, name=None, flops=None):
    cost = None
    if flops is not None:
        cost = pl.CostEstimate(flops=flops, bytes_accessed=1024, transcendentals=0)
    return pl.pallas_call(
        kernel,
        out_shape=out_shape,
        in_specs=in_specs,
        out_specs=jax.tree.map(lambda _: VMEM_SPEC, out_shape),
        scratch_shapes=list(scratch),
        compiler_params=pltpu.CompilerParams(vmem_limit_bytes=limit * MIB),
        cost_estimate=cost,
        name=name,
    )


def in_hbm(value):
    return pltpu.with_memory_space_constraint(value, pltpu.HBM)


def in_vmem(value):
    return pltpu.with_memory_space_constraint(value, pltpu.VMEM)


def attention_kernel(cols, far, lengths, *rest):
    half = cols // 2
    sources, outs = rest[:5], rest[5 : 5 + half]
    held, (sized, packed, sems) = rest[5 + half : 10 + half], rest[10 + half :]
    column = lax.axis_index("col")
    heads = KV_HEADS // 2
    part = jnp.bitwise_xor(column // half, far)

    def lanes(source):
        width = source.shape[2] // 2
        return source.at[:, :, pl.ds(pl.multiple_of(part * width, 128), width)]

    copies = [
        pltpu.make_async_copy(lanes(source), target, sems.at[i])
        for i, (source, target) in enumerate(zip(sources, held))
    ]
    copies.append(pltpu.make_async_copy(lengths, sized, sems.at[5]))
    for copy in copies:
        copy.start()
    query, new_keys, new_values, keys, values = held
    rows, span, _ = keys.shape
    hb = HEADS // cols
    inv_root = 1.0 / math.sqrt(HD)
    n = TOKENS * GROUP
    cells = TOKENS * rows
    pairs = [(b, g) for b in range(rows) for g in range(heads)]
    for i in (0, 1, 2, 5, 3):
        copies[i].wait()
    q32 = query[...].astype(jnp.float32)
    nk, nv = new_keys[...].astype(jnp.float32), new_values[...].astype(jnp.float32)
    zeros = jnp.zeros((8 - TOKENS, HD), jnp.float32)

    def fresh(block, b, g):
        lanes = slice(g * HD, (g + 1) * HD)
        return jnp.concatenate([block[t, b : b + 1, lanes] for t in range(TOKENS)] + [zeros], axis=0)

    scores, fresh_scores = [], []
    for b, g in pairs:
        q = jnp.concatenate(
            [
                q32[t, b : b + 1, (g * GROUP + h) * HD : (g * GROUP + h + 1) * HD]
                for t in range(TOKENS)
                for h in range(GROUP)
            ],
            axis=0,
        ).astype(jnp.bfloat16)
        s = dot_t(q, keys[b, :, g * HD : (g + 1) * HD]) * inv_root
        position = column * span + lax.broadcasted_iota(jnp.int32, (n, span), 1)
        scores.append(jnp.where(position < sized[b], s, very_low))
        f = dot_t(q, fresh(nk, b, g).astype(jnp.bfloat16)) * inv_root
        token = lax.broadcasted_iota(jnp.int32, (n, 8), 0) // GROUP
        slot = lax.broadcasted_iota(jnp.int32, (n, 8), 1)
        seen = jnp.logical_and(slot <= token, column == 0)
        fresh_scores.append(jnp.where(seen, f, very_low))
    scores = jnp.concatenate(scores, axis=0)
    fresh_scores = jnp.concatenate(fresh_scores, axis=0)
    peak = jnp.maximum(
        jnp.max(scores, axis=1, keepdims=True), jnp.max(fresh_scores, axis=1, keepdims=True)
    )
    weights = jnp.where(scores > 0.5 * very_low, jnp.exp(scores - peak), 0.0)
    fresh_weights = jnp.where(fresh_scores > 0.5 * very_low, jnp.exp(fresh_scores - peak), 0.0)
    total = jnp.sum(weights, axis=1, keepdims=True) + jnp.sum(fresh_weights, axis=1, keepdims=True)

    def halves(w):
        high = w.astype(jnp.bfloat16)
        low = (w - high.astype(jnp.float32)).astype(jnp.bfloat16)
        return jnp.concatenate([high, low], axis=0)

    lane = lax.broadcasted_iota(jnp.int32, (GROUP, HD), 1)
    stats = [jnp.zeros((GROUP, HD), jnp.float32) for _ in range(heads)]
    copies[4].wait()
    for i, (b, g) in enumerate(pairs):
        here = slice(i * n, (i + 1) * n)
        s = dot(halves(weights[here]), values[b, :, g * HD : (g + 1) * HD])
        s = s + dot(halves(fresh_weights[here]), fresh(nv, b, g).astype(jnp.bfloat16))
        s = s[:n] + s[n:]
        for t in range(TOKENS):
            tb = t * rows + b
            part = slice(i * n + t * GROUP, i * n + (t + 1) * GROUP)
            for i_piece, pair in enumerate(zip(pieces(peak[part]), pieces(total[part]))):
                at = 2 * (cells * i_piece + tb)
                stats[g] = jnp.where(lane == at, pair[0], stats[g])
                stats[g] = jnp.where(lane == at + 1, pair[1], stats[g])
            block = s[t * GROUP : (t + 1) * GROUP].astype(WIRE)
            if hb >= GROUP:
                at = g * GROUP
                packed[at // hb, tb, at % hb : at % hb + GROUP] = block
            else:
                for j in range(GROUP // hb):
                    packed[g * (GROUP // hb) + j, tb] = block[j * hb : (j + 1) * hb]
    stats = [block.astype(WIRE) for block in stats]
    for g in range(heads):
        if hb >= GROUP:
            at = g * GROUP
            packed[at // hb, TOKENS * rows, at % hb : at % hb + GROUP] = stats[g]
        else:
            for j in range(GROUP // hb):
                packed[g * (GROUP // hb) + j, TOKENS * rows] = stats[g][j * hb : (j + 1) * hb]
    for k in range(half):
        outs[k][...] = packed[jnp.bitwise_xor(column % half, k)]


def combine_kernel(cols, *refs):
    parts, out = refs[:cols], refs[cols]
    cells = parts[0].shape[0] - 1
    hb = parts[0].shape[1]
    stats = [p[cells].astype(jnp.float32) for p in parts]
    n = 2 * cells
    stats = [s[:, :n] + s[:, n : 2 * n] + s[:, 2 * n : 3 * n] for s in stats]
    attended = []
    for tb in range(cells):
        peaks = [s[:, 2 * tb : 2 * tb + 1] for s in stats]
        totals = [s[:, 2 * tb + 1 : 2 * tb + 2] for s in stats]
        top = functools.reduce(jnp.maximum, peaks)
        scales = [jnp.exp(p - top) for p in peaks]
        total = tree_sum([t * s for t, s in zip(totals, scales)])
        summed = tree_sum([p[tb].astype(jnp.float32) * s for p, s in zip(parts, scales)])
        attended.append(summed / total)
    rows = [
        jnp.concatenate([attended[tb][h : h + 1] for tb in range(cells)], axis=0) for h in range(hb)
    ]
    out[...] = jnp.concatenate(rows, axis=1).astype(out.dtype)


def group_order(value, groups):
    here = value.shape[1] // groups
    return jnp.concatenate(
        [value[t, r * here : (r + 1) * here] for r in range(groups) for t in range(TOKENS)], axis=0
    )


def canonical(parts, canon, me):
    cells = parts[0].shape[0]
    for k, part in enumerate(parts):
        canon[jnp.bitwise_xor(me, k), :cells] = part[...].astype(jnp.float32)
    rows = [canon[r, :cells] for r in range(len(parts))]
    return jnp.concatenate(rows, axis=0).astype(jnp.bfloat16)


def over_columns(width, body):
    size = width // 2 if width % 256 == 0 else width

    def step(j, carry):
        body(pl.multiple_of(j * size, 128), size)
        return carry

    lax.fori_loop(0, width // size, step, 0)


def out_kernel(groups, *refs):
    parts, (weight, out, canon, attended) = refs[:groups], refs[groups:]
    attended[...] = canonical(parts, canon, lax.axis_index("row"))

    def body(at, size):
        out[:, pl.ds(at, size)] = dot(attended[...], weight[:, pl.ds(at, size)]).astype(out.dtype)

    over_columns(out.shape[1], body)


def in_pieces(squares):
    lane = lax.broadcasted_iota(jnp.int32, (squares.shape[0], HD), 1)
    result = jnp.zeros(lane.shape, jnp.float32)
    for i, piece in enumerate(pieces(squares)):
        result = jnp.where(lane == i, piece, result)
    return result


def add_kernel(first, second, out):
    out[...] = (first[...].astype(jnp.float32) + second[...].astype(jnp.float32)).astype(out.dtype)


def lift_kernel(groups, cols, split, residual, gains, gate_weight, up_weight, *refs):
    parts, mid_out, (lifted, packed) = refs[:cols], refs[cols], refs[-2:]
    outs = refs[cols + 1 : -2]
    hidden = gate_weight.shape[1] // split
    start = lax.axis_index("side") * hidden if split > 1 else 0
    half = packed.shape[1] // 2
    mid = tree_sum([p[...].astype(jnp.float32) for p in parts])
    mid = group_order(residual[...].astype(jnp.float32), groups) + mid
    mid_out[...] = mid
    sent = in_pieces(jnp.sum(mid * mid, axis=1, keepdims=True))
    lifted[...] = (mid * gains[...].astype(jnp.float32).reshape(1, mid.shape[1])).astype(jnp.bfloat16)
    for i in range(2):
        piece = sent[i * half : (i + 1) * half]
        packed[i, :, hidden:] = jnp.concatenate([piece, piece], axis=0)

    def body(at, size):
        block = pl.ds(pl.multiple_of(start + at, 128), size)
        gate = dot(lifted[...], gate_weight[:, block])
        up = dot(lifted[...], up_weight[:, block])
        for i in range(2):
            rows = slice(i * half, (i + 1) * half)
            packed[i, :, pl.ds(at, size)] = jnp.concatenate([gate[rows], up[rows]], axis=0)

    over_columns(hidden, body)
    bit = lax.axis_index("row") & 1
    mine, theirs = (packed[i].astype(outs[0].dtype) for i in (bit, 1 - bit))
    for k, out in enumerate(outs):
        out[...] = theirs if k % 2 else mine


def act_kernel(model, *refs):
    parts, out = refs[:1] + refs[-2:0:-1], refs[-1]
    hidden = parts[0].shape[1] - HD
    cells = parts[0].shape[0] // 2
    values = [p[...].astype(jnp.float32) for p in parts]
    total = tree_sum(values[0::2]) + tree_sum(values[1::2])
    squares = jnp.sum(total[:cells, hidden:], axis=1, keepdims=True)
    inv = lax.rsqrt(squares / model + 1e-05)
    gate = total[:cells, :hidden] * inv
    up = total[cells:, :hidden] * inv
    out[...] = (gate / (1.0 + jnp.exp(-gate)) * up).astype(out.dtype)


def gather_kernel(own, received, out, packed):
    bit = lax.axis_index("row") & 1
    packed[bit] = own[...].astype(jnp.float32)
    packed[1 - bit] = received[...].astype(jnp.float32)
    out[...] = jnp.concatenate([packed[0], packed[1]], axis=0).astype(out.dtype)


def down_kernel(other, act, weight, *refs):
    out = refs[-1]
    hidden = act.shape[1]
    start = 0
    if weight.shape[0] > hidden:
        start = pl.multiple_of(jnp.bitwise_xor(lax.axis_index("side"), other) * hidden, 128)

    def body(at, size):
        product = dot(act[...], weight[pl.ds(start, hidden), pl.ds(at, size)])
        if len(refs) > 1:
            product = product + refs[0][:, pl.ds(at, size)]
        out[:, pl.ds(at, size)] = product.astype(out.dtype)

    over_columns(out.shape[1], body)


def final_kernel(groups, mid, *refs):
    parts, out = refs[:-1], refs[-1]
    total = mid[...] + tree_sum([p[...].astype(jnp.float32) for p in parts])
    here = out.shape[1] // groups
    for t in range(TOKENS):
        block = [
            total[(r * TOKENS + t) * here : (r * TOKENS + t + 1) * here] for r in range(groups)
        ]
        out[t] = jnp.concatenate(block, axis=0).astype(out.dtype)


def shards(
    query,
    new_keys,
    new_values,
    key_cache,
    value_cache,
    lengths,
    residual,
    out_weight,
    norm_gain,
    gate_weight,
    up_weight,
    down_weight,
):
    sides, groups, cols = (lax.axis_size(a) for a in ("side", "row", "col"))
    rows_here = key_cache.shape[0]
    total_rows = residual.shape[1]
    width_share = residual.shape[2]
    hidden_share = gate_weight.shape[1]
    features = out_weight.shape[0]
    model = width_share * groups
    m = TOKENS * total_rows
    cells = TOKENS * rows_here
    hb = HEADS // cols
    split = 2 if sides == 2 and (hidden_share // 2) % 128 == 0 else 1
    hidden = hidden_share // split
    f32, bf16 = jnp.float32, jnp.bfloat16
    shape = jax.ShapeDtypeStruct
    pad = -(-cells // 8) * 8

    sources = [query, new_keys, new_values, key_cache, value_cache]
    message = shape((cells + 1, hb, HD), WIRE)
    sources = [query, new_keys, new_values, key_cache, value_cache]

    def messages(far):
        return call(
            functools.partial(attention_kernel, cols, far),
            [message] * (cols // 2),
            [ANY_SPEC] * 6,
            [pltpu.VMEM((*a.shape[:2], a.shape[2] // 2), a.dtype) for a in sources]
            + [pltpu.SMEM(lengths.shape, lengths.dtype)]
            + [pltpu.VMEM((cols // 2, *message.shape), WIRE), pltpu.SemaphoreType.DMA((6,))],
            name="attention_far" if far else "attention_near",
        )(*[in_hbm(a) for a in [lengths, *sources]])

    parts = messages(1)
    parts = [partner(parts[k], "col", cols // 2 + k) for k in range(cols // 2)]
    near = messages(0)
    parts = [near[0]] + [partner(near[k], "col", k) for k in range(1, cols // 2)] + parts
    attended = call(
        functools.partial(combine_kernel, cols),
        shape((cells, features), bf16),
        [VMEM_SPEC] * cols,
        flops=40 * 10**9,
        name="combine",
    )(*parts)
    gathered = spread(attended, "row")
    partial = call(
        functools.partial(out_kernel, groups),
        shape((m, width_share), WIRE),
        [VMEM_SPEC] * (groups + 1),
        [pltpu.VMEM((groups, pad, features), f32), pltpu.VMEM((m, features), bf16)],
        name="out_projection",
    )(*gathered, in_vmem(out_weight))
    mid, *sums = call(
        functools.partial(lift_kernel, groups, cols, split),
        [shape((m, width_share), f32)] + [shape((m, hidden + HD), WIRE)] * groups,
        [VMEM_SPEC] * (cols + 4),
        [pltpu.VMEM((m, width_share), bf16), pltpu.VMEM((2, m, hidden + HD), f32)],
        name="gate_up",
    )(
        in_vmem(residual), in_vmem(norm_gain), in_vmem(gate_weight), in_vmem(up_weight),
        *spread(partial, "col"),
    )
    sums = sums[:1] + [partner(sums[k], "row", k) for k in range(1, groups)]
    act = call(
        functools.partial(act_kernel, model),
        shape((m // 2, hidden), bf16),
        [VMEM_SPEC] * groups,
        name="activation",
    )(sums[0], *sums[:0:-1])
    down_weight = in_vmem(down_weight)

    def down_part(same, from_row, other, before, result):
        rows = call(
            gather_kernel,
            shape((m, hidden), bf16),
            [VMEM_SPEC] * 2,
            [pltpu.VMEM((2, m // 2, hidden), f32)],
            name="gather_act",
        )(same, from_row)
        return call(
            functools.partial(down_kernel, other),
            shape((m, width_share), result),
            [VMEM_SPEC] * (2 + len(before)),
            name="down",
        )(rows, down_weight, *before)

    near = partner(act, "row", 1)
    if split > 1:
        first = down_part(act, near, 0, [], f32)
        far = partner(act, ("side", "row"), groups + 1)
        down = down_part(partner(act, "side", 1), far, 1, [first], WIRE)
    else:
        down = down_part(act, near, 0, [], WIRE)
    step = 1
    while step < cols // 2:
        down = call(add_kernel, shape(down.shape, WIRE), [VMEM_SPEC] * 2, name="add")(
            down, partner(down, "col", 2 * step - 1)
        )
        step *= 2
    return call(
        functools.partial(final_kernel, groups),
        shape((TOKENS, total_rows, width_share), bf16),
        [VMEM_SPEC] * 3,
        name="final",
    )(mid, down, partner(down, "col", 2 * step - 1))


def solution(mesh):
    in_specs = (
        P(None, "row", None),
        P(None, "row", None),
        P(None, "row", None),
        P("row", "col", None),
        P("row", "col", None),
        P("row"),
        P(None, None, "row"),
        P("col", "row"),
        P("row"),
        P("row", "col"),
        P("row", "col"),
        P("col", "row"),
    )
    out_specs = P(None, None, "row")
    return jax.shard_map(shards, mesh=mesh, in_specs=in_specs, out_specs=out_specs, check_vma=False)
```

```python
import functools
import math

import jax
import jax.numpy as jnp
from jax import lax
from jax.experimental import pallas as pl
from jax.experimental.pallas import tpu as pltpu
from jax.sharding import PartitionSpec as P

HEADS = 32
KV_HEADS = 4
HD = 128
GROUP = HEADS // KV_HEADS
TOKENS = 2
very_low = -1e30
MIB = 1024 * 1024
WIRE = jnp.bfloat16
VMEM_SPEC = pl.BlockSpec(memory_space=pltpu.VMEM)
ANY_SPEC = pl.BlockSpec(memory_space=pl.ANY)


def partner(value, axis, k):
    return lax.ppermute(value, axis, [(i, i ^ k) for i in range(lax.axis_size(axis))])


def spread(piece, axis):
    return [piece] + [partner(piece, axis, k) for k in range(1, lax.axis_size(axis))]


def tree_sum(values):
    while len(values) > 1:
        values = [values[i] + values[i + 1] for i in range(0, len(values), 2)]
    return values[0]


def dot(a, b):
    return jnp.dot(a, b, preferred_element_type=jnp.float32)


def dot_t(a, b):
    return lax.dot_general(a, b, (((1,), (1,)), ((), ())), preferred_element_type=jnp.float32)


def call(kernel, out_shape, in_specs, scratch=(), limit=4, name=None, flops=None):
    cost = None
    if flops is not None:
        cost = pl.CostEstimate(flops=flops, bytes_accessed=1024, transcendentals=0)
    return pl.pallas_call(
        kernel,
        out_shape=out_shape,
        in_specs=in_specs,
        out_specs=jax.tree.map(lambda _: VMEM_SPEC, out_shape),
        scratch_shapes=list(scratch),
        compiler_params=pltpu.CompilerParams(vmem_limit_bytes=limit * MIB),
        cost_estimate=cost,
        name=name,
    )


def in_hbm(value):
    return pltpu.with_memory_space_constraint(value, pltpu.HBM)


def in_vmem(value):
    return pltpu.with_memory_space_constraint(value, pltpu.VMEM)


def attention_far_kernel(cols, *refs):
    half = cols // 2
    sources, (lengths, *outs), kept = refs[:5], refs[5 : 6 + half], refs[6 + half : 12 + half]
    held, (sized, packed, sems) = refs[12 + half : 17 + half], refs[17 + half :]
    mine = lax.axis_index("col") // half

    def copies(part, targets, row):
        result = []
        for i, (source, target) in enumerate(zip(sources, targets)):
            width = target.shape[2]
            view = source.at[:, :, pl.ds(pl.multiple_of(part * width, 128), width)]
            result.append(pltpu.make_async_copy(view, target, sems.at[row, i]))
        return result

    far, near = copies(1 - mine, held, 0), copies(mine, kept, 1)
    far.append(pltpu.make_async_copy(lengths, sized, sems.at[0, 5]))
    for copy in far + near:
        copy.start()
    for copy in far:
        copy.wait()
    rows = held[3].shape[0]
    row = lax.broadcasted_iota(jnp.int32, (8, HD), 0)
    limits = jnp.zeros((8, HD), jnp.int32)
    for b in range(rows):
        limits = jnp.where(row == b, sized[b], limits)
    kept[5][...] = limits
    attention(cols, limits, *held, outs, packed)
    for copy in near:
        copy.wait()


def attention_near_kernel(cols, *refs):
    attention(cols, refs[5][...], *refs[:5], refs[6:-1], refs[-1])


def attention(cols, limits, query, new_keys, new_values, keys, values, outs, packed):
    half = cols // 2
    heads = KV_HEADS // 2
    column = lax.axis_index("col")
    rows, span, _ = keys.shape
    hb = HEADS // cols
    inv_root = 1.0 / math.sqrt(HD)
    n = TOKENS * GROUP
    pairs = [(b, g) for b in range(rows) for g in range(heads)]
    q32 = query[...].astype(jnp.float32)
    nk, nv = new_keys[...].astype(jnp.float32), new_values[...].astype(jnp.float32)
    zeros = jnp.zeros((8 - TOKENS, HD), jnp.float32)

    def fresh(block, b, g):
        lanes = slice(g * HD, (g + 1) * HD)
        return jnp.concatenate([block[t, b : b + 1, lanes] for t in range(TOKENS)] + [zeros], axis=0)

    scores, fresh_scores = [], []
    for b, g in pairs:
        q = jnp.concatenate(
            [
                q32[t, b : b + 1, (g * GROUP + h) * HD : (g * GROUP + h + 1) * HD]
                for t in range(TOKENS)
                for h in range(GROUP)
            ],
            axis=0,
        ).astype(jnp.bfloat16)
        s = dot_t(q, keys[b, :, g * HD : (g + 1) * HD]) * inv_root
        position = column * span + lax.broadcasted_iota(jnp.int32, (n, span), 1)
        scores.append(jnp.where(position < limits[b : b + 1, :1], s, very_low))
        f = dot_t(q, fresh(nk, b, g).astype(jnp.bfloat16)) * inv_root
        token = lax.broadcasted_iota(jnp.int32, (n, 8), 0) // GROUP
        slot = lax.broadcasted_iota(jnp.int32, (n, 8), 1)
        seen = jnp.logical_and(slot <= token, column == 0)
        fresh_scores.append(jnp.where(seen, f, very_low))
    scores = jnp.concatenate(scores, axis=0)
    fresh_scores = jnp.concatenate(fresh_scores, axis=0)
    peak = jnp.maximum(
        jnp.max(scores, axis=1, keepdims=True), jnp.max(fresh_scores, axis=1, keepdims=True)
    )
    weights = jnp.where(scores > 0.5 * very_low, jnp.exp(scores - peak), 0.0)
    fresh_weights = jnp.where(fresh_scores > 0.5 * very_low, jnp.exp(fresh_scores - peak), 0.0)
    total = jnp.sum(weights, axis=1, keepdims=True) + jnp.sum(fresh_weights, axis=1, keepdims=True)

    def halves(w):
        high = w.astype(jnp.bfloat16)
        low = (w - high.astype(jnp.float32)).astype(jnp.bfloat16)
        return jnp.concatenate([high, low], axis=0)

    lane = lax.broadcasted_iota(jnp.int32, (GROUP, HD), 1)
    stats = [jnp.zeros((GROUP, HD), jnp.float32) for _ in range(heads)]
    for i, (b, g) in enumerate(pairs):
        here = slice(i * n, (i + 1) * n)
        s = dot(halves(weights[here]), values[b, :, g * HD : (g + 1) * HD])
        s = s + dot(halves(fresh_weights[here]), fresh(nv, b, g).astype(jnp.bfloat16))
        s = s[:n] + s[n:]
        for t in range(TOKENS):
            tb = t * rows + b
            part = slice(i * n + t * GROUP, i * n + (t + 1) * GROUP)
            stats[g] = jnp.where(lane == 2 * tb, peak[part], stats[g])
            stats[g] = jnp.where(lane == 2 * tb + 1, total[part], stats[g])
            block = s[t * GROUP : (t + 1) * GROUP]
            if hb >= GROUP:
                at = g * GROUP
                packed[at // hb, tb, at % hb : at % hb + GROUP] = block
            else:
                for j in range(GROUP // hb):
                    packed[g * (GROUP // hb) + j, tb] = block[j * hb : (j + 1) * hb]
    for g in range(heads):
        if hb >= GROUP:
            at = g * GROUP
            packed[at // hb, TOKENS * rows, at % hb : at % hb + GROUP] = stats[g]
        else:
            for j in range(GROUP // hb):
                packed[g * (GROUP // hb) + j, TOKENS * rows] = stats[g][j * hb : (j + 1) * hb]
    for k in range(half):
        outs[k][...] = packed[jnp.bitwise_xor(column % half, k)]


def combine_kernel(cols, *refs):
    parts, out = refs[:cols], refs[cols]
    cells = parts[0].shape[0] - 1
    hb = parts[0].shape[1]
    stats = [p[cells] for p in parts]
    attended = []
    for tb in range(cells):
        peaks = [s[:, 2 * tb : 2 * tb + 1] for s in stats]
        totals = [s[:, 2 * tb + 1 : 2 * tb + 2] for s in stats]
        top = functools.reduce(jnp.maximum, peaks)
        scales = [jnp.exp(p - top) for p in peaks]
        total = tree_sum([t * s for t, s in zip(totals, scales)])
        summed = tree_sum([p[tb] * s for p, s in zip(parts, scales)])
        attended.append(summed / total)
    rows = [
        jnp.concatenate([attended[tb][h : h + 1] for tb in range(cells)], axis=0) for h in range(hb)
    ]
    out[...] = jnp.concatenate(rows, axis=1).astype(out.dtype)


def group_order(value, groups):
    here = value.shape[1] // groups
    return jnp.concatenate(
        [value[t, r * here : (r + 1) * here] for r in range(groups) for t in range(TOKENS)], axis=0
    )


def canonical(parts, canon, me):
    cells = parts[0].shape[0]
    for k, part in enumerate(parts):
        canon[jnp.bitwise_xor(me, k), :cells] = part[...].astype(jnp.float32)
    rows = [canon[r, :cells] for r in range(len(parts))]
    return jnp.concatenate(rows, axis=0).astype(jnp.bfloat16)


def over_columns(width, body):
    size = width // 2 if width % 256 == 0 else width

    def step(j, carry):
        body(pl.multiple_of(j * size, 128), size)
        return carry

    lax.fori_loop(0, width // size, step, 0)


def out_kernel(groups, *refs):
    parts, (weight, out, canon, attended) = refs[:groups], refs[groups:]
    attended[...] = canonical(parts, canon, lax.axis_index("row"))

    def body(at, size):
        out[:, pl.ds(at, size)] = dot(attended[...], weight[:, pl.ds(at, size)]).astype(out.dtype)

    over_columns(out.shape[1], body)


def in_pieces(squares):
    first = squares.astype(WIRE).astype(jnp.float32)
    second = (squares - first).astype(WIRE).astype(jnp.float32)
    third = squares - first - second
    lane = lax.broadcasted_iota(jnp.int32, (squares.shape[0], HD), 1)
    return jnp.where(
        lane == 0, first, jnp.where(lane == 1, second, jnp.where(lane == 2, third, 0.0))
    )


def lift_kernel(groups, split, residual, gains, gate_weight, up_weight, *refs):
    parts, (mid_out, keep, send, lifted, packed) = refs[:-5], refs[-5:]
    hidden = gate_weight.shape[1] // split
    start = lax.axis_index("side") * hidden if split > 1 else 0
    half = packed.shape[1] // 2
    mid = tree_sum([p[...].astype(jnp.float32) for p in parts])
    mid = group_order(residual[...].astype(jnp.float32), groups) + mid
    mid_out[...] = mid
    sent = in_pieces(jnp.sum(mid * mid, axis=1, keepdims=True))
    lifted[...] = (mid * gains[...].astype(jnp.float32).reshape(1, mid.shape[1])).astype(jnp.bfloat16)
    for i in range(2):
        piece = sent[i * half : (i + 1) * half]
        packed[i, :, hidden:] = jnp.concatenate([piece, piece], axis=0)

    def body(at, size):
        block = pl.ds(pl.multiple_of(start + at, 128), size)
        gate = dot(lifted[...], gate_weight[:, block])
        up = dot(lifted[...], up_weight[:, block])
        for i in range(2):
            rows = slice(i * half, (i + 1) * half)
            packed[i, :, pl.ds(at, size)] = jnp.concatenate([gate[rows], up[rows]], axis=0)

    over_columns(hidden, body)
    bit = lax.axis_index("row") & 1
    keep[...] = packed[bit].astype(keep.dtype)
    send[...] = packed[1 - bit].astype(send.dtype)


def act_kernel(model, *refs):
    parts, out = refs[:-1], refs[-1]
    hidden = parts[0].shape[1] - HD
    cells = parts[0].shape[0] // 2
    values = [p[...].astype(jnp.float32) for p in parts]
    total = tree_sum(values[0::2]) + tree_sum(values[1::2])
    squares = jnp.sum(total[:cells, hidden:], axis=1, keepdims=True)
    inv = lax.rsqrt(squares / model + 1e-05)
    gate = total[:cells, :hidden] * inv
    up = total[cells:, :hidden] * inv
    out[...] = (gate / (1.0 + jnp.exp(-gate)) * up).astype(out.dtype)


def gather_kernel(own, received, out, packed):
    bit = lax.axis_index("row") & 1
    packed[bit] = own[...].astype(jnp.float32)
    packed[1 - bit] = received[...].astype(jnp.float32)
    out[...] = jnp.concatenate([packed[0], packed[1]], axis=0).astype(out.dtype)


def down_kernel(other, act, weight, *refs):
    out = refs[-1]
    hidden = act.shape[1]
    start = 0
    if weight.shape[0] > hidden:
        start = pl.multiple_of(jnp.bitwise_xor(lax.axis_index("side"), other) * hidden, 128)

    def body(at, size):
        product = dot(act[...], weight[pl.ds(start, hidden), pl.ds(at, size)])
        if len(refs) > 1:
            product = product + refs[0][:, pl.ds(at, size)]
        out[:, pl.ds(at, size)] = product.astype(out.dtype)

    over_columns(out.shape[1], body)


def final_kernel(groups, mid, *refs):
    parts, out = refs[:-1], refs[-1]
    total = mid[...] + tree_sum([p[...].astype(jnp.float32) for p in parts])
    here = out.shape[1] // groups
    for t in range(TOKENS):
        block = [
            total[(r * TOKENS + t) * here : (r * TOKENS + t + 1) * here] for r in range(groups)
        ]
        out[t] = jnp.concatenate(block, axis=0).astype(out.dtype)


def shards(
    query,
    new_keys,
    new_values,
    key_cache,
    value_cache,
    lengths,
    residual,
    out_weight,
    norm_gain,
    gate_weight,
    up_weight,
    down_weight,
):
    sides, groups, cols = (lax.axis_size(a) for a in ("side", "row", "col"))
    rows_here = key_cache.shape[0]
    total_rows = residual.shape[1]
    width_share = residual.shape[2]
    hidden_share = gate_weight.shape[1]
    features = out_weight.shape[0]
    model = width_share * groups
    m = TOKENS * total_rows
    cells = TOKENS * rows_here
    hb = HEADS // cols
    split = 2 if sides == 2 and (hidden_share // 2) % 128 == 0 else 1
    hidden = hidden_share // split
    f32, bf16 = jnp.float32, jnp.bfloat16
    shape = jax.ShapeDtypeStruct
    pad = -(-cells // 8) * 8

    sources = [query, new_keys, new_values, key_cache, value_cache]
    message = shape((cells + 1, hb, HD), f32)
    sources = [query, new_keys, new_values, key_cache, value_cache]

    inputs = [pltpu.VMEM((*a.shape[:2], a.shape[2] // 2), a.dtype) for a in sources]
    packed = pltpu.VMEM((cols // 2, *message.shape), f32)
    result = call(
        functools.partial(attention_far_kernel, cols),
        [message] * (cols // 2) + inputs + [pltpu.VMEM((8, HD), jnp.int32)],
        [ANY_SPEC] * 6,
        inputs
        + [pltpu.SMEM(lengths.shape, lengths.dtype), packed, pltpu.SemaphoreType.DMA((2, 6))],
        limit=8,
        name="attention_far",
    )(*[in_hbm(a) for a in [*sources, lengths]])
    far, inputs = result[: cols // 2], result[cols // 2 :]
    far = [partner(far[k], "col", cols // 2 + k) for k in range(cols // 2)]
    near = call(
        functools.partial(attention_near_kernel, cols),
        [message] * (cols // 2),
        [VMEM_SPEC] * 6,
        [packed],
        name="attention_near",
    )(*[in_vmem(a) for a in inputs])
    parts = far + [near[0]] + [partner(near[k], "col", k) for k in range(1, cols // 2)]
    attended = call(
        functools.partial(combine_kernel, cols),
        shape((cells, features), bf16),
        [VMEM_SPEC] * cols,
        flops=40 * 10**9,
        name="combine",
    )(*parts)
    gathered = spread(attended, "row")
    partial = call(
        functools.partial(out_kernel, groups),
        shape((m, width_share), WIRE),
        [VMEM_SPEC] * (groups + 1),
        [pltpu.VMEM((groups, pad, features), f32), pltpu.VMEM((m, features), bf16)],
        name="out_projection",
    )(*gathered, in_vmem(out_weight))
    mid, keep, send = call(
        functools.partial(lift_kernel, groups, split),
        [shape((m, width_share), f32)] + [shape((m, hidden + HD), WIRE)] * 2,
        [VMEM_SPEC] * (cols + 4),
        [pltpu.VMEM((m, width_share), bf16), pltpu.VMEM((2, m, hidden + HD), f32)],
        name="gate_up",
    )(
        in_vmem(residual), in_vmem(norm_gain), in_vmem(gate_weight), in_vmem(up_weight),
        *spread(partial, "col"),
    )
    sums = [keep] + [partner((keep, send)[k % 2], "row", k) for k in range(1, groups)]
    act = call(
        functools.partial(act_kernel, model),
        shape((m // 2, hidden), bf16),
        [VMEM_SPEC] * groups,
        name="activation",
    )(*sums)
    down_weight = in_vmem(down_weight)

    def down_part(same, from_row, other, before, result):
        rows = call(
            gather_kernel,
            shape((m, hidden), bf16),
            [VMEM_SPEC] * 2,
            [pltpu.VMEM((2, m // 2, hidden), f32)],
            name="gather_act",
        )(same, from_row)
        return call(
            functools.partial(down_kernel, other),
            shape((m, width_share), result),
            [VMEM_SPEC] * (2 + len(before)),
            name="down",
        )(rows, down_weight, *before)

    near = partner(act, "row", 1)
    if split > 1:
        first = down_part(act, near, 0, [], f32)
        far = partner(act, ("side", "row"), groups + 1)
        down = down_part(partner(act, "side", 1), far, 1, [first], WIRE)
    else:
        down = down_part(act, near, 0, [], WIRE)
    return call(
        functools.partial(final_kernel, groups),
        shape((TOKENS, total_rows, width_share), bf16),
        [VMEM_SPEC] * (cols + 1),
        name="final",
    )(mid, *spread(down, "col"))


def solution(mesh):
    in_specs = (
        P(None, "row", None),
        P(None, "row", None),
        P(None, "row", None),
        P("row", "col", None),
        P("row", "col", None),
        P("row"),
        P(None, None, "row"),
        P("col", "row"),
        P("row"),
        P("row", "col"),
        P("row", "col"),
        P("col", "row"),
    )
    out_specs = P(None, None, "row")
    return jax.shard_map(shards, mesh=mesh, in_specs=in_specs, out_specs=out_specs, check_vma=False)
```

```python
import functools
import math

import jax
import jax.numpy as jnp
from jax import lax
from jax.experimental import pallas as pl
from jax.experimental.pallas import tpu as pltpu
from jax.sharding import PartitionSpec as P

HEADS = 32
KV_HEADS = 4
HD = 128
GROUP = HEADS // KV_HEADS
TOKENS = 2
very_low = -1e30
MIB = 1024 * 1024
WIRE = jnp.bfloat16
VMEM_SPEC = pl.BlockSpec(memory_space=pltpu.VMEM)
ANY_SPEC = pl.BlockSpec(memory_space=pl.ANY)


def partner(value, axis, k):
    return lax.ppermute(value, axis, [(i, i ^ k) for i in range(lax.axis_size(axis))])


def spread(piece, axis):
    return [piece] + [partner(piece, axis, k) for k in range(1, lax.axis_size(axis))]


def tree_sum(values):
    while len(values) > 1:
        values = [values[i] + values[i + 1] for i in range(0, len(values), 2)]
    return values[0]


def dot(a, b):
    return jnp.dot(a, b, preferred_element_type=jnp.float32)


def dot_t(a, b):
    return lax.dot_general(a, b, (((1,), (1,)), ((), ())), preferred_element_type=jnp.float32)


def call(kernel, out_shape, in_specs, scratch=(), limit=4, name=None, flops=None):
    cost = None
    if flops is not None:
        cost = pl.CostEstimate(flops=flops, bytes_accessed=1024, transcendentals=0)
    return pl.pallas_call(
        kernel,
        out_shape=out_shape,
        in_specs=in_specs,
        out_specs=jax.tree.map(lambda _: VMEM_SPEC, out_shape),
        scratch_shapes=list(scratch),
        compiler_params=pltpu.CompilerParams(vmem_limit_bytes=limit * MIB),
        cost_estimate=cost,
        name=name,
    )


def in_hbm(value):
    return pltpu.with_memory_space_constraint(value, pltpu.HBM)


def in_vmem(value):
    return pltpu.with_memory_space_constraint(value, pltpu.VMEM)


def attention_far_kernel(cols, *refs):
    half = cols // 2
    sources, (lengths, *outs), kept = refs[:5], refs[5 : 6 + half], refs[6 + half : 12 + half]
    held, (sized, packed, sems) = refs[12 + half : 17 + half], refs[17 + half :]
    mine = lax.axis_index("col") // half

    def copies(part, targets, row):
        result = []
        for i, (source, target) in enumerate(zip(sources, targets)):
            width = target.shape[2]
            view = source.at[:, :, pl.ds(pl.multiple_of(part * width, 128), width)]
            result.append(pltpu.make_async_copy(view, target, sems.at[row, i]))
        return result

    far, near = copies(1 - mine, held, 0), copies(mine, kept, 1)
    far.append(pltpu.make_async_copy(lengths, sized, sems.at[0, 5]))
    for copy in far + near:
        copy.start()
    for i in (0, 1, 2, 5, 3):
        far[i].wait()
    rows = held[3].shape[0]
    row = lax.broadcasted_iota(jnp.int32, (8, HD), 0)
    limits = jnp.zeros((8, HD), jnp.int32)
    for b in range(rows):
        limits = jnp.where(row == b, sized[b], limits)
    kept[5][...] = limits
    attention(cols, limits, *held, outs, packed, far[4].wait)
    for copy in near:
        copy.wait()


def attention_near_kernel(cols, *refs):
    attention(cols, refs[5][...], *refs[:5], refs[6:-1], refs[-1])


def attention(
    cols, limits, query, new_keys, new_values, keys, values, outs, packed, values_there=lambda: None
):
    half = cols // 2
    heads = KV_HEADS // 2
    column = lax.axis_index("col")
    rows, span, _ = keys.shape
    hb = HEADS // cols
    inv_root = 1.0 / math.sqrt(HD)
    n = TOKENS * GROUP
    pairs = [(b, g) for b in range(rows) for g in range(heads)]
    q32 = query[...].astype(jnp.float32)
    nk, nv = new_keys[...].astype(jnp.float32), new_values[...].astype(jnp.float32)
    zeros = jnp.zeros((8 - TOKENS, HD), jnp.float32)

    def fresh(block, b, g):
        lanes = slice(g * HD, (g + 1) * HD)
        return jnp.concatenate([block[t, b : b + 1, lanes] for t in range(TOKENS)] + [zeros], axis=0)

    scores, fresh_scores = [], []
    for b, g in pairs:
        q = jnp.concatenate(
            [
                q32[t, b : b + 1, (g * GROUP + h) * HD : (g * GROUP + h + 1) * HD]
                for t in range(TOKENS)
                for h in range(GROUP)
            ],
            axis=0,
        ).astype(jnp.bfloat16)
        s = dot_t(q, keys[b, :, g * HD : (g + 1) * HD]) * inv_root
        position = column * span + lax.broadcasted_iota(jnp.int32, (n, span), 1)
        scores.append(jnp.where(position < limits[b : b + 1, :1], s, very_low))
        f = dot_t(q, fresh(nk, b, g).astype(jnp.bfloat16)) * inv_root
        token = lax.broadcasted_iota(jnp.int32, (n, 8), 0) // GROUP
        slot = lax.broadcasted_iota(jnp.int32, (n, 8), 1)
        seen = jnp.logical_and(slot <= token, column == 0)
        fresh_scores.append(jnp.where(seen, f, very_low))
    scores = jnp.concatenate(scores, axis=0)
    fresh_scores = jnp.concatenate(fresh_scores, axis=0)
    peak = jnp.maximum(
        jnp.max(scores, axis=1, keepdims=True), jnp.max(fresh_scores, axis=1, keepdims=True)
    )
    weights = jnp.where(scores > 0.5 * very_low, jnp.exp(scores - peak), 0.0)
    fresh_weights = jnp.where(fresh_scores > 0.5 * very_low, jnp.exp(fresh_scores - peak), 0.0)
    total = jnp.sum(weights, axis=1, keepdims=True) + jnp.sum(fresh_weights, axis=1, keepdims=True)

    def halves(w):
        high = w.astype(jnp.bfloat16)
        low = (w - high.astype(jnp.float32)).astype(jnp.bfloat16)
        return jnp.concatenate([high, low], axis=0)

    lane = lax.broadcasted_iota(jnp.int32, (GROUP, HD), 1)
    stats = [jnp.zeros((GROUP, HD), jnp.float32) for _ in range(heads)]
    values_there()
    for i, (b, g) in enumerate(pairs):
        here = slice(i * n, (i + 1) * n)
        s = dot(halves(weights[here]), values[b, :, g * HD : (g + 1) * HD])
        s = s + dot(halves(fresh_weights[here]), fresh(nv, b, g).astype(jnp.bfloat16))
        s = s[:n] + s[n:]
        for t in range(TOKENS):
            tb = t * rows + b
            part = slice(i * n + t * GROUP, i * n + (t + 1) * GROUP)
            stats[g] = jnp.where(lane == 2 * tb, peak[part], stats[g])
            stats[g] = jnp.where(lane == 2 * tb + 1, total[part], stats[g])
            block = s[t * GROUP : (t + 1) * GROUP]
            if hb >= GROUP:
                at = g * GROUP
                packed[at // hb, tb, at % hb : at % hb + GROUP] = block
            else:
                for j in range(GROUP // hb):
                    packed[g * (GROUP // hb) + j, tb] = block[j * hb : (j + 1) * hb]
    for g in range(heads):
        if hb >= GROUP:
            at = g * GROUP
            packed[at // hb, TOKENS * rows, at % hb : at % hb + GROUP] = stats[g]
        else:
            for j in range(GROUP // hb):
                packed[g * (GROUP // hb) + j, TOKENS * rows] = stats[g][j * hb : (j + 1) * hb]
    for k in range(half):
        outs[k][...] = packed[jnp.bitwise_xor(column % half, k)]


def combine_kernel(cols, *refs):
    parts, out = refs[:cols], refs[cols]
    cells = parts[0].shape[0] - 1
    hb = parts[0].shape[1]
    stats = [p[cells] for p in parts]
    attended = []
    for tb in range(cells):
        peaks = [s[:, 2 * tb : 2 * tb + 1] for s in stats]
        totals = [s[:, 2 * tb + 1 : 2 * tb + 2] for s in stats]
        top = functools.reduce(jnp.maximum, peaks)
        scales = [jnp.exp(p - top) for p in peaks]
        total = tree_sum([t * s for t, s in zip(totals, scales)])
        summed = tree_sum([p[tb] * s for p, s in zip(parts, scales)])
        attended.append(summed / total)
    rows = [
        jnp.concatenate([attended[tb][h : h + 1] for tb in range(cells)], axis=0) for h in range(hb)
    ]
    out[...] = jnp.concatenate(rows, axis=1).astype(out.dtype)


def group_order(value, groups):
    here = value.shape[1] // groups
    return jnp.concatenate(
        [value[t, r * here : (r + 1) * here] for r in range(groups) for t in range(TOKENS)], axis=0
    )


def canonical(parts, canon, me):
    cells = parts[0].shape[0]
    for k, part in enumerate(parts):
        canon[jnp.bitwise_xor(me, k), :cells] = part[...].astype(jnp.float32)
    rows = [canon[r, :cells] for r in range(len(parts))]
    return jnp.concatenate(rows, axis=0).astype(jnp.bfloat16)


def over_columns(width, body):
    size = width // 2 if width % 256 == 0 else width

    def step(j, carry):
        body(pl.multiple_of(j * size, 128), size)
        return carry

    lax.fori_loop(0, width // size, step, 0)


def gather_order(groups):
    return [0, 1, 3, 2] if groups == 4 else list(range(groups))


def out_kernel(groups, *refs):
    weight, out, canon, attended = refs[groups:]
    parts = [refs[gather_order(groups).index(k)] for k in range(groups)]
    attended[...] = canonical(parts, canon, lax.axis_index("row"))

    def body(at, size):
        out[:, pl.ds(at, size)] = dot(attended[...], weight[:, pl.ds(at, size)]).astype(out.dtype)

    over_columns(out.shape[1], body)


def in_pieces(squares):
    first = squares.astype(WIRE).astype(jnp.float32)
    second = (squares - first).astype(WIRE).astype(jnp.float32)
    third = squares - first - second
    lane = lax.broadcasted_iota(jnp.int32, (squares.shape[0], HD), 1)
    return jnp.where(
        lane == 0, first, jnp.where(lane == 1, second, jnp.where(lane == 2, third, 0.0))
    )


def lift_kernel(groups, split, residual, gains, gate_weight, up_weight, *refs):
    mid_out, keep, send, lifted, packed = refs[-5:]
    parts = [refs[gather_order(len(refs) - 5).index(k)] for k in range(len(refs) - 5)]
    hidden = gate_weight.shape[1] // split
    start = lax.axis_index("side") * hidden if split > 1 else 0
    half = packed.shape[1] // 2
    mid = tree_sum([p[...].astype(jnp.float32) for p in parts])
    mid = group_order(residual[...].astype(jnp.float32), groups) + mid
    mid_out[...] = mid
    sent = in_pieces(jnp.sum(mid * mid, axis=1, keepdims=True))
    lifted[...] = (mid * gains[...].astype(jnp.float32).reshape(1, mid.shape[1])).astype(jnp.bfloat16)
    for i in range(2):
        piece = sent[i * half : (i + 1) * half]
        packed[i, :, hidden:] = jnp.concatenate([piece, piece], axis=0)

    def body(at, size):
        block = pl.ds(pl.multiple_of(start + at, 128), size)
        gate = dot(lifted[...], gate_weight[:, block])
        up = dot(lifted[...], up_weight[:, block])
        for i in range(2):
            rows = slice(i * half, (i + 1) * half)
            packed[i, :, pl.ds(at, size)] = jnp.concatenate([gate[rows], up[rows]], axis=0)

    over_columns(hidden, body)
    bit = lax.axis_index("row") & 1
    keep[...] = packed[bit].astype(keep.dtype)
    send[...] = packed[1 - bit].astype(send.dtype)


def act_kernel(model, *refs):
    parts, out = refs[:-1], refs[-1]
    hidden = parts[0].shape[1] - HD
    cells = parts[0].shape[0] // 2
    values = [p[...].astype(jnp.float32) for p in parts]
    total = tree_sum(values[0::2]) + tree_sum(values[1::2])
    squares = jnp.sum(total[:cells, hidden:], axis=1, keepdims=True)
    inv = lax.rsqrt(squares / model + 1e-05)
    gate = total[:cells, :hidden] * inv
    up = total[cells:, :hidden] * inv
    out[...] = (gate / (1.0 + jnp.exp(-gate)) * up).astype(out.dtype)


def gather_kernel(own, received, out, packed):
    bit = lax.axis_index("row") & 1
    packed[bit] = own[...].astype(jnp.float32)
    packed[1 - bit] = received[...].astype(jnp.float32)
    out[...] = jnp.concatenate([packed[0], packed[1]], axis=0).astype(out.dtype)


def down_kernel(other, act, weight, *refs):
    out = refs[-1]
    hidden = act.shape[1]
    start = 0
    if weight.shape[0] > hidden:
        start = pl.multiple_of(jnp.bitwise_xor(lax.axis_index("side"), other) * hidden, 128)

    def body(at, size):
        product = dot(act[...], weight[pl.ds(start, hidden), pl.ds(at, size)])
        if len(refs) > 1:
            product = product + refs[0][:, pl.ds(at, size)]
        out[:, pl.ds(at, size)] = product.astype(out.dtype)

    over_columns(out.shape[1], body)


def final_kernel(groups, mid, *refs):
    parts, out = refs[:-1], refs[-1]
    total = mid[...] + tree_sum([p[...].astype(jnp.float32) for p in parts])
    here = out.shape[1] // groups
    for t in range(TOKENS):
        block = [
            total[(r * TOKENS + t) * here : (r * TOKENS + t + 1) * here] for r in range(groups)
        ]
        out[t] = jnp.concatenate(block, axis=0).astype(out.dtype)


def shards(
    query,
    new_keys,
    new_values,
    key_cache,
    value_cache,
    lengths,
    residual,
    out_weight,
    norm_gain,
    gate_weight,
    up_weight,
    down_weight,
):
    sides, groups, cols = (lax.axis_size(a) for a in ("side", "row", "col"))
    rows_here = key_cache.shape[0]
    total_rows = residual.shape[1]
    width_share = residual.shape[2]
    hidden_share = gate_weight.shape[1]
    features = out_weight.shape[0]
    model = width_share * groups
    m = TOKENS * total_rows
    cells = TOKENS * rows_here
    hb = HEADS // cols
    split = 2 if sides == 2 and (hidden_share // 2) % 128 == 0 else 1
    hidden = hidden_share // split
    f32, bf16 = jnp.float32, jnp.bfloat16
    shape = jax.ShapeDtypeStruct
    pad = -(-cells // 8) * 8

    sources = [query, new_keys, new_values, key_cache, value_cache]
    message = shape((cells + 1, hb, HD), f32)
    sources = [query, new_keys, new_values, key_cache, value_cache]

    inputs = [pltpu.VMEM((*a.shape[:2], a.shape[2] // 2), a.dtype) for a in sources]
    packed = pltpu.VMEM((cols // 2, *message.shape), f32)
    result = call(
        functools.partial(attention_far_kernel, cols),
        [message] * (cols // 2) + inputs + [pltpu.VMEM((8, HD), jnp.int32)],
        [ANY_SPEC] * 6,
        inputs
        + [pltpu.SMEM(lengths.shape, lengths.dtype), packed, pltpu.SemaphoreType.DMA((2, 6))],
        limit=8,
        name="attention_far",
    )(*[in_hbm(a) for a in [*sources, lengths]])
    far, inputs = result[: cols // 2], result[cols // 2 :]
    far = [partner(far[k], "col", cols // 2 + k) for k in range(cols // 2)]
    near = call(
        functools.partial(attention_near_kernel, cols),
        [message] * (cols // 2),
        [VMEM_SPEC] * 6,
        [packed],
        name="attention_near",
    )(*[in_vmem(a) for a in inputs])
    parts = far + [near[0]] + [partner(near[k], "col", k) for k in range(1, cols // 2)]
    attended = call(
        functools.partial(combine_kernel, cols),
        shape((cells, features), bf16),
        [VMEM_SPEC] * cols,
        flops=40 * 10**9,
        name="combine",
    )(*parts)
    gathered = spread(attended, "row")
    partial = call(
        functools.partial(out_kernel, groups),
        shape((m, width_share), WIRE),
        [VMEM_SPEC] * (groups + 1),
        [pltpu.VMEM((groups, pad, features), f32), pltpu.VMEM((m, features), bf16)],
        name="out_projection",
    )(*[gathered[k] for k in gather_order(groups)], in_vmem(out_weight))
    partials = spread(partial, "col")
    mid, keep, send = call(
        functools.partial(lift_kernel, groups, split),
        [shape((m, width_share), f32)] + [shape((m, hidden + HD), WIRE)] * 2,
        [VMEM_SPEC] * (cols + 4),
        [pltpu.VMEM((m, width_share), bf16), pltpu.VMEM((2, m, hidden + HD), f32)],
        name="gate_up",
    )(
        in_vmem(residual), in_vmem(norm_gain), in_vmem(gate_weight), in_vmem(up_weight),
        *[partials[k] for k in gather_order(cols)],
    )
    sums = [keep] + [partner((keep, send)[k % 2], "row", k) for k in range(1, groups)]
    act = call(
        functools.partial(act_kernel, model),
        shape((m // 2, hidden), bf16),
        [VMEM_SPEC] * groups,
        name="activation",
    )(*sums)
    down_weight = in_vmem(down_weight)

    def down_part(same, from_row, other, before, result):
        rows = call(
            gather_kernel,
            shape((m, hidden), bf16),
            [VMEM_SPEC] * 2,
            [pltpu.VMEM((2, m // 2, hidden), f32)],
            name="gather_act",
        )(same, from_row)
        return call(
            functools.partial(down_kernel, other),
            shape((m, width_share), result),
            [VMEM_SPEC] * (2 + len(before)),
            name="down",
        )(rows, down_weight, *before)

    near = partner(act, "row", 1)
    if split > 1:
        first = down_part(act, near, 0, [], f32)
        far = partner(act, ("side", "row"), groups + 1)
        down = down_part(partner(act, "side", 1), far, 1, [first], WIRE)
    else:
        down = down_part(act, near, 0, [], WIRE)
    return call(
        functools.partial(final_kernel, groups),
        shape((TOKENS, total_rows, width_share), bf16),
        [VMEM_SPEC] * (cols + 1),
        name="final",
    )(mid, *spread(down, "col"))


def solution(mesh):
    in_specs = (
        P(None, "row", None),
        P(None, "row", None),
        P(None, "row", None),
        P("row", "col", None),
        P("row", "col", None),
        P("row"),
        P(None, None, "row"),
        P("col", "row"),
        P("row"),
        P("row", "col"),
        P("row", "col"),
        P("col", "row"),
    )
    out_specs = P(None, None, "row")
    return jax.shard_map(shards, mesh=mesh, in_specs=in_specs, out_specs=out_specs, check_vma=False)
```

```python
import functools
import math

import jax
import jax.numpy as jnp
from jax import lax
from jax.experimental import pallas as pl
from jax.experimental.pallas import tpu as pltpu
from jax.sharding import PartitionSpec as P

HEADS = 32
KV_HEADS = 4
HD = 128
GROUP = HEADS // KV_HEADS
TOKENS = 2
very_low = -1e30
MIB = 1024 * 1024
WIRE = jnp.bfloat16
VMEM_SPEC = pl.BlockSpec(memory_space=pltpu.VMEM)
ANY_SPEC = pl.BlockSpec(memory_space=pl.ANY)


def partner(value, axis, k):
    return lax.ppermute(value, axis, [(i, i ^ k) for i in range(lax.axis_size(axis))])


def spread(piece, axis):
    return [piece] + [partner(piece, axis, k) for k in range(1, lax.axis_size(axis))]


def tree_sum(values):
    while len(values) > 1:
        values = [values[i] + values[i + 1] for i in range(0, len(values), 2)]
    return values[0]


def dot(a, b):
    return jnp.dot(a, b, preferred_element_type=jnp.float32)


def dot_t(a, b):
    return lax.dot_general(a, b, (((1,), (1,)), ((), ())), preferred_element_type=jnp.float32)


def call(kernel, out_shape, in_specs, scratch=(), limit=4, name=None, flops=None):
    cost = None
    if flops is not None:
        cost = pl.CostEstimate(flops=flops, bytes_accessed=1024, transcendentals=0)
    return pl.pallas_call(
        kernel,
        out_shape=out_shape,
        in_specs=in_specs,
        out_specs=jax.tree.map(lambda _: VMEM_SPEC, out_shape),
        scratch_shapes=list(scratch),
        compiler_params=pltpu.CompilerParams(vmem_limit_bytes=limit * MIB),
        cost_estimate=cost,
        name=name,
    )


def in_hbm(value):
    return pltpu.with_memory_space_constraint(value, pltpu.HBM)


def in_vmem(value):
    return pltpu.with_memory_space_constraint(value, pltpu.VMEM)


def attention_far_kernel(cols, *refs):
    half = cols // 2
    sources, (lengths, *outs), kept = refs[:5], refs[5 : 6 + half], refs[6 + half : 12 + half]
    held, (sized, packed, sems) = refs[12 + half : 17 + half], refs[17 + half :]
    mine = lax.axis_index("col") // half

    def copies(part, targets, row):
        result = []
        for i, (source, target) in enumerate(zip(sources, targets)):
            width = target.shape[2]
            view = source.at[:, :, pl.ds(pl.multiple_of(part * width, 128), width)]
            result.append(pltpu.make_async_copy(view, target, sems.at[row, i]))
        return result

    far, near = copies(1 - mine, held, 0), copies(mine, kept, 1)
    far.append(pltpu.make_async_copy(lengths, sized, sems.at[0, 5]))
    for copy in far + near:
        copy.start()
    for i in (0, 1, 2, 5, 3):
        far[i].wait()
    rows = held[3].shape[0]
    row = lax.broadcasted_iota(jnp.int32, (8, HD), 0)
    limits = jnp.zeros((8, HD), jnp.int32)
    for b in range(rows):
        limits = jnp.where(row == b, sized[b], limits)
    kept[5][...] = limits
    attention(cols, limits, *held, outs, packed, far[4].wait)
    for copy in near:
        copy.wait()


def attention_near_kernel(cols, *refs):
    attention(cols, refs[5][...], *refs[:5], refs[6:-1], refs[-1])


def attention(
    cols, limits, query, new_keys, new_values, keys, values, outs, packed, values_there=lambda: None
):
    half = cols // 2
    heads = KV_HEADS // 2
    column = lax.axis_index("col")
    rows, span, _ = keys.shape
    hb = HEADS // cols
    inv_root = 1.0 / math.sqrt(HD)
    n = TOKENS * GROUP
    pairs = [(b, g) for b in range(rows) for g in range(heads)]
    q32 = query[...].astype(jnp.float32)
    nk, nv = new_keys[...].astype(jnp.float32), new_values[...].astype(jnp.float32)
    zeros = jnp.zeros((8 - TOKENS, HD), jnp.float32)

    def fresh(block, b, g):
        lanes = slice(g * HD, (g + 1) * HD)
        return jnp.concatenate([block[t, b : b + 1, lanes] for t in range(TOKENS)] + [zeros], axis=0)

    scores, fresh_scores = [], []
    for b, g in pairs:
        q = jnp.concatenate(
            [
                q32[t, b : b + 1, (g * GROUP + h) * HD : (g * GROUP + h + 1) * HD]
                for t in range(TOKENS)
                for h in range(GROUP)
            ],
            axis=0,
        ).astype(jnp.bfloat16)
        s = dot_t(q, keys[b, :, g * HD : (g + 1) * HD]) * inv_root
        position = column * span + lax.broadcasted_iota(jnp.int32, (n, span), 1)
        scores.append(jnp.where(position < limits[b : b + 1, :1], s, very_low))
        f = dot_t(q, fresh(nk, b, g).astype(jnp.bfloat16)) * inv_root
        token = lax.broadcasted_iota(jnp.int32, (n, 8), 0) // GROUP
        slot = lax.broadcasted_iota(jnp.int32, (n, 8), 1)
        seen = jnp.logical_and(slot <= token, column == 0)
        fresh_scores.append(jnp.where(seen, f, very_low))
    scores = jnp.concatenate(scores, axis=0)
    fresh_scores = jnp.concatenate(fresh_scores, axis=0)
    peak = jnp.maximum(
        jnp.max(scores, axis=1, keepdims=True), jnp.max(fresh_scores, axis=1, keepdims=True)
    )
    weights = jnp.where(scores > 0.5 * very_low, jnp.exp(scores - peak), 0.0)
    fresh_weights = jnp.where(fresh_scores > 0.5 * very_low, jnp.exp(fresh_scores - peak), 0.0)
    total = jnp.sum(weights, axis=1, keepdims=True) + jnp.sum(fresh_weights, axis=1, keepdims=True)

    def halves(w):
        high = w.astype(jnp.bfloat16)
        low = (w - high.astype(jnp.float32)).astype(jnp.bfloat16)
        return jnp.concatenate([high, low], axis=0)

    lane = lax.broadcasted_iota(jnp.int32, (GROUP, HD), 1)
    stats = [jnp.zeros((GROUP, HD), jnp.float32) for _ in range(heads)]
    values_there()
    for i, (b, g) in enumerate(pairs):
        here = slice(i * n, (i + 1) * n)
        s = dot(halves(weights[here]), values[b, :, g * HD : (g + 1) * HD])
        s = s + dot(halves(fresh_weights[here]), fresh(nv, b, g).astype(jnp.bfloat16))
        s = s[:n] + s[n:]
        for t in range(TOKENS):
            tb = t * rows + b
            part = slice(i * n + t * GROUP, i * n + (t + 1) * GROUP)
            stats[g] = jnp.where(lane == 2 * tb, peak[part], stats[g])
            stats[g] = jnp.where(lane == 2 * tb + 1, total[part], stats[g])
            block = s[t * GROUP : (t + 1) * GROUP]
            if hb >= GROUP:
                at = g * GROUP
                packed[at // hb, tb, at % hb : at % hb + GROUP] = block
            else:
                for j in range(GROUP // hb):
                    packed[g * (GROUP // hb) + j, tb] = block[j * hb : (j + 1) * hb]
    for g in range(heads):
        if hb >= GROUP:
            at = g * GROUP
            packed[at // hb, TOKENS * rows, at % hb : at % hb + GROUP] = stats[g]
        else:
            for j in range(GROUP // hb):
                packed[g * (GROUP // hb) + j, TOKENS * rows] = stats[g][j * hb : (j + 1) * hb]
    for k in range(half):
        outs[k][...] = packed[jnp.bitwise_xor(column % half, k)]


def combine_kernel(cols, *refs):
    parts, out = refs[:cols], refs[cols]
    cells = parts[0].shape[0] - 1
    hb = parts[0].shape[1]
    stats = [p[cells] for p in parts]
    attended = []
    for tb in range(cells):
        peaks = [s[:, 2 * tb : 2 * tb + 1] for s in stats]
        totals = [s[:, 2 * tb + 1 : 2 * tb + 2] for s in stats]
        top = functools.reduce(jnp.maximum, peaks)
        scales = [jnp.exp(p - top) for p in peaks]
        total = tree_sum([t * s for t, s in zip(totals, scales)])
        summed = tree_sum([p[tb] * s for p, s in zip(parts, scales)])
        attended.append(summed / total)
    rows = [
        jnp.concatenate([attended[tb][h : h + 1] for tb in range(cells)], axis=0) for h in range(hb)
    ]
    out[...] = jnp.concatenate(rows, axis=1).astype(out.dtype)


def group_order(value, groups):
    here = value.shape[1] // groups
    return jnp.concatenate(
        [value[t, r * here : (r + 1) * here] for r in range(groups) for t in range(TOKENS)], axis=0
    )


def canonical(parts, canon, me):
    cells = parts[0].shape[0]
    for k, part in enumerate(parts):
        canon[jnp.bitwise_xor(me, k), :cells] = part[...].astype(jnp.float32)
    rows = [canon[r, :cells] for r in range(len(parts))]
    return jnp.concatenate(rows, axis=0).astype(jnp.bfloat16)


def over_columns(width, body):
    size = width // 2 if width % 256 == 0 else width

    def step(j, carry):
        body(pl.multiple_of(j * size, 128), size)
        return carry

    lax.fori_loop(0, width // size, step, 0)


def gather_order(groups):
    return [0, 1, 3, 2] if groups == 4 else list(range(groups))


def sum_order(groups):
    return [0, 3, 1, 2] if groups == 4 else list(range(groups))


def out_kernel(groups, *refs):
    weight, out, canon, attended = refs[groups:]
    parts = [refs[gather_order(groups).index(k)] for k in range(groups)]
    attended[...] = canonical(parts, canon, lax.axis_index("row"))

    def body(at, size):
        out[:, pl.ds(at, size)] = dot(attended[...], weight[:, pl.ds(at, size)]).astype(out.dtype)

    over_columns(out.shape[1], body)


def in_pieces(squares):
    first = squares.astype(WIRE).astype(jnp.float32)
    second = (squares - first).astype(WIRE).astype(jnp.float32)
    third = squares - first - second
    lane = lax.broadcasted_iota(jnp.int32, (squares.shape[0], HD), 1)
    return jnp.where(
        lane == 0, first, jnp.where(lane == 1, second, jnp.where(lane == 2, third, 0.0))
    )


def lift_kernel(groups, cols, split, residual, gains, gate_weight, up_weight, *refs):
    parts, mid_out, (lifted, packed) = refs[:cols], refs[cols], refs[-2:]
    outs = refs[cols + 1 : -2]
    hidden = gate_weight.shape[1] // split
    start = lax.axis_index("side") * hidden if split > 1 else 0
    half = packed.shape[1] // 2
    mid = tree_sum([p[...].astype(jnp.float32) for p in parts])
    mid = group_order(residual[...].astype(jnp.float32), groups) + mid
    mid_out[...] = mid
    sent = in_pieces(jnp.sum(mid * mid, axis=1, keepdims=True))
    lifted[...] = (mid * gains[...].astype(jnp.float32).reshape(1, mid.shape[1])).astype(jnp.bfloat16)
    for i in range(2):
        piece = sent[i * half : (i + 1) * half]
        packed[i, :, hidden:] = jnp.concatenate([piece, piece], axis=0)

    def body(at, size):
        block = pl.ds(pl.multiple_of(start + at, 128), size)
        gate = dot(lifted[...], gate_weight[:, block])
        up = dot(lifted[...], up_weight[:, block])
        for i in range(2):
            rows = slice(i * half, (i + 1) * half)
            packed[i, :, pl.ds(at, size)] = jnp.concatenate([gate[rows], up[rows]], axis=0)

    over_columns(hidden, body)
    bit = lax.axis_index("row") & 1
    mine, theirs = (packed[i].astype(outs[0].dtype) for i in (bit, 1 - bit))
    for k, out in enumerate(outs):
        out[...] = theirs if k % 2 else mine


def act_kernel(model, *refs):
    out = refs[-1]
    parts = [refs[sum_order(len(refs) - 1).index(k)] for k in range(len(refs) - 1)]
    hidden = parts[0].shape[1] - HD
    cells = parts[0].shape[0] // 2
    values = [p[...].astype(jnp.float32) for p in parts]
    total = tree_sum(values[0::2]) + tree_sum(values[1::2])
    squares = jnp.sum(total[:cells, hidden:], axis=1, keepdims=True)
    inv = lax.rsqrt(squares / model + 1e-05)
    gate = total[:cells, :hidden] * inv
    up = total[cells:, :hidden] * inv
    out[...] = (gate / (1.0 + jnp.exp(-gate)) * up).astype(out.dtype)


def gather_kernel(own, received, out, packed):
    bit = lax.axis_index("row") & 1
    packed[bit] = own[...].astype(jnp.float32)
    packed[1 - bit] = received[...].astype(jnp.float32)
    out[...] = jnp.concatenate([packed[0], packed[1]], axis=0).astype(out.dtype)


def down_kernel(other, act, weight, *refs):
    out = refs[-1]
    hidden = act.shape[1]
    start = 0
    if weight.shape[0] > hidden:
        start = pl.multiple_of(jnp.bitwise_xor(lax.axis_index("side"), other) * hidden, 128)

    def body(at, size):
        product = dot(act[...], weight[pl.ds(start, hidden), pl.ds(at, size)])
        if len(refs) > 1:
            product = product + refs[0][:, pl.ds(at, size)]
        out[:, pl.ds(at, size)] = product.astype(out.dtype)

    over_columns(out.shape[1], body)


def final_kernel(groups, mid, *refs):
    parts, out = refs[:-1], refs[-1]
    total = mid[...] + tree_sum([p[...].astype(jnp.float32) for p in parts])
    here = out.shape[1] // groups
    for t in range(TOKENS):
        block = [
            total[(r * TOKENS + t) * here : (r * TOKENS + t + 1) * here] for r in range(groups)
        ]
        out[t] = jnp.concatenate(block, axis=0).astype(out.dtype)


def shards(
    query,
    new_keys,
    new_values,
    key_cache,
    value_cache,
    lengths,
    residual,
    out_weight,
    norm_gain,
    gate_weight,
    up_weight,
    down_weight,
):
    sides, groups, cols = (lax.axis_size(a) for a in ("side", "row", "col"))
    rows_here = key_cache.shape[0]
    total_rows = residual.shape[1]
    width_share = residual.shape[2]
    hidden_share = gate_weight.shape[1]
    features = out_weight.shape[0]
    model = width_share * groups
    m = TOKENS * total_rows
    cells = TOKENS * rows_here
    hb = HEADS // cols
    split = 2 if sides == 2 and (hidden_share // 2) % 128 == 0 else 1
    hidden = hidden_share // split
    f32, bf16 = jnp.float32, jnp.bfloat16
    shape = jax.ShapeDtypeStruct
    pad = -(-cells // 8) * 8

    sources = [query, new_keys, new_values, key_cache, value_cache]
    message = shape((cells + 1, hb, HD), f32)
    sources = [query, new_keys, new_values, key_cache, value_cache]

    inputs = [pltpu.VMEM((*a.shape[:2], a.shape[2] // 2), a.dtype) for a in sources]
    packed = pltpu.VMEM((cols // 2, *message.shape), f32)
    result = call(
        functools.partial(attention_far_kernel, cols),
        [message] * (cols // 2) + inputs + [pltpu.VMEM((8, HD), jnp.int32)],
        [ANY_SPEC] * 6,
        inputs
        + [pltpu.SMEM(lengths.shape, lengths.dtype), packed, pltpu.SemaphoreType.DMA((2, 6))],
        limit=8,
        name="attention_far",
    )(*[in_hbm(a) for a in [*sources, lengths]])
    far, inputs = result[: cols // 2], result[cols // 2 :]
    far = [partner(far[k], "col", cols // 2 + k) for k in range(cols // 2)]
    near = call(
        functools.partial(attention_near_kernel, cols),
        [message] * (cols // 2),
        [VMEM_SPEC] * 6,
        [packed],
        name="attention_near",
    )(*[in_vmem(a) for a in inputs])
    parts = far + [near[0]] + [partner(near[k], "col", k) for k in range(1, cols // 2)]
    attended = call(
        functools.partial(combine_kernel, cols),
        shape((cells, features), bf16),
        [VMEM_SPEC] * cols,
        flops=40 * 10**9,
        name="combine",
    )(*parts)
    gathered = spread(attended, "row")
    partial = call(
        functools.partial(out_kernel, groups),
        shape((m, width_share), WIRE),
        [VMEM_SPEC] * (groups + 1),
        [pltpu.VMEM((groups, pad, features), f32), pltpu.VMEM((m, features), bf16)],
        name="out_projection",
    )(*[gathered[k] for k in gather_order(groups)], in_vmem(out_weight))
    partials = spread(partial, "col")
    mid, *sums = call(
        functools.partial(lift_kernel, groups, cols, split),
        [shape((m, width_share), f32)] + [shape((m, hidden + HD), WIRE)] * groups,
        [VMEM_SPEC] * (cols + 4),
        [pltpu.VMEM((m, width_share), bf16), pltpu.VMEM((2, m, hidden + HD), f32)],
        name="gate_up",
    )(
        in_vmem(residual), in_vmem(norm_gain), in_vmem(gate_weight), in_vmem(up_weight),
        *partials,
    )
    sums = sums[:1] + [partner(sums[k], "row", k) for k in range(1, groups)]
    act = call(
        functools.partial(act_kernel, model),
        shape((m // 2, hidden), bf16),
        [VMEM_SPEC] * groups,
        name="activation",
    )(*[sums[k] for k in sum_order(groups)])
    down_weight = in_vmem(down_weight)

    def down_part(same, from_row, other, before, result):
        rows = call(
            gather_kernel,
            shape((m, hidden), bf16),
            [VMEM_SPEC] * 2,
            [pltpu.VMEM((2, m // 2, hidden), f32)],
            name="gather_act",
        )(same, from_row)
        return call(
            functools.partial(down_kernel, other),
            shape((m, width_share), result),
            [VMEM_SPEC] * (2 + len(before)),
            name="down",
        )(rows, down_weight, *before)

    near = partner(act, "row", 1)
    if split > 1:
        first = down_part(act, near, 0, [], f32)
        far = partner(act, ("side", "row"), groups + 1)
        down = down_part(partner(act, "side", 1), far, 1, [first], WIRE)
    else:
        down = down_part(act, near, 0, [], WIRE)
    return call(
        functools.partial(final_kernel, groups),
        shape((TOKENS, total_rows, width_share), bf16),
        [VMEM_SPEC] * (cols + 1),
        name="final",
    )(mid, *spread(down, "col"))


def solution(mesh):
    in_specs = (
        P(None, "row", None),
        P(None, "row", None),
        P(None, "row", None),
        P("row", "col", None),
        P("row", "col", None),
        P("row"),
        P(None, None, "row"),
        P("col", "row"),
        P("row"),
        P("row", "col"),
        P("row", "col"),
        P("col", "row"),
    )
    out_specs = P(None, None, "row")
    return jax.shard_map(shards, mesh=mesh, in_specs=in_specs, out_specs=out_specs, check_vma=False)
```

```python
import functools
import math

import jax
import jax.numpy as jnp
from jax import lax
from jax.experimental import pallas as pl
from jax.experimental.pallas import tpu as pltpu
from jax.sharding import PartitionSpec as P

HEADS = 32
KV_HEADS = 4
HD = 128
GROUP = HEADS // KV_HEADS
TOKENS = 2
very_low = -1e30
MIB = 1024 * 1024
WIRE = jnp.bfloat16
VMEM_SPEC = pl.BlockSpec(memory_space=pltpu.VMEM)
ANY_SPEC = pl.BlockSpec(memory_space=pl.ANY)


def partner(value, axis, k):
    return lax.ppermute(value, axis, [(i, i ^ k) for i in range(lax.axis_size(axis))])


def spread(piece, axis):
    return [piece] + [partner(piece, axis, k) for k in range(1, lax.axis_size(axis))]


def tree_sum(values):
    while len(values) > 1:
        values = [values[i] + values[i + 1] for i in range(0, len(values), 2)]
    return values[0]


def dot(a, b):
    return jnp.dot(a, b, preferred_element_type=jnp.float32)


def dot_t(a, b):
    return lax.dot_general(a, b, (((1,), (1,)), ((), ())), preferred_element_type=jnp.float32)


def call(kernel, out_shape, in_specs, scratch=(), limit=4, name=None, flops=None):
    cost = None
    if flops is not None:
        cost = pl.CostEstimate(flops=flops, bytes_accessed=1024, transcendentals=0)
    return pl.pallas_call(
        kernel,
        out_shape=out_shape,
        in_specs=in_specs,
        out_specs=jax.tree.map(lambda _: VMEM_SPEC, out_shape),
        scratch_shapes=list(scratch),
        compiler_params=pltpu.CompilerParams(vmem_limit_bytes=limit * MIB),
        cost_estimate=cost,
        name=name,
    )


def in_hbm(value):
    return pltpu.with_memory_space_constraint(value, pltpu.HBM)


def in_vmem(value):
    return pltpu.with_memory_space_constraint(value, pltpu.VMEM)


def attention_far_kernel(cols, *refs):
    half = cols // 2
    sources, (lengths, *outs), kept = refs[:5], refs[5 : 6 + half], refs[6 + half : 12 + half]
    sized, packed, sems = refs[12 + half :]
    copies = [
        pltpu.make_async_copy(source, target, sems.at[i])
        for i, (source, target) in enumerate(zip(sources, kept))
    ]
    copies.append(pltpu.make_async_copy(lengths, sized, sems.at[5]))
    for copy in copies:
        copy.start()
    for i in (0, 1, 2, 5, 3):
        copies[i].wait()
    row = lax.broadcasted_iota(jnp.int32, (8, HD), 0)
    limits = jnp.zeros((8, HD), jnp.int32)
    for b in range(kept[3].shape[0]):
        limits = jnp.where(row == b, sized[b], limits)
    kept[5][...] = limits
    attention(cols, 1, limits, *kept[:5], outs, packed, copies[4].wait)


def attention_near_kernel(cols, *refs):
    attention(cols, 0, refs[5][...], *refs[:5], refs[6:-1], refs[-1], lambda: None)


def attention(
    cols, far, limits, query, new_keys, new_values, keys, values, outs, packed, values_there
):
    half = cols // 2
    heads = KV_HEADS // 2
    column = lax.axis_index("col")
    chosen = jnp.bitwise_xor(column // half, far)

    def lanes(source):
        width = source.shape[2] // 2
        return source[:, :, pl.ds(pl.multiple_of(chosen * width, 128), width)].astype(jnp.float32)

    def head(source, b, g):
        return source[b, :, pl.ds(pl.multiple_of((chosen * heads + g) * HD, 128), HD)]

    rows, span, _ = keys.shape
    hb = HEADS // cols
    inv_root = 1.0 / math.sqrt(HD)
    n = TOKENS * GROUP
    pairs = [(b, g) for b in range(rows) for g in range(heads)]
    q32, nk, nv = lanes(query), lanes(new_keys), lanes(new_values)
    zeros = jnp.zeros((8 - TOKENS, HD), jnp.float32)

    def fresh(block, b, g):
        lanes = slice(g * HD, (g + 1) * HD)
        return jnp.concatenate([block[t, b : b + 1, lanes] for t in range(TOKENS)] + [zeros], axis=0)

    scores, fresh_scores = [], []
    for b, g in pairs:
        q = jnp.concatenate(
            [
                q32[t, b : b + 1, (g * GROUP + h) * HD : (g * GROUP + h + 1) * HD]
                for t in range(TOKENS)
                for h in range(GROUP)
            ],
            axis=0,
        ).astype(jnp.bfloat16)
        s = dot_t(q, head(keys, b, g)) * inv_root
        position = column * span + lax.broadcasted_iota(jnp.int32, (n, span), 1)
        scores.append(jnp.where(position < limits[b : b + 1, :1], s, very_low))
        f = dot_t(q, fresh(nk, b, g).astype(jnp.bfloat16)) * inv_root
        token = lax.broadcasted_iota(jnp.int32, (n, 8), 0) // GROUP
        slot = lax.broadcasted_iota(jnp.int32, (n, 8), 1)
        seen = jnp.logical_and(slot <= token, column == 0)
        fresh_scores.append(jnp.where(seen, f, very_low))
    scores = jnp.concatenate(scores, axis=0)
    fresh_scores = jnp.concatenate(fresh_scores, axis=0)
    peak = jnp.maximum(
        jnp.max(scores, axis=1, keepdims=True), jnp.max(fresh_scores, axis=1, keepdims=True)
    )
    weights = jnp.where(scores > 0.5 * very_low, jnp.exp(scores - peak), 0.0)
    fresh_weights = jnp.where(fresh_scores > 0.5 * very_low, jnp.exp(fresh_scores - peak), 0.0)
    total = jnp.sum(weights, axis=1, keepdims=True) + jnp.sum(fresh_weights, axis=1, keepdims=True)

    def halves(w):
        high = w.astype(jnp.bfloat16)
        low = (w - high.astype(jnp.float32)).astype(jnp.bfloat16)
        return jnp.concatenate([high, low], axis=0)

    lane = lax.broadcasted_iota(jnp.int32, (GROUP, HD), 1)
    stats = [jnp.zeros((GROUP, HD), jnp.float32) for _ in range(heads)]
    values_there()
    for i, (b, g) in enumerate(pairs):
        here = slice(i * n, (i + 1) * n)
        s = dot(halves(weights[here]), head(values, b, g))
        s = s + dot(halves(fresh_weights[here]), fresh(nv, b, g).astype(jnp.bfloat16))
        s = s[:n] + s[n:]
        for t in range(TOKENS):
            tb = t * rows + b
            part = slice(i * n + t * GROUP, i * n + (t + 1) * GROUP)
            stats[g] = jnp.where(lane == 2 * tb, peak[part], stats[g])
            stats[g] = jnp.where(lane == 2 * tb + 1, total[part], stats[g])
            block = s[t * GROUP : (t + 1) * GROUP]
            if hb >= GROUP:
                at = g * GROUP
                packed[at // hb, tb, at % hb : at % hb + GROUP] = block
            else:
                for j in range(GROUP // hb):
                    packed[g * (GROUP // hb) + j, tb] = block[j * hb : (j + 1) * hb]
    for g in range(heads):
        if hb >= GROUP:
            at = g * GROUP
            packed[at // hb, TOKENS * rows, at % hb : at % hb + GROUP] = stats[g]
        else:
            for j in range(GROUP // hb):
                packed[g * (GROUP // hb) + j, TOKENS * rows] = stats[g][j * hb : (j + 1) * hb]
    for k in range(half):
        outs[k][...] = packed[jnp.bitwise_xor(column % half, k)]


def combine_kernel(cols, *refs):
    parts, out = refs[:cols], refs[cols]
    cells = parts[0].shape[0] - 1
    hb = parts[0].shape[1]
    stats = [p[cells] for p in parts]
    attended = []
    for tb in range(cells):
        peaks = [s[:, 2 * tb : 2 * tb + 1] for s in stats]
        totals = [s[:, 2 * tb + 1 : 2 * tb + 2] for s in stats]
        top = functools.reduce(jnp.maximum, peaks)
        scales = [jnp.exp(p - top) for p in peaks]
        total = tree_sum([t * s for t, s in zip(totals, scales)])
        summed = tree_sum([p[tb] * s for p, s in zip(parts, scales)])
        attended.append(summed / total)
    rows = [
        jnp.concatenate([attended[tb][h : h + 1] for tb in range(cells)], axis=0) for h in range(hb)
    ]
    out[...] = jnp.concatenate(rows, axis=1).astype(out.dtype)


def group_order(value, groups):
    here = value.shape[1] // groups
    return jnp.concatenate(
        [value[t, r * here : (r + 1) * here] for r in range(groups) for t in range(TOKENS)], axis=0
    )


def canonical(parts, canon, me):
    cells = parts[0].shape[0]
    for k, part in enumerate(parts):
        canon[jnp.bitwise_xor(me, k), :cells] = part[...].astype(jnp.float32)
    rows = [canon[r, :cells] for r in range(len(parts))]
    return jnp.concatenate(rows, axis=0).astype(jnp.bfloat16)


def over_columns(width, body):
    size = width

    def step(j, carry):
        body(pl.multiple_of(j * size, 128), size)
        return carry

    lax.fori_loop(0, width // size, step, 0)


def across(count):
    return [0, *range(count - 1, 0, -1)]


def by_distance(refs):
    order = across(len(refs))
    return [refs[order.index(k)] for k in range(len(refs))]


def out_kernel(groups, *refs):
    parts, (weight, *outs) = refs[:groups], refs[groups:-3]
    canon, attended, packed = refs[-3:]
    half = packed.shape[2]
    attended[...] = canonical(parts, canon, lax.axis_index("row"))
    for i in range(2):
        packed[i] = dot(attended[...], weight[:, i * half : (i + 1) * half])
    bit = lax.axis_index("col") & 1
    for k, out in enumerate(outs):
        out[...] = packed[jnp.bitwise_xor(bit, k & 1)].astype(out.dtype)


def in_pieces(squares):
    first = squares.astype(WIRE).astype(jnp.float32)
    second = (squares - first).astype(WIRE).astype(jnp.float32)
    third = squares - first - second
    lane = lax.broadcasted_iota(jnp.int32, (squares.shape[0], HD), 1)
    return jnp.where(
        lane == 0, first, jnp.where(lane == 1, second, jnp.where(lane == 2, third, 0.0))
    )


def lanes_of(bit, half):
    return pl.ds(pl.multiple_of(bit * half, 128), half)


def mid_kernel(groups, residual, gains, *refs):
    parts, (mid, lifted) = by_distance(refs[:-2]), refs[-2:]
    half = mid.shape[1]
    here = lanes_of(lax.axis_index("col") & 1, half)
    own = residual[:, :, here].astype(jnp.float32)
    value = group_order(own, groups) + tree_sum([p[...].astype(jnp.float32) for p in parts])
    mid[...] = value
    lifted[...] = (value * gains[here].astype(jnp.float32).reshape(1, half)).astype(jnp.bfloat16)


def products(lifted, bit, gate_weight, up_weight, out_hidden):
    half = lifted.shape[1]
    start = 0
    if gate_weight.shape[1] > out_hidden:
        start = pl.multiple_of(lax.axis_index("side") * out_hidden, 128)
    rows, columns = lanes_of(bit, half), pl.ds(start, out_hidden)
    return dot(lifted, gate_weight[rows, columns]), dot(lifted, up_weight[rows, columns])


def lift_first_kernel(lifted, gate_weight, up_weight, gate, up):
    bit = lax.axis_index("col") & 1
    gate[...], up[...] = products(lifted[...], bit, gate_weight, up_weight, gate.shape[1])


def lift_second_kernel(
    own, received, gains, gate_weight, up_weight, gate_first, up_first, mid, keep, send, packed
):
    rows, hidden = gate_first.shape
    half, bit = rows // 2, lax.axis_index("col") & 1
    width = own.shape[1]
    mid[:, lanes_of(bit, width)] = own[...]
    mid[:, lanes_of(1 - bit, width)] = received[...]
    value = received[...]
    squares = own[...] * own[...] + value * value
    sent = in_pieces(jnp.sum(squares, axis=1, keepdims=True))
    gain = gains[lanes_of(1 - bit, width)].astype(jnp.float32).reshape(1, width)
    lifted = (value * gain).astype(jnp.bfloat16)
    gate, up = products(lifted, 1 - bit, gate_weight, up_weight, hidden)
    gate, up = gate + gate_first[...], up + up_first[...]
    for i in range(2):
        part = slice(i * half, (i + 1) * half)
        packed[i, :, hidden:] = jnp.concatenate([sent[part], sent[part]], axis=0)
        packed[i, :, :hidden] = jnp.concatenate([gate[part], up[part]], axis=0)
    bit = lax.axis_index("row") & 1
    keep[...] = packed[bit].astype(keep.dtype)
    send[...] = packed[1 - bit].astype(send.dtype)


def act_kernel(model, *refs):
    parts, out = refs[:-1], refs[-1]
    hidden = parts[0].shape[1] - HD
    cells = parts[0].shape[0] // 2
    values = [p[...].astype(jnp.float32) for p in parts]
    total = tree_sum(values[0::2]) + tree_sum(values[1::2])
    squares = jnp.sum(total[:cells, hidden:], axis=1, keepdims=True)
    inv = lax.rsqrt(squares / model + 1e-05)
    gate = total[:cells, :hidden] * inv
    up = total[cells:, :hidden] * inv
    out[...] = (gate / (1.0 + jnp.exp(-gate)) * up).astype(out.dtype)


def gather_kernel(own, received, out, packed):
    bit = lax.axis_index("row") & 1
    packed[bit] = own[...].astype(jnp.float32)
    packed[1 - bit] = received[...].astype(jnp.float32)
    out[...] = jnp.concatenate([packed[0], packed[1]], axis=0).astype(out.dtype)


def down_kernel(other, act, weight, *refs):
    out = refs[-1]
    hidden = act.shape[1]
    start = 0
    if weight.shape[0] > hidden:
        start = pl.multiple_of(jnp.bitwise_xor(lax.axis_index("side"), other) * hidden, 128)

    def body(at, size):
        product = dot(act[...], weight[pl.ds(start, hidden), pl.ds(at, size)])
        if len(refs) > 1:
            product = product + refs[0][:, pl.ds(at, size)]
        out[:, pl.ds(at, size)] = product.astype(out.dtype)

    over_columns(out.shape[1], body)


def final_kernel(groups, mid, *refs):
    parts, out = refs[:-1], refs[-1]
    total = mid[...] + tree_sum([p[...].astype(jnp.float32) for p in parts])
    here = out.shape[1] // groups
    for t in range(TOKENS):
        block = [
            total[(r * TOKENS + t) * here : (r * TOKENS + t + 1) * here] for r in range(groups)
        ]
        out[t] = jnp.concatenate(block, axis=0).astype(out.dtype)


def shards(
    query,
    new_keys,
    new_values,
    key_cache,
    value_cache,
    lengths,
    residual,
    out_weight,
    norm_gain,
    gate_weight,
    up_weight,
    down_weight,
):
    sides, groups, cols = (lax.axis_size(a) for a in ("side", "row", "col"))
    rows_here = key_cache.shape[0]
    total_rows = residual.shape[1]
    width_share = residual.shape[2]
    hidden_share = gate_weight.shape[1]
    features = out_weight.shape[0]
    model = width_share * groups
    m = TOKENS * total_rows
    cells = TOKENS * rows_here
    hb = HEADS // cols
    split = 2 if sides == 2 and (hidden_share // 2) % 128 == 0 else 1
    hidden = hidden_share // split
    f32, bf16 = jnp.float32, jnp.bfloat16
    shape = jax.ShapeDtypeStruct
    pad = -(-cells // 8) * 8

    sources = [query, new_keys, new_values, key_cache, value_cache]
    message = shape((cells + 1, hb, HD), f32)
    sources = [query, new_keys, new_values, key_cache, value_cache]

    inputs = [pltpu.VMEM(a.shape, a.dtype) for a in sources]
    packed = pltpu.VMEM((cols // 2, *message.shape), f32)
    result = call(
        functools.partial(attention_far_kernel, cols),
        [message] * (cols // 2) + inputs + [pltpu.VMEM((8, HD), jnp.int32)],
        [ANY_SPEC] * 6,
        [pltpu.SMEM(lengths.shape, lengths.dtype), packed, pltpu.SemaphoreType.DMA((6,))],
        name="attention_far",
    )(*[in_hbm(a) for a in [*sources, lengths]])
    far, inputs = result[: cols // 2], result[cols // 2 :]
    far = [partner(far[k], "col", cols // 2 + k) for k in range(cols // 2)]
    near = call(
        functools.partial(attention_near_kernel, cols),
        [message] * (cols // 2),
        [VMEM_SPEC] * 6,
        [packed],
        name="attention_near",
    )(*[in_vmem(a) for a in inputs])
    parts = far + [near[0]] + [partner(near[k], "col", k) for k in range(1, cols // 2)]
    attended = call(
        functools.partial(combine_kernel, cols),
        shape((cells, features), bf16),
        [VMEM_SPEC] * cols,
        flops=40 * 10**9,
        name="combine",
    )(*parts)
    gathered = spread(attended, "row")
    half = width_share // 2
    partials = call(
        functools.partial(out_kernel, groups),
        [shape((m, half), WIRE)] * cols,
        [VMEM_SPEC] * (groups + 1),
        [
            pltpu.VMEM((groups, pad, features), f32),
            pltpu.VMEM((m, features), bf16),
            pltpu.VMEM((2, m, half), f32),
        ],
        name="out_projection",
    )(*gathered, in_vmem(out_weight))
    partials = [partials[0]] + [partner(partials[k], "col", k) for k in range(1, cols)]
    norm_gain = in_vmem(norm_gain)
    own, own_lifted = call(
        functools.partial(mid_kernel, groups),
        [shape((m, half), f32), shape((m, half), bf16)],
        [VMEM_SPEC] * (cols + 2),
        name="mid",
    )(in_vmem(residual), norm_gain, *[partials[k] for k in across(cols)])
    received = partner(own, "col", 1)
    weights = [in_vmem(gate_weight), in_vmem(up_weight)]
    first = call(
        lift_first_kernel,
        [shape((m, hidden), f32)] * 2,
        [VMEM_SPEC] * 3,
        name="gate_up_first",
    )(own_lifted, *weights)
    mid, keep, send = call(
        lift_second_kernel,
        [shape((m, width_share), f32)] + [shape((m, hidden + HD), WIRE)] * 2,
        [VMEM_SPEC] * 7,
        [pltpu.VMEM((2, m, hidden + HD), f32)],
        limit=8,
        name="gate_up_second",
    )(own, received, norm_gain, *weights, *first)
    sums = [keep] + [partner((keep, send)[k % 2], "row", k) for k in range(1, groups)]
    act = call(
        functools.partial(act_kernel, model),
        shape((m // 2, hidden), bf16),
        [VMEM_SPEC] * groups,
        name="activation",
    )(*sums)
    down_weight = in_vmem(down_weight)

    def down_part(same, from_row, other, before, result):
        rows = call(
            gather_kernel,
            shape((m, hidden), bf16),
            [VMEM_SPEC] * 2,
            [pltpu.VMEM((2, m // 2, hidden), f32)],
            name="gather_act",
        )(same, from_row)
        return call(
            functools.partial(down_kernel, other),
            shape((m, width_share), result),
            [VMEM_SPEC] * (2 + len(before)),
            name="down",
        )(rows, down_weight, *before)

    near = partner(act, "row", 1)
    if split > 1:
        first = down_part(act, near, 0, [], f32)
        far = partner(act, ("side", "row"), groups + 1)
        down = down_part(partner(act, "side", 1), far, 1, [first], WIRE)
    else:
        down = down_part(act, near, 0, [], WIRE)
    return call(
        functools.partial(final_kernel, groups),
        shape((TOKENS, total_rows, width_share), bf16),
        [VMEM_SPEC] * (cols + 1),
        name="final",
    )(mid, *spread(down, "col"))


def solution(mesh):
    in_specs = (
        P(None, "row", None),
        P(None, "row", None),
        P(None, "row", None),
        P("row", "col", None),
        P("row", "col", None),
        P("row"),
        P(None, None, "row"),
        P("col", "row"),
        P("row"),
        P("row", "col"),
        P("row", "col"),
        P("col", "row"),
    )
    out_specs = P(None, None, "row")
    return jax.shard_map(shards, mesh=mesh, in_specs=in_specs, out_specs=out_specs, check_vma=False)
```

```python
import functools
import math

import jax
import jax.numpy as jnp
from jax import lax
from jax.experimental import pallas as pl
from jax.experimental.pallas import tpu as pltpu
from jax.sharding import PartitionSpec as P

HEADS = 32
KV_HEADS = 4
HD = 128
GROUP = HEADS // KV_HEADS
TOKENS = 2
very_low = -1e30
MIB = 1024 * 1024
WIRE = jnp.bfloat16
VMEM_SPEC = pl.BlockSpec(memory_space=pltpu.VMEM)
ANY_SPEC = pl.BlockSpec(memory_space=pl.ANY)


def partner(value, axis, k):
    return lax.ppermute(value, axis, [(i, i ^ k) for i in range(lax.axis_size(axis))])


def spread(piece, axis):
    return [piece] + [partner(piece, axis, k) for k in range(1, lax.axis_size(axis))]


def tree_sum(values):
    while len(values) > 1:
        values = [values[i] + values[i + 1] for i in range(0, len(values), 2)]
    return values[0]


def dot(a, b):
    return jnp.dot(a, b, preferred_element_type=jnp.float32)


def dot_t(a, b):
    return lax.dot_general(a, b, (((1,), (1,)), ((), ())), preferred_element_type=jnp.float32)


def call(kernel, out_shape, in_specs, scratch=(), limit=4, name=None, flops=None):
    cost = None
    if flops is not None:
        cost = pl.CostEstimate(flops=flops, bytes_accessed=1024, transcendentals=0)
    return pl.pallas_call(
        kernel,
        out_shape=out_shape,
        in_specs=in_specs,
        out_specs=jax.tree.map(lambda _: VMEM_SPEC, out_shape),
        scratch_shapes=list(scratch),
        compiler_params=pltpu.CompilerParams(vmem_limit_bytes=limit * MIB),
        cost_estimate=cost,
        name=name,
    )


def in_hbm(value):
    return pltpu.with_memory_space_constraint(value, pltpu.HBM)


def in_vmem(value):
    return pltpu.with_memory_space_constraint(value, pltpu.VMEM)


def attention_far_kernel(cols, *refs):
    half = cols // 2
    sources, (lengths, *outs), kept = refs[:5], refs[5 : 6 + half], refs[6 + half : 12 + half]
    sized, packed, sems = refs[12 + half :]
    copies = [
        pltpu.make_async_copy(source, target, sems.at[i])
        for i, (source, target) in enumerate(zip(sources, kept))
    ]
    copies.append(pltpu.make_async_copy(lengths, sized, sems.at[5]))
    for copy in copies:
        copy.start()
    for i in (0, 1, 2, 5, 3):
        copies[i].wait()
    row = lax.broadcasted_iota(jnp.int32, (8, HD), 0)
    limits = jnp.zeros((8, HD), jnp.int32)
    for b in range(kept[3].shape[0]):
        limits = jnp.where(row == b, sized[b], limits)
    kept[5][...] = limits
    attention(cols, 1, limits, *kept[:5], outs, packed, copies[4].wait)


def attention_near_kernel(cols, *refs):
    attention(cols, 0, refs[5][...], *refs[:5], refs[6:-1], refs[-1], lambda: None)


def attention(
    cols, far, limits, query, new_keys, new_values, keys, values, outs, packed, values_there
):
    half = cols // 2
    heads = KV_HEADS // 2
    column = lax.axis_index("col")
    chosen = jnp.bitwise_xor(column // half, far)

    def lanes(source):
        width = source.shape[2] // 2
        return source[:, :, pl.ds(pl.multiple_of(chosen * width, 128), width)].astype(jnp.float32)

    def head(source, b, g):
        return source[b, :, pl.ds(pl.multiple_of((chosen * heads + g) * HD, 128), HD)]

    rows, span, _ = keys.shape
    hb = HEADS // cols
    inv_root = 1.0 / math.sqrt(HD)
    n = TOKENS * GROUP
    pairs = [(b, g) for b in range(rows) for g in range(heads)]
    q32, nk, nv = lanes(query), lanes(new_keys), lanes(new_values)
    zeros = jnp.zeros((8 - TOKENS, HD), jnp.float32)

    def fresh(block, b, g):
        lanes = slice(g * HD, (g + 1) * HD)
        return jnp.concatenate([block[t, b : b + 1, lanes] for t in range(TOKENS)] + [zeros], axis=0)

    scores, fresh_scores = [], []
    for b, g in pairs:
        q = jnp.concatenate(
            [
                q32[t, b : b + 1, (g * GROUP + h) * HD : (g * GROUP + h + 1) * HD]
                for t in range(TOKENS)
                for h in range(GROUP)
            ],
            axis=0,
        ).astype(jnp.bfloat16)
        s = dot_t(q, head(keys, b, g)) * inv_root
        position = column * span + lax.broadcasted_iota(jnp.int32, (n, span), 1)
        scores.append(jnp.where(position < limits[b : b + 1, :1], s, very_low))
        f = dot_t(q, fresh(nk, b, g).astype(jnp.bfloat16)) * inv_root
        token = lax.broadcasted_iota(jnp.int32, (n, 8), 0) // GROUP
        slot = lax.broadcasted_iota(jnp.int32, (n, 8), 1)
        seen = jnp.logical_and(slot <= token, column == 0)
        fresh_scores.append(jnp.where(seen, f, very_low))
    scores = jnp.concatenate(scores, axis=0)
    fresh_scores = jnp.concatenate(fresh_scores, axis=0)
    peak = jnp.maximum(
        jnp.max(scores, axis=1, keepdims=True), jnp.max(fresh_scores, axis=1, keepdims=True)
    )
    weights = jnp.where(scores > 0.5 * very_low, jnp.exp(scores - peak), 0.0)
    fresh_weights = jnp.where(fresh_scores > 0.5 * very_low, jnp.exp(fresh_scores - peak), 0.0)
    total = jnp.sum(weights, axis=1, keepdims=True) + jnp.sum(fresh_weights, axis=1, keepdims=True)

    def halves(w):
        high = w.astype(jnp.bfloat16)
        low = (w - high.astype(jnp.float32)).astype(jnp.bfloat16)
        return jnp.concatenate([high, low], axis=0)

    lane = lax.broadcasted_iota(jnp.int32, (GROUP, HD), 1)
    stats = [jnp.zeros((GROUP, HD), jnp.float32) for _ in range(heads)]
    values_there()
    for i, (b, g) in enumerate(pairs):
        here = slice(i * n, (i + 1) * n)
        s = dot(halves(weights[here]), head(values, b, g))
        s = s + dot(halves(fresh_weights[here]), fresh(nv, b, g).astype(jnp.bfloat16))
        s = s[:n] + s[n:]
        for t in range(TOKENS):
            tb = t * rows + b
            part = slice(i * n + t * GROUP, i * n + (t + 1) * GROUP)
            stats[g] = jnp.where(lane == 2 * tb, peak[part], stats[g])
            stats[g] = jnp.where(lane == 2 * tb + 1, total[part], stats[g])
            block = s[t * GROUP : (t + 1) * GROUP]
            if hb >= GROUP:
                at = g * GROUP
                packed[at // hb, tb, at % hb : at % hb + GROUP] = block
            else:
                for j in range(GROUP // hb):
                    packed[g * (GROUP // hb) + j, tb] = block[j * hb : (j + 1) * hb]
    for g in range(heads):
        if hb >= GROUP:
            at = g * GROUP
            packed[at // hb, TOKENS * rows, at % hb : at % hb + GROUP] = stats[g]
        else:
            for j in range(GROUP // hb):
                packed[g * (GROUP // hb) + j, TOKENS * rows] = stats[g][j * hb : (j + 1) * hb]
    for k in range(half):
        outs[k][...] = packed[jnp.bitwise_xor(column % half, k)]


def combine_kernel(cols, *refs):
    parts, out = refs[:cols], refs[cols]
    cells = parts[0].shape[0] - 1
    hb = parts[0].shape[1]
    stats = [p[cells] for p in parts]
    attended = []
    for tb in range(cells):
        peaks = [s[:, 2 * tb : 2 * tb + 1] for s in stats]
        totals = [s[:, 2 * tb + 1 : 2 * tb + 2] for s in stats]
        top = functools.reduce(jnp.maximum, peaks)
        scales = [jnp.exp(p - top) for p in peaks]
        total = tree_sum([t * s for t, s in zip(totals, scales)])
        summed = tree_sum([p[tb] * s for p, s in zip(parts, scales)])
        attended.append(summed / total)
    rows = [
        jnp.concatenate([attended[tb][h : h + 1] for tb in range(cells)], axis=0) for h in range(hb)
    ]
    out[...] = jnp.concatenate(rows, axis=1).astype(out.dtype)


def group_order(value, groups):
    here = value.shape[1] // groups
    return jnp.concatenate(
        [value[t, r * here : (r + 1) * here] for r in range(groups) for t in range(TOKENS)], axis=0
    )


def canonical(parts, canon, me):
    cells = parts[0].shape[0]
    for k, part in enumerate(parts):
        canon[jnp.bitwise_xor(me, k), :cells] = part[...].astype(jnp.float32)
    rows = [canon[r, :cells] for r in range(len(parts))]
    return jnp.concatenate(rows, axis=0).astype(jnp.bfloat16)


def over_columns(width, body):
    size = width

    def step(j, carry):
        body(pl.multiple_of(j * size, 128), size)
        return carry

    lax.fori_loop(0, width // size, step, 0)


def across(count):
    return [0, *range(count - 1, 0, -1)]


def by_distance(refs):
    order = across(len(refs))
    return [refs[order.index(k)] for k in range(len(refs))]


def out_kernel(groups, *refs):
    parts, (weight, *outs) = refs[:groups], refs[groups:-3]
    canon, attended, packed = refs[-3:]
    half = packed.shape[2]
    attended[...] = canonical(parts, canon, lax.axis_index("row"))
    for i in range(2):
        packed[i] = dot(attended[...], weight[:, i * half : (i + 1) * half])
    bit = lax.axis_index("col") & 1
    for k, out in enumerate(outs):
        out[...] = packed[jnp.bitwise_xor(bit, k & 1)].astype(out.dtype)


def in_pieces(squares):
    first = squares.astype(WIRE).astype(jnp.float32)
    second = (squares - first).astype(WIRE).astype(jnp.float32)
    third = squares - first - second
    lane = lax.broadcasted_iota(jnp.int32, (squares.shape[0], HD), 1)
    return jnp.where(
        lane == 0, first, jnp.where(lane == 1, second, jnp.where(lane == 2, third, 0.0))
    )


def lanes_of(bit, half):
    return pl.ds(pl.multiple_of(bit * half, 128), half)


def mid_kernel(groups, residual, gains, *refs):
    parts, (mid, lifted) = by_distance(refs[:-2]), refs[-2:]
    half = mid.shape[1]
    here = lanes_of(lax.axis_index("col") & 1, half)
    own = residual[:, :, here].astype(jnp.float32)
    value = group_order(own, groups) + tree_sum([p[...].astype(jnp.float32) for p in parts])
    mid[...] = value
    lifted[...] = (value * gains[here].astype(jnp.float32).reshape(1, half)).astype(jnp.bfloat16)


def products(lifted, bit, gate_weight, up_weight, out_hidden):
    half = lifted.shape[1]
    start = 0
    if gate_weight.shape[1] > out_hidden:
        start = pl.multiple_of(lax.axis_index("side") * out_hidden, 128)
    rows, columns = lanes_of(bit, half), pl.ds(start, out_hidden)
    return dot(lifted, gate_weight[rows, columns]), dot(lifted, up_weight[rows, columns])


def lift_first_kernel(lifted, gate_weight, up_weight, gate, up):
    bit = lax.axis_index("col") & 1
    gate[...], up[...] = products(lifted[...], bit, gate_weight, up_weight, gate.shape[1])


def lift_second_kernel(
    own, received, gains, gate_weight, up_weight, gate_first, up_first, mid, keep, send, packed
):
    rows, hidden = gate_first.shape
    half, bit = rows // 2, lax.axis_index("col") & 1
    width = own.shape[1]
    mid[:, lanes_of(bit, width)] = own[...]
    mid[:, lanes_of(1 - bit, width)] = received[...]
    value = received[...]
    squares = own[...] * own[...] + value * value
    sent = in_pieces(jnp.sum(squares, axis=1, keepdims=True))
    gain = gains[lanes_of(1 - bit, width)].astype(jnp.float32).reshape(1, width)
    lifted = (value * gain).astype(jnp.bfloat16)
    gate, up = products(lifted, 1 - bit, gate_weight, up_weight, hidden)
    gate, up = gate + gate_first[...], up + up_first[...]
    for i in range(2):
        part = slice(i * half, (i + 1) * half)
        packed[i, :, hidden:] = jnp.concatenate([sent[part], sent[part]], axis=0)
        packed[i, :, :hidden] = jnp.concatenate([gate[part], up[part]], axis=0)
    bit = lax.axis_index("row") & 1
    keep[...] = packed[bit].astype(keep.dtype)
    send[...] = packed[1 - bit].astype(send.dtype)


def act_kernel(model, *refs):
    parts, out = refs[:-1], refs[-1]
    hidden = parts[0].shape[1] - HD
    cells = parts[0].shape[0] // 2
    values = [p[...].astype(jnp.float32) for p in parts]
    total = tree_sum(values[0::2]) + tree_sum(values[1::2])
    squares = jnp.sum(total[:cells, hidden:], axis=1, keepdims=True)
    inv = lax.rsqrt(squares / model + 1e-05)
    gate = total[:cells, :hidden] * inv
    up = total[cells:, :hidden] * inv
    out[...] = (gate / (1.0 + jnp.exp(-gate)) * up).astype(out.dtype)


def gather_kernel(own, received, out, packed):
    bit = lax.axis_index("row") & 1
    packed[bit] = own[...].astype(jnp.float32)
    packed[1 - bit] = received[...].astype(jnp.float32)
    out[...] = jnp.concatenate([packed[0], packed[1]], axis=0).astype(out.dtype)


def down_kernel(other, act, weight, *refs):
    out = refs[-1]
    hidden = act.shape[1]
    start = 0
    if weight.shape[0] > hidden:
        start = pl.multiple_of(jnp.bitwise_xor(lax.axis_index("side"), other) * hidden, 128)

    def body(at, size):
        product = dot(act[...], weight[pl.ds(start, hidden), pl.ds(at, size)])
        if len(refs) > 1:
            product = product + refs[0][:, pl.ds(at, size)]
        out[:, pl.ds(at, size)] = product.astype(out.dtype)

    over_columns(out.shape[1], body)


def final_kernel(groups, mid, *refs):
    parts, out = refs[:-1], refs[-1]
    total = mid[...] + tree_sum([p[...].astype(jnp.float32) for p in parts])
    here = out.shape[1] // groups
    for t in range(TOKENS):
        block = [
            total[(r * TOKENS + t) * here : (r * TOKENS + t + 1) * here] for r in range(groups)
        ]
        out[t] = jnp.concatenate(block, axis=0).astype(out.dtype)


def shards(
    query,
    new_keys,
    new_values,
    key_cache,
    value_cache,
    lengths,
    residual,
    out_weight,
    norm_gain,
    gate_weight,
    up_weight,
    down_weight,
):
    sides, groups, cols = (lax.axis_size(a) for a in ("side", "row", "col"))
    rows_here = key_cache.shape[0]
    total_rows = residual.shape[1]
    width_share = residual.shape[2]
    hidden_share = gate_weight.shape[1]
    features = out_weight.shape[0]
    model = width_share * groups
    m = TOKENS * total_rows
    cells = TOKENS * rows_here
    hb = HEADS // cols
    split = 2 if sides == 2 and (hidden_share // 2) % 128 == 0 else 1
    hidden = hidden_share // split
    f32, bf16 = jnp.float32, jnp.bfloat16
    shape = jax.ShapeDtypeStruct
    pad = -(-cells // 8) * 8

    sources = [query, new_keys, new_values, key_cache, value_cache]
    message = shape((cells + 1, hb, HD), f32)
    sources = [query, new_keys, new_values, key_cache, value_cache]

    inputs = [pltpu.VMEM(a.shape, a.dtype) for a in sources]
    packed = pltpu.VMEM((cols // 2, *message.shape), f32)
    result = call(
        functools.partial(attention_far_kernel, cols),
        [message] * (cols // 2) + inputs + [pltpu.VMEM((8, HD), jnp.int32)],
        [ANY_SPEC] * 6,
        [pltpu.SMEM(lengths.shape, lengths.dtype), packed, pltpu.SemaphoreType.DMA((6,))],
        name="attention_far",
    )(*[in_hbm(a) for a in [*sources, lengths]])
    far, inputs = result[: cols // 2], result[cols // 2 :]
    far = [partner(far[k], "col", cols // 2 + k) for k in range(cols // 2)]
    near = call(
        functools.partial(attention_near_kernel, cols),
        [message] * (cols // 2),
        [VMEM_SPEC] * 6,
        [packed],
        name="attention_near",
    )(*[in_vmem(a) for a in inputs])
    parts = far + [near[0]] + [partner(near[k], "col", k) for k in range(1, cols // 2)]
    attended = call(
        functools.partial(combine_kernel, cols),
        shape((cells, features), bf16),
        [VMEM_SPEC] * cols,
        flops=40 * 10**9,
        name="combine",
    )(*parts)
    gathered = spread(attended, "row")
    half = width_share // 2
    partials = call(
        functools.partial(out_kernel, groups),
        [shape((m, half), WIRE)] * cols,
        [VMEM_SPEC] * (groups + 1),
        [
            pltpu.VMEM((groups, pad, features), f32),
            pltpu.VMEM((m, features), bf16),
            pltpu.VMEM((2, m, half), f32),
        ],
        name="out_projection",
    )(*gathered, in_vmem(out_weight))
    partials = [partials[0]] + [partner(partials[k], "col", k) for k in range(1, cols)]
    norm_gain = in_vmem(norm_gain)
    own, own_lifted = call(
        functools.partial(mid_kernel, groups),
        [shape((m, half), f32), shape((m, half), bf16)],
        [VMEM_SPEC] * (cols + 2),
        name="mid",
    )(in_vmem(residual), norm_gain, *[partials[k] for k in across(cols)])
    received = partner(own, "col", 1)
    weights = [in_vmem(gate_weight), in_vmem(up_weight)]
    first = call(
        lift_first_kernel,
        [shape((m, hidden), f32)] * 2,
        [VMEM_SPEC] * 3,
        name="gate_up_first",
    )(own_lifted, *weights)
    mid, keep, send = call(
        lift_second_kernel,
        [shape((m, width_share), f32)] + [shape((m, hidden + HD), WIRE)] * 2,
        [VMEM_SPEC] * 7,
        [pltpu.VMEM((2, m, hidden + HD), f32)],
        flops=40 * 10**9,
        name="gate_up_second",
    )(own, received, norm_gain, *weights, *first)
    sums = [keep] + [partner((keep, send)[k % 2], "row", k) for k in range(1, groups)]
    act = call(
        functools.partial(act_kernel, model),
        shape((m // 2, hidden), bf16),
        [VMEM_SPEC] * groups,
        name="activation",
    )(*sums)
    down_weight = in_vmem(down_weight)

    def down_part(same, from_row, other, before, result):
        rows = call(
            gather_kernel,
            shape((m, hidden), bf16),
            [VMEM_SPEC] * 2,
            [pltpu.VMEM((2, m // 2, hidden), f32)],
            name="gather_act",
        )(same, from_row)
        return call(
            functools.partial(down_kernel, other),
            shape((m, width_share), result),
            [VMEM_SPEC] * (2 + len(before)),
            name="down",
        )(rows, down_weight, *before)

    near = partner(act, "row", 1)
    if split > 1:
        first = down_part(act, near, 0, [], f32)
        far = partner(act, ("side", "row"), groups + 1)
        down = down_part(partner(act, "side", 1), far, 1, [first], WIRE)
    else:
        down = down_part(act, near, 0, [], WIRE)
    return call(
        functools.partial(final_kernel, groups),
        shape((TOKENS, total_rows, width_share), bf16),
        [VMEM_SPEC] * (cols + 1),
        name="final",
    )(mid, *spread(down, "col"))


def solution(mesh):
    in_specs = (
        P(None, "row", None),
        P(None, "row", None),
        P(None, "row", None),
        P("row", "col", None),
        P("row", "col", None),
        P("row"),
        P(None, None, "row"),
        P("col", "row"),
        P("row"),
        P("row", "col"),
        P("row", "col"),
        P("col", "row"),
    )
    out_specs = P(None, None, "row")
    return jax.shard_map(shards, mesh=mesh, in_specs=in_specs, out_specs=out_specs, check_vma=False)
```

```python
import functools
import math

import jax
import jax.numpy as jnp
from jax import lax
from jax.experimental import pallas as pl
from jax.experimental.pallas import tpu as pltpu
from jax.sharding import PartitionSpec as P

HEADS = 32
KV_HEADS = 4
HD = 128
GROUP = HEADS // KV_HEADS
TOKENS = 2
very_low = -1e30
MIB = 1024 * 1024
WIRE = jnp.bfloat16
VMEM_SPEC = pl.BlockSpec(memory_space=pltpu.VMEM)
ANY_SPEC = pl.BlockSpec(memory_space=pl.ANY)


def partner(value, axis, k):
    return lax.ppermute(value, axis, [(i, i ^ k) for i in range(lax.axis_size(axis))])


def spread(piece, axis):
    return [piece] + [partner(piece, axis, k) for k in range(1, lax.axis_size(axis))]


def tree_sum(values):
    while len(values) > 1:
        values = [values[i] + values[i + 1] for i in range(0, len(values), 2)]
    return values[0]


def dot(a, b):
    return jnp.dot(a, b, preferred_element_type=jnp.float32)


def dot_t(a, b):
    return lax.dot_general(a, b, (((1,), (1,)), ((), ())), preferred_element_type=jnp.float32)


def pieces(value):
    first = value.astype(WIRE).astype(jnp.float32)
    second = (value - first).astype(WIRE).astype(jnp.float32)
    return first, second, value - first - second


def call(kernel, out_shape, in_specs, scratch=(), limit=4, name=None, flops=None):
    cost = None
    if flops is not None:
        cost = pl.CostEstimate(flops=flops, bytes_accessed=1024, transcendentals=0)
    return pl.pallas_call(
        kernel,
        out_shape=out_shape,
        in_specs=in_specs,
        out_specs=jax.tree.map(lambda _: VMEM_SPEC, out_shape),
        scratch_shapes=list(scratch),
        compiler_params=pltpu.CompilerParams(vmem_limit_bytes=limit * MIB),
        cost_estimate=cost,
        name=name,
    )


def in_hbm(value):
    return pltpu.with_memory_space_constraint(value, pltpu.HBM)


def in_vmem(value):
    return pltpu.with_memory_space_constraint(value, pltpu.VMEM)


def attention_far_kernel(cols, *refs):
    half = cols // 2
    sources, (lengths, *outs), kept = refs[:5], refs[5 : 6 + half], refs[6 + half : 12 + half]
    sized, packed, sems = refs[12 + half :]
    keys, values, small = [], [], [pltpu.make_async_copy(lengths, sized, sems.at[0])]
    for i, (source, target) in enumerate(zip(sources, kept)):
        if i < 3:
            small.append(pltpu.make_async_copy(source, target, sems.at[i + 1]))
            continue
        for b in range(source.shape[0]):
            sem = sems.at[4 + (i - 3) * source.shape[0] + b]
            copy = pltpu.make_async_copy(source.at[b], target.at[b], sem)
            (keys, values)[i - 3].append(copy)
    for copy in small[:2] + keys + small[2:] + values:
        copy.start()
    for copy in small + keys:
        copy.wait()

    def values_there():
        for copy in values:
            copy.wait()

    row = lax.broadcasted_iota(jnp.int32, (8, HD), 0)
    limits = jnp.zeros((8, HD), jnp.int32)
    for b in range(kept[3].shape[0]):
        limits = jnp.where(row == b, sized[b], limits)
    kept[5][...] = limits
    attention(cols, 1, limits, *kept[:5], outs, packed, values_there)


def attention_near_kernel(cols, *refs):
    attention(cols, 0, refs[5][...], *refs[:5], refs[6:-1], refs[-1], lambda: None)


def attention(
    cols, far, limits, query, new_keys, new_values, keys, values, outs, packed, values_there
):
    half = cols // 2
    heads = KV_HEADS // 2
    column = lax.axis_index("col")
    chosen = jnp.bitwise_xor(column // half, far)

    def lanes(source):
        width = source.shape[2] // 2
        return source[:, :, pl.ds(pl.multiple_of(chosen * width, 128), width)].astype(jnp.float32)

    def head(source, b, g):
        return source[b, :, pl.ds(pl.multiple_of((chosen * heads + g) * HD, 128), HD)]

    rows, span, _ = keys.shape
    hb = HEADS // cols
    inv_root = 1.0 / math.sqrt(HD)
    n = TOKENS * GROUP
    pairs = [(b, g) for b in range(rows) for g in range(heads)]
    q32, nk, nv = lanes(query), lanes(new_keys), lanes(new_values)
    zeros = jnp.zeros((8 - TOKENS, HD), jnp.float32)

    def fresh(block, b, g):
        lanes = slice(g * HD, (g + 1) * HD)
        return jnp.concatenate([block[t, b : b + 1, lanes] for t in range(TOKENS)] + [zeros], axis=0)

    scores, fresh_scores = [], []
    for b, g in pairs:
        q = jnp.concatenate(
            [
                q32[t, b : b + 1, (g * GROUP + h) * HD : (g * GROUP + h + 1) * HD]
                for t in range(TOKENS)
                for h in range(GROUP)
            ],
            axis=0,
        ).astype(jnp.bfloat16)
        s = dot_t(q, head(keys, b, g)) * inv_root
        position = column * span + lax.broadcasted_iota(jnp.int32, (n, span), 1)
        scores.append(jnp.where(position < limits[b : b + 1, :1], s, very_low))
        f = dot_t(q, fresh(nk, b, g).astype(jnp.bfloat16)) * inv_root
        token = lax.broadcasted_iota(jnp.int32, (n, 8), 0) // GROUP
        slot = lax.broadcasted_iota(jnp.int32, (n, 8), 1)
        seen = jnp.logical_and(slot <= token, column == 0)
        fresh_scores.append(jnp.where(seen, f, very_low))
    scores = jnp.concatenate(scores, axis=0)
    fresh_scores = jnp.concatenate(fresh_scores, axis=0)
    peak = jnp.maximum(
        jnp.max(scores, axis=1, keepdims=True), jnp.max(fresh_scores, axis=1, keepdims=True)
    )
    weights = jnp.where(scores > 0.5 * very_low, jnp.exp(scores - peak), 0.0)
    fresh_weights = jnp.where(fresh_scores > 0.5 * very_low, jnp.exp(fresh_scores - peak), 0.0)
    total = jnp.sum(weights, axis=1, keepdims=True) + jnp.sum(fresh_weights, axis=1, keepdims=True)

    def halves(w):
        high = w.astype(jnp.bfloat16)
        low = (w - high.astype(jnp.float32)).astype(jnp.bfloat16)
        return jnp.concatenate([high, low], axis=0)

    lane = lax.broadcasted_iota(jnp.int32, (GROUP, HD), 1)
    stats = [jnp.zeros((GROUP, HD), jnp.float32) for _ in range(heads)]
    values_there()
    for i, (b, g) in enumerate(pairs):
        here = slice(i * n, (i + 1) * n)
        s = dot(halves(weights[here]), head(values, b, g))
        s = s + dot(halves(fresh_weights[here]), fresh(nv, b, g).astype(jnp.bfloat16))
        s = s[:n] + s[n:]
        for t in range(TOKENS):
            tb = t * rows + b
            part = slice(i * n + t * GROUP, i * n + (t + 1) * GROUP)
            for k, pair in enumerate(zip(pieces(peak[part]), pieces(total[part]))):
                at = 2 * (TOKENS * rows * k + tb)
                stats[g] = jnp.where(lane == at, pair[0], stats[g])
                stats[g] = jnp.where(lane == at + 1, pair[1], stats[g])
            block = s[t * GROUP : (t + 1) * GROUP].astype(WIRE)
            if hb >= GROUP:
                at = g * GROUP
                packed[at // hb, tb, at % hb : at % hb + GROUP] = block
            else:
                for j in range(GROUP // hb):
                    packed[g * (GROUP // hb) + j, tb] = block[j * hb : (j + 1) * hb]
    stats = [block.astype(WIRE) for block in stats]
    for g in range(heads):
        if hb >= GROUP:
            at = g * GROUP
            packed[at // hb, TOKENS * rows, at % hb : at % hb + GROUP] = stats[g]
        else:
            for j in range(GROUP // hb):
                packed[g * (GROUP // hb) + j, TOKENS * rows] = stats[g][j * hb : (j + 1) * hb]
    for k in range(half):
        outs[k][...] = packed[jnp.bitwise_xor(column % half, k)]


def combine_kernel(cols, *refs):
    parts, out = refs[:cols], refs[cols]
    cells = parts[0].shape[0] - 1
    hb = parts[0].shape[1]
    n = 2 * cells
    stats = [p[cells].astype(jnp.float32) for p in parts]
    stats = [s[:, :n] + s[:, n : 2 * n] + s[:, 2 * n : 3 * n] for s in stats]
    attended = []
    for tb in range(cells):
        peaks = [s[:, 2 * tb : 2 * tb + 1] for s in stats]
        totals = [s[:, 2 * tb + 1 : 2 * tb + 2] for s in stats]
        top = functools.reduce(jnp.maximum, peaks)
        scales = [jnp.exp(p - top) for p in peaks]
        total = tree_sum([t * s for t, s in zip(totals, scales)])
        summed = tree_sum([p[tb].astype(jnp.float32) * s for p, s in zip(parts, scales)])
        attended.append(summed / total)
    rows = [
        jnp.concatenate([attended[tb][h : h + 1] for tb in range(cells)], axis=0) for h in range(hb)
    ]
    out[...] = jnp.concatenate(rows, axis=1).astype(out.dtype)


def group_order(value, groups):
    here = value.shape[1] // groups
    return jnp.concatenate(
        [value[t, r * here : (r + 1) * here] for r in range(groups) for t in range(TOKENS)], axis=0
    )


def canonical(parts, canon, me):
    cells = parts[0].shape[0]
    for k, part in enumerate(parts):
        canon[jnp.bitwise_xor(me, k), :cells] = part[...].astype(jnp.float32)
    rows = [canon[r, :cells] for r in range(len(parts))]
    return jnp.concatenate(rows, axis=0).astype(jnp.bfloat16)


def over_columns(width, body):
    size = width

    def step(j, carry):
        body(pl.multiple_of(j * size, 128), size)
        return carry

    lax.fori_loop(0, width // size, step, 0)


def across(count):
    return [0, *range(count - 1, 0, -1)]


def by_distance(refs):
    order = across(len(refs))
    return [refs[order.index(k)] for k in range(len(refs))]


def out_kernel(groups, *refs):
    parts, (weight, *outs) = refs[:groups], refs[groups:-3]
    canon, attended, packed = refs[-3:]
    half = packed.shape[2]
    attended[...] = canonical(parts, canon, lax.axis_index("row"))
    for i in range(2):
        packed[i] = dot(attended[...], weight[:, i * half : (i + 1) * half])
    bit = lax.axis_index("col") & 1
    for k, out in enumerate(outs):
        out[...] = packed[jnp.bitwise_xor(bit, k & 1)].astype(out.dtype)


def in_pieces(squares):
    lane = lax.broadcasted_iota(jnp.int32, (squares.shape[0], HD), 1)
    result = jnp.zeros(lane.shape, jnp.float32)
    for i, piece in enumerate(pieces(squares)):
        result = jnp.where(lane == i, piece, result)
    return result


def lanes_of(bit, half):
    return pl.ds(pl.multiple_of(bit * half, 128), half)


def mid_kernel(groups, residual, gains, *refs):
    parts, (mid, lifted) = by_distance(refs[:-2]), refs[-2:]
    half = mid.shape[1]
    here = lanes_of(lax.axis_index("col") & 1, half)
    own = residual[:, :, here].astype(jnp.float32)
    value = group_order(own, groups) + tree_sum([p[...].astype(jnp.float32) for p in parts])
    mid[...] = value
    lifted[...] = (value * gains[here].astype(jnp.float32).reshape(1, half)).astype(jnp.bfloat16)


def products(lifted, bit, gate_weight, up_weight, out_hidden):
    half = lifted.shape[1]
    start = 0
    if gate_weight.shape[1] > out_hidden:
        start = pl.multiple_of(lax.axis_index("side") * out_hidden, 128)
    rows, columns = lanes_of(bit, half), pl.ds(start, out_hidden)
    return dot(lifted, gate_weight[rows, columns]), dot(lifted, up_weight[rows, columns])


def lift_first_kernel(lifted, gate_weight, up_weight, gate, up):
    bit = lax.axis_index("col") & 1
    gate[...], up[...] = products(lifted[...], bit, gate_weight, up_weight, gate.shape[1])


def lift_second_kernel(
    own, received, gains, gate_weight, up_weight, gate_first, up_first, mid, keep, send, packed
):
    rows, hidden = gate_first.shape
    half, bit = rows // 2, lax.axis_index("col") & 1
    width = own.shape[1]
    mid[:, lanes_of(bit, width)] = own[...]
    mid[:, lanes_of(1 - bit, width)] = received[...]
    value = received[...]
    squares = own[...] * own[...] + value * value
    sent = in_pieces(jnp.sum(squares, axis=1, keepdims=True))
    gain = gains[lanes_of(1 - bit, width)].astype(jnp.float32).reshape(1, width)
    lifted = (value * gain).astype(jnp.bfloat16)
    gate, up = products(lifted, 1 - bit, gate_weight, up_weight, hidden)
    gate, up = gate + gate_first[...], up + up_first[...]
    for i in range(2):
        part = slice(i * half, (i + 1) * half)
        packed[i, :, hidden:] = jnp.concatenate([sent[part], sent[part]], axis=0)
        packed[i, :, :hidden] = jnp.concatenate([gate[part], up[part]], axis=0)
    bit = lax.axis_index("row") & 1
    keep[...] = packed[bit].astype(keep.dtype)
    send[...] = packed[1 - bit].astype(send.dtype)


def act_kernel(model, *refs):
    parts, out = refs[:-1], refs[-1]
    hidden = parts[0].shape[1] - HD
    cells = parts[0].shape[0] // 2
    values = [p[...].astype(jnp.float32) for p in parts]
    total = tree_sum(values[0::2]) + tree_sum(values[1::2])
    squares = jnp.sum(total[:cells, hidden:], axis=1, keepdims=True)
    inv = lax.rsqrt(squares / model + 1e-05)
    gate = total[:cells, :hidden] * inv
    up = total[cells:, :hidden] * inv
    out[...] = (gate / (1.0 + jnp.exp(-gate)) * up).astype(out.dtype)


def gather_kernel(own, received, out, packed):
    bit = lax.axis_index("row") & 1
    packed[bit] = own[...].astype(jnp.float32)
    packed[1 - bit] = received[...].astype(jnp.float32)
    out[...] = jnp.concatenate([packed[0], packed[1]], axis=0).astype(out.dtype)


def down_kernel(other, act, weight, *refs):
    out = refs[-1]
    hidden = act.shape[1]
    start = 0
    if weight.shape[0] > hidden:
        start = pl.multiple_of(jnp.bitwise_xor(lax.axis_index("side"), other) * hidden, 128)

    def body(at, size):
        product = dot(act[...], weight[pl.ds(start, hidden), pl.ds(at, size)])
        if len(refs) > 1:
            product = product + refs[0][:, pl.ds(at, size)]
        out[:, pl.ds(at, size)] = product.astype(out.dtype)

    over_columns(out.shape[1], body)


def final_kernel(groups, mid, *refs):
    parts, out = refs[:-1], refs[-1]
    total = mid[...] + tree_sum([p[...].astype(jnp.float32) for p in parts])
    here = out.shape[1] // groups
    for t in range(TOKENS):
        block = [
            total[(r * TOKENS + t) * here : (r * TOKENS + t + 1) * here] for r in range(groups)
        ]
        out[t] = jnp.concatenate(block, axis=0).astype(out.dtype)


def shards(
    query,
    new_keys,
    new_values,
    key_cache,
    value_cache,
    lengths,
    residual,
    out_weight,
    norm_gain,
    gate_weight,
    up_weight,
    down_weight,
):
    sides, groups, cols = (lax.axis_size(a) for a in ("side", "row", "col"))
    rows_here = key_cache.shape[0]
    total_rows = residual.shape[1]
    width_share = residual.shape[2]
    hidden_share = gate_weight.shape[1]
    features = out_weight.shape[0]
    model = width_share * groups
    m = TOKENS * total_rows
    cells = TOKENS * rows_here
    hb = HEADS // cols
    split = 2 if sides == 2 and (hidden_share // 2) % 128 == 0 else 1
    hidden = hidden_share // split
    f32, bf16 = jnp.float32, jnp.bfloat16
    shape = jax.ShapeDtypeStruct
    pad = -(-cells // 8) * 8

    sources = [query, new_keys, new_values, key_cache, value_cache]
    message = shape((cells + 1, hb, HD), WIRE)
    sources = [query, new_keys, new_values, key_cache, value_cache]

    inputs = [pltpu.VMEM(a.shape, a.dtype) for a in sources]
    packed = pltpu.VMEM((cols // 2, *message.shape), WIRE)
    result = call(
        functools.partial(attention_far_kernel, cols),
        [message] * (cols // 2) + inputs + [pltpu.VMEM((8, HD), jnp.int32)],
        [ANY_SPEC] * 6,
        [
            pltpu.SMEM(lengths.shape, lengths.dtype),
            packed,
            pltpu.SemaphoreType.DMA((4 + 2 * rows_here,)),
        ],
        name="attention_far",
    )(*[in_hbm(a) for a in [*sources, lengths]])
    far, inputs = result[: cols // 2], result[cols // 2 :]
    far = [partner(far[k], "col", cols // 2 + k) for k in range(cols // 2)]
    near = call(
        functools.partial(attention_near_kernel, cols),
        [message] * (cols // 2),
        [VMEM_SPEC] * 6,
        [packed],
        name="attention_near",
    )(*[in_vmem(a) for a in inputs])
    parts = far + [near[0]] + [partner(near[k], "col", k) for k in range(1, cols // 2)]
    attended = call(
        functools.partial(combine_kernel, cols),
        shape((cells, features), bf16),
        [VMEM_SPEC] * cols,
        flops=40 * 10**9,
        name="combine",
    )(*parts)
    gathered = spread(attended, "row")
    half = width_share // 2
    partials = call(
        functools.partial(out_kernel, groups),
        [shape((m, half), WIRE)] * cols,
        [VMEM_SPEC] * (groups + 1),
        [
            pltpu.VMEM((groups, pad, features), f32),
            pltpu.VMEM((m, features), bf16),
            pltpu.VMEM((2, m, half), f32),
        ],
        name="out_projection",
    )(*gathered, in_vmem(out_weight))
    partials = [partials[0]] + [partner(partials[k], "col", k) for k in range(1, cols)]
    norm_gain = in_vmem(norm_gain)
    own, own_lifted = call(
        functools.partial(mid_kernel, groups),
        [shape((m, half), f32), shape((m, half), bf16)],
        [VMEM_SPEC] * (cols + 2),
        name="mid",
    )(in_vmem(residual), norm_gain, *[partials[k] for k in across(cols)])
    received = partner(own, "col", 1)
    weights = [in_vmem(gate_weight), in_vmem(up_weight)]
    first = call(
        lift_first_kernel,
        [shape((m, hidden), f32)] * 2,
        [VMEM_SPEC] * 3,
        name="gate_up_first",
    )(own_lifted, *weights)
    mid, keep, send = call(
        lift_second_kernel,
        [shape((m, width_share), f32)] + [shape((m, hidden + HD), WIRE)] * 2,
        [VMEM_SPEC] * 7,
        [pltpu.VMEM((2, m, hidden + HD), f32)],
        flops=40 * 10**9,
        name="gate_up_second",
    )(own, received, norm_gain, *weights, *first)
    sums = [keep] + [partner((keep, send)[k % 2], "row", k) for k in range(1, groups)]
    act = call(
        functools.partial(act_kernel, model),
        shape((m // 2, hidden), bf16),
        [VMEM_SPEC] * groups,
        name="activation",
    )(*sums)
    down_weight = in_vmem(down_weight)

    def down_part(same, from_row, other, before, result):
        rows = call(
            gather_kernel,
            shape((m, hidden), bf16),
            [VMEM_SPEC] * 2,
            [pltpu.VMEM((2, m // 2, hidden), f32)],
            name="gather_act",
        )(same, from_row)
        return call(
            functools.partial(down_kernel, other),
            shape((m, width_share), result),
            [VMEM_SPEC] * (2 + len(before)),
            name="down",
        )(rows, down_weight, *before)

    near = partner(act, "row", 1)
    if split > 1:
        first = down_part(act, near, 0, [], f32)
        far = partner(act, ("side", "row"), groups + 1)
        down = down_part(partner(act, "side", 1), far, 1, [first], WIRE)
    else:
        down = down_part(act, near, 0, [], WIRE)
    return call(
        functools.partial(final_kernel, groups),
        shape((TOKENS, total_rows, width_share), bf16),
        [VMEM_SPEC] * (cols + 1),
        name="final",
    )(mid, *spread(down, "col"))


def solution(mesh):
    in_specs = (
        P(None, "row", None),
        P(None, "row", None),
        P(None, "row", None),
        P("row", "col", None),
        P("row", "col", None),
        P("row"),
        P(None, None, "row"),
        P("col", "row"),
        P("row"),
        P("row", "col"),
        P("row", "col"),
        P("col", "row"),
    )
    out_specs = P(None, None, "row")
    return jax.shard_map(shards, mesh=mesh, in_specs=in_specs, out_specs=out_specs, check_vma=False)
```

```python
import functools
import math

import jax
import jax.numpy as jnp
from jax import lax
from jax.experimental import pallas as pl
from jax.experimental.pallas import tpu as pltpu
from jax.sharding import PartitionSpec as P

HEADS = 32
KV_HEADS = 4
HD = 128
GROUP = HEADS // KV_HEADS
TOKENS = 2
very_low = -1e30
MIB = 1024 * 1024
WIRE = jnp.bfloat16
VMEM_SPEC = pl.BlockSpec(memory_space=pltpu.VMEM)
ANY_SPEC = pl.BlockSpec(memory_space=pl.ANY)


def partner(value, axis, k):
    return lax.ppermute(value, axis, [(i, i ^ k) for i in range(lax.axis_size(axis))])


def spread(piece, axis):
    return [piece] + [partner(piece, axis, k) for k in range(1, lax.axis_size(axis))]


def tree_sum(values):
    while len(values) > 1:
        values = [values[i] + values[i + 1] for i in range(0, len(values), 2)]
    return values[0]


def dot(a, b):
    return jnp.dot(a, b, preferred_element_type=jnp.float32)


def dot_t(a, b):
    return lax.dot_general(a, b, (((1,), (1,)), ((), ())), preferred_element_type=jnp.float32)


def call(kernel, out_shape, in_specs, scratch=(), limit=4, name=None, flops=None):
    cost = None
    if flops is not None:
        cost = pl.CostEstimate(flops=flops, bytes_accessed=1024, transcendentals=0)
    return pl.pallas_call(
        kernel,
        out_shape=out_shape,
        in_specs=in_specs,
        out_specs=jax.tree.map(lambda _: VMEM_SPEC, out_shape),
        scratch_shapes=list(scratch),
        compiler_params=pltpu.CompilerParams(vmem_limit_bytes=limit * MIB),
        cost_estimate=cost,
        name=name,
    )


def in_hbm(value):
    return pltpu.with_memory_space_constraint(value, pltpu.HBM)


def in_vmem(value):
    return pltpu.with_memory_space_constraint(value, pltpu.VMEM)


def attention_far_kernel(cols, *refs):
    half = cols // 2
    sources, (lengths, *outs), kept = refs[:5], refs[5 : 6 + half], refs[6 + half : 12 + half]
    sized, packed, sems = refs[12 + half :]
    copies = [
        pltpu.make_async_copy(source, target, sems.at[i])
        for i, (source, target) in enumerate(zip(sources, kept))
    ]
    copies.append(pltpu.make_async_copy(lengths, sized, sems.at[5]))
    for copy in copies:
        copy.start()
    for i in (0, 1, 2, 5, 3):
        copies[i].wait()
    row = lax.broadcasted_iota(jnp.int32, (8, HD), 0)
    limits = jnp.zeros((8, HD), jnp.int32)
    for b in range(kept[3].shape[0]):
        limits = jnp.where(row == b, sized[b], limits)
    kept[5][...] = limits
    attention(cols, 1, limits, *kept[:5], outs, packed, copies[4].wait)


def attention_near_kernel(cols, *refs):
    attention(cols, 0, refs[5][...], *refs[:5], refs[6:-1], refs[-1], lambda: None)


def attention(
    cols, far, limits, query, new_keys, new_values, keys, values, outs, packed, values_there
):
    half = cols // 2
    heads = KV_HEADS // 2
    column = lax.axis_index("col")
    chosen = jnp.bitwise_xor(column // half, far)

    def lanes(source):
        width = source.shape[2] // 2
        return source[:, :, pl.ds(pl.multiple_of(chosen * width, 128), width)].astype(jnp.float32)

    def head(source, b, g):
        return source[b, :, pl.ds(pl.multiple_of((chosen * heads + g) * HD, 128), HD)]

    rows, span, _ = keys.shape
    hb = HEADS // cols
    inv_root = 1.0 / math.sqrt(HD)
    n = TOKENS * GROUP
    pairs = [(b, g) for b in range(rows) for g in range(heads)]
    q32, nk, nv = lanes(query), lanes(new_keys), lanes(new_values)
    zeros = jnp.zeros((8 - TOKENS, HD), jnp.float32)

    def fresh(block, b, g):
        lanes = slice(g * HD, (g + 1) * HD)
        return jnp.concatenate([block[t, b : b + 1, lanes] for t in range(TOKENS)] + [zeros], axis=0)

    scores, fresh_scores = [], []
    for b, g in pairs:
        q = jnp.concatenate(
            [
                q32[t, b : b + 1, (g * GROUP + h) * HD : (g * GROUP + h + 1) * HD]
                for t in range(TOKENS)
                for h in range(GROUP)
            ],
            axis=0,
        ).astype(jnp.bfloat16)
        s = dot_t(q, head(keys, b, g)) * inv_root
        position = column * span + lax.broadcasted_iota(jnp.int32, (n, span), 1)
        scores.append(jnp.where(position < limits[b : b + 1, :1], s, very_low))
        f = dot_t(q, fresh(nk, b, g).astype(jnp.bfloat16)) * inv_root
        token = lax.broadcasted_iota(jnp.int32, (n, 8), 0) // GROUP
        slot = lax.broadcasted_iota(jnp.int32, (n, 8), 1)
        seen = jnp.logical_and(slot <= token, column == 0)
        fresh_scores.append(jnp.where(seen, f, very_low))
    scores = jnp.concatenate(scores, axis=0)
    fresh_scores = jnp.concatenate(fresh_scores, axis=0)
    peak = jnp.maximum(
        jnp.max(scores, axis=1, keepdims=True), jnp.max(fresh_scores, axis=1, keepdims=True)
    )
    weights = jnp.where(scores > 0.5 * very_low, jnp.exp(scores - peak), 0.0)
    fresh_weights = jnp.where(fresh_scores > 0.5 * very_low, jnp.exp(fresh_scores - peak), 0.0)
    total = jnp.sum(weights, axis=1, keepdims=True) + jnp.sum(fresh_weights, axis=1, keepdims=True)

    def halves(w):
        high = w.astype(jnp.bfloat16)
        low = (w - high.astype(jnp.float32)).astype(jnp.bfloat16)
        return jnp.concatenate([high, low], axis=0)

    lane = lax.broadcasted_iota(jnp.int32, (GROUP, HD), 1)
    stats = [jnp.zeros((GROUP, HD), jnp.float32) for _ in range(heads)]
    values_there()
    for i, (b, g) in enumerate(pairs):
        here = slice(i * n, (i + 1) * n)
        s = dot(halves(weights[here]), head(values, b, g))
        s = s + dot(halves(fresh_weights[here]), fresh(nv, b, g).astype(jnp.bfloat16))
        s = s[:n] + s[n:]
        for t in range(TOKENS):
            tb = t * rows + b
            part = slice(i * n + t * GROUP, i * n + (t + 1) * GROUP)
            stats[g] = jnp.where(lane == 2 * tb, peak[part], stats[g])
            stats[g] = jnp.where(lane == 2 * tb + 1, total[part], stats[g])
            block = s[t * GROUP : (t + 1) * GROUP]
            if hb >= GROUP:
                at = g * GROUP
                packed[at // hb, tb, at % hb : at % hb + GROUP] = block
            else:
                for j in range(GROUP // hb):
                    packed[g * (GROUP // hb) + j, tb] = block[j * hb : (j + 1) * hb]
    for g in range(heads):
        if hb >= GROUP:
            at = g * GROUP
            packed[at // hb, TOKENS * rows, at % hb : at % hb + GROUP] = stats[g]
        else:
            for j in range(GROUP // hb):
                packed[g * (GROUP // hb) + j, TOKENS * rows] = stats[g][j * hb : (j + 1) * hb]
    for k in range(half):
        outs[k][...] = packed[jnp.bitwise_xor(column % half, k)]


def combine_kernel(cols, *refs):
    parts, out = refs[:cols], refs[cols]
    cells = parts[0].shape[0] - 1
    hb = parts[0].shape[1]
    stats = [p[cells] for p in parts]
    attended = []
    for tb in range(cells):
        peaks = [s[:, 2 * tb : 2 * tb + 1] for s in stats]
        totals = [s[:, 2 * tb + 1 : 2 * tb + 2] for s in stats]
        top = functools.reduce(jnp.maximum, peaks)
        scales = [jnp.exp(p - top) for p in peaks]
        total = tree_sum([t * s for t, s in zip(totals, scales)])
        summed = tree_sum([p[tb] * s for p, s in zip(parts, scales)])
        attended.append(summed / total)
    rows = [
        jnp.concatenate([attended[tb][h : h + 1] for tb in range(cells)], axis=0) for h in range(hb)
    ]
    out[...] = jnp.concatenate(rows, axis=1).astype(out.dtype)


def group_order(value, groups):
    here = value.shape[1] // groups
    return jnp.concatenate(
        [value[t, r * here : (r + 1) * here] for r in range(groups) for t in range(TOKENS)], axis=0
    )


def canonical(parts, canon, me):
    cells = parts[0].shape[0]
    for k, part in enumerate(parts):
        canon[jnp.bitwise_xor(me, k), :cells] = part[...].astype(jnp.float32)
    rows = [canon[r, :cells] for r in range(len(parts))]
    return jnp.concatenate(rows, axis=0).astype(jnp.bfloat16)


def over_columns(width, body):
    size = width

    def step(j, carry):
        body(pl.multiple_of(j * size, 128), size)
        return carry

    lax.fori_loop(0, width // size, step, 0)


def across(count):
    return [0, *range(count - 1, 0, -1)]


def by_distance(refs):
    order = across(len(refs))
    return [refs[order.index(k)] for k in range(len(refs))]


def gather_order(groups):
    return [0, 1, 3, 2] if groups == 4 else list(range(groups))


def sum_order(groups):
    return [0, 3, 1, 2] if groups == 4 else list(range(groups))


def out_kernel(groups, *refs):
    parts = [refs[gather_order(groups).index(k)] for k in range(groups)]
    weight, *outs = refs[groups:-3]
    canon, attended, packed = refs[-3:]
    half = packed.shape[2]
    attended[...] = canonical(parts, canon, lax.axis_index("row"))
    for i in range(2):
        packed[i] = dot(attended[...], weight[:, i * half : (i + 1) * half])
    bit = lax.axis_index("col") & 1
    for k, out in enumerate(outs):
        out[...] = packed[jnp.bitwise_xor(bit, k & 1)].astype(out.dtype)


def in_pieces(squares):
    first = squares.astype(WIRE).astype(jnp.float32)
    second = (squares - first).astype(WIRE).astype(jnp.float32)
    third = squares - first - second
    lane = lax.broadcasted_iota(jnp.int32, (squares.shape[0], HD), 1)
    return jnp.where(
        lane == 0, first, jnp.where(lane == 1, second, jnp.where(lane == 2, third, 0.0))
    )


def lanes_of(bit, half):
    return pl.ds(pl.multiple_of(bit * half, 128), half)


def mid_kernel(groups, residual, gains, *refs):
    parts, (mid, lifted) = by_distance(refs[:-2]), refs[-2:]
    half = mid.shape[1]
    here = lanes_of(lax.axis_index("col") & 1, half)
    own = residual[:, :, here].astype(jnp.float32)
    value = group_order(own, groups) + tree_sum([p[...].astype(jnp.float32) for p in parts])
    mid[...] = value
    lifted[...] = (value * gains[here].astype(jnp.float32).reshape(1, half)).astype(jnp.bfloat16)


def products(lifted, bit, gate_weight, up_weight, out_hidden):
    half = lifted.shape[1]
    start = 0
    if gate_weight.shape[1] > out_hidden:
        start = pl.multiple_of(lax.axis_index("side") * out_hidden, 128)
    rows, columns = lanes_of(bit, half), pl.ds(start, out_hidden)
    return dot(lifted, gate_weight[rows, columns]), dot(lifted, up_weight[rows, columns])


def lift_first_kernel(lifted, gate_weight, up_weight, gate, up):
    bit = lax.axis_index("col") & 1
    gate[...], up[...] = products(lifted[...], bit, gate_weight, up_weight, gate.shape[1])


def lift_second_kernel(
    own, received, gains, gate_weight, up_weight, gate_first, up_first, mid, *rest
):
    outs, packed = rest[:-1], rest[-1]
    rows, hidden = gate_first.shape
    half, bit = rows // 2, lax.axis_index("col") & 1
    width = own.shape[1]
    mid[:, lanes_of(bit, width)] = own[...]
    mid[:, lanes_of(1 - bit, width)] = received[...]
    value = received[...]
    squares = own[...] * own[...] + value * value
    sent = in_pieces(jnp.sum(squares, axis=1, keepdims=True))
    gain = gains[lanes_of(1 - bit, width)].astype(jnp.float32).reshape(1, width)
    lifted = (value * gain).astype(jnp.bfloat16)
    gate, up = products(lifted, 1 - bit, gate_weight, up_weight, hidden)
    gate, up = gate + gate_first[...], up + up_first[...]
    for i in range(2):
        part = slice(i * half, (i + 1) * half)
        packed[i, :, hidden:] = jnp.concatenate([sent[part], sent[part]], axis=0)
        packed[i, :, :hidden] = jnp.concatenate([gate[part], up[part]], axis=0)
    bit = lax.axis_index("row") & 1
    mine, theirs = (packed[i].astype(outs[0].dtype) for i in (bit, 1 - bit))
    for k, out in enumerate(outs):
        out[...] = theirs if k % 2 else mine


def act_kernel(model, *refs):
    out = refs[-1]
    parts = [refs[sum_order(len(refs) - 1).index(k)] for k in range(len(refs) - 1)]
    hidden = parts[0].shape[1] - HD
    cells = parts[0].shape[0] // 2
    values = [p[...].astype(jnp.float32) for p in parts]
    total = tree_sum(values[0::2]) + tree_sum(values[1::2])
    squares = jnp.sum(total[:cells, hidden:], axis=1, keepdims=True)
    inv = lax.rsqrt(squares / model + 1e-05)
    gate = total[:cells, :hidden] * inv
    up = total[cells:, :hidden] * inv
    out[...] = (gate / (1.0 + jnp.exp(-gate)) * up).astype(out.dtype)


def gather_kernel(own, received, out, packed):
    bit = lax.axis_index("row") & 1
    packed[bit] = own[...].astype(jnp.float32)
    packed[1 - bit] = received[...].astype(jnp.float32)
    out[...] = jnp.concatenate([packed[0], packed[1]], axis=0).astype(out.dtype)


def down_kernel(other, act, weight, *refs):
    out = refs[-1]
    hidden = act.shape[1]
    start = 0
    if weight.shape[0] > hidden:
        start = pl.multiple_of(jnp.bitwise_xor(lax.axis_index("side"), other) * hidden, 128)

    def body(at, size):
        product = dot(act[...], weight[pl.ds(start, hidden), pl.ds(at, size)])
        if len(refs) > 1:
            product = product + refs[0][:, pl.ds(at, size)]
        out[:, pl.ds(at, size)] = product.astype(out.dtype)

    over_columns(out.shape[1], body)


def final_kernel(groups, mid, *refs):
    parts, out = refs[:-1], refs[-1]
    total = mid[...] + tree_sum([p[...].astype(jnp.float32) for p in parts])
    here = out.shape[1] // groups
    for t in range(TOKENS):
        block = [
            total[(r * TOKENS + t) * here : (r * TOKENS + t + 1) * here] for r in range(groups)
        ]
        out[t] = jnp.concatenate(block, axis=0).astype(out.dtype)


def shards(
    query,
    new_keys,
    new_values,
    key_cache,
    value_cache,
    lengths,
    residual,
    out_weight,
    norm_gain,
    gate_weight,
    up_weight,
    down_weight,
):
    sides, groups, cols = (lax.axis_size(a) for a in ("side", "row", "col"))
    rows_here = key_cache.shape[0]
    total_rows = residual.shape[1]
    width_share = residual.shape[2]
    hidden_share = gate_weight.shape[1]
    features = out_weight.shape[0]
    model = width_share * groups
    m = TOKENS * total_rows
    cells = TOKENS * rows_here
    hb = HEADS // cols
    split = 2 if sides == 2 and (hidden_share // 2) % 128 == 0 else 1
    hidden = hidden_share // split
    f32, bf16 = jnp.float32, jnp.bfloat16
    shape = jax.ShapeDtypeStruct
    pad = -(-cells // 8) * 8

    sources = [query, new_keys, new_values, key_cache, value_cache]
    message = shape((cells + 1, hb, HD), f32)
    sources = [query, new_keys, new_values, key_cache, value_cache]

    inputs = [pltpu.VMEM(a.shape, a.dtype) for a in sources]
    packed = pltpu.VMEM((cols // 2, *message.shape), f32)
    result = call(
        functools.partial(attention_far_kernel, cols),
        [message] * (cols // 2) + inputs + [pltpu.VMEM((8, HD), jnp.int32)],
        [ANY_SPEC] * 6,
        [pltpu.SMEM(lengths.shape, lengths.dtype), packed, pltpu.SemaphoreType.DMA((6,))],
        name="attention_far",
    )(*[in_hbm(a) for a in [*sources, lengths]])
    far, inputs = result[: cols // 2], result[cols // 2 :]
    far = [partner(far[k], "col", cols // 2 + k) for k in range(cols // 2)]
    near = call(
        functools.partial(attention_near_kernel, cols),
        [message] * (cols // 2),
        [VMEM_SPEC] * 6,
        [packed],
        name="attention_near",
    )(*[in_vmem(a) for a in inputs])
    parts = far + [near[0]] + [partner(near[k], "col", k) for k in range(1, cols // 2)]
    attended = call(
        functools.partial(combine_kernel, cols),
        shape((cells, features), bf16),
        [VMEM_SPEC] * cols,
        flops=40 * 10**9,
        name="combine",
    )(*parts)
    gathered = spread(attended, "row")
    half = width_share // 2
    partials = call(
        functools.partial(out_kernel, groups),
        [shape((m, half), WIRE)] * cols,
        [VMEM_SPEC] * (groups + 1),
        [
            pltpu.VMEM((groups, pad, features), f32),
            pltpu.VMEM((m, features), bf16),
            pltpu.VMEM((2, m, half), f32),
        ],
        name="out_projection",
    )(*[gathered[k] for k in gather_order(groups)], in_vmem(out_weight))
    partials = [partials[0]] + [partner(partials[k], "col", k) for k in range(1, cols)]
    norm_gain = in_vmem(norm_gain)
    own, own_lifted = call(
        functools.partial(mid_kernel, groups),
        [shape((m, half), f32), shape((m, half), bf16)],
        [VMEM_SPEC] * (cols + 2),
        name="mid",
    )(in_vmem(residual), norm_gain, *[partials[k] for k in across(cols)])
    received = partner(own, "col", 1)
    weights = [in_vmem(gate_weight), in_vmem(up_weight)]
    first = call(
        lift_first_kernel,
        [shape((m, hidden), f32)] * 2,
        [VMEM_SPEC] * 3,
        name="gate_up_first",
    )(own_lifted, *weights)
    mid, *sums = call(
        lift_second_kernel,
        [shape((m, width_share), f32)] + [shape((m, hidden + HD), WIRE)] * groups,
        [VMEM_SPEC] * 7,
        [pltpu.VMEM((2, m, hidden + HD), f32)],
        flops=40 * 10**9,
        name="gate_up_second",
    )(own, received, norm_gain, *weights, *first)
    sums = sums[:1] + [partner(sums[k], "row", k) for k in range(1, groups)]
    act = call(
        functools.partial(act_kernel, model),
        shape((m // 2, hidden), bf16),
        [VMEM_SPEC] * groups,
        name="activation",
    )(*[sums[k] for k in sum_order(groups)])
    down_weight = in_vmem(down_weight)

    def down_part(same, from_row, other, before, result):
        rows = call(
            gather_kernel,
            shape((m, hidden), bf16),
            [VMEM_SPEC] * 2,
            [pltpu.VMEM((2, m // 2, hidden), f32)],
            name="gather_act",
        )(same, from_row)
        return call(
            functools.partial(down_kernel, other),
            shape((m, width_share), result),
            [VMEM_SPEC] * (2 + len(before)),
            name="down",
        )(rows, down_weight, *before)

    near = partner(act, "row", 1)
    if split > 1:
        first = down_part(act, near, 0, [], f32)
        far = partner(act, ("side", "row"), groups + 1)
        down = down_part(partner(act, "side", 1), far, 1, [first], WIRE)
    else:
        down = down_part(act, near, 0, [], WIRE)
    return call(
        functools.partial(final_kernel, groups),
        shape((TOKENS, total_rows, width_share), bf16),
        [VMEM_SPEC] * (cols + 1),
        name="final",
    )(mid, *spread(down, "col"))


def solution(mesh):
    in_specs = (
        P(None, "row", None),
        P(None, "row", None),
        P(None, "row", None),
        P("row", "col", None),
        P("row", "col", None),
        P("row"),
        P(None, None, "row"),
        P("col", "row"),
        P("row"),
        P("row", "col"),
        P("row", "col"),
        P("col", "row"),
    )
    out_specs = P(None, None, "row")
    return jax.shard_map(shards, mesh=mesh, in_specs=in_specs, out_specs=out_specs, check_vma=False)
```

```python
import functools
import math

import jax
import jax.numpy as jnp
from jax import lax
from jax.experimental import pallas as pl
from jax.experimental.pallas import tpu as pltpu
from jax.sharding import PartitionSpec as P

HEADS = 32
KV_HEADS = 4
HD = 128
GROUP = HEADS // KV_HEADS
TOKENS = 2
very_low = -1e30
MIB = 1024 * 1024
WIRE = jnp.bfloat16
VMEM_SPEC = pl.BlockSpec(memory_space=pltpu.VMEM)
ANY_SPEC = pl.BlockSpec(memory_space=pl.ANY)


def partner(value, axis, k):
    return lax.ppermute(value, axis, [(i, i ^ k) for i in range(lax.axis_size(axis))])


def spread(piece, axis):
    return [piece] + [partner(piece, axis, k) for k in range(1, lax.axis_size(axis))]


def tree_sum(values):
    while len(values) > 1:
        values = [values[i] + values[i + 1] for i in range(0, len(values), 2)]
    return values[0]


def dot(a, b):
    return jnp.dot(a, b, preferred_element_type=jnp.float32)


def dot_t(a, b):
    return lax.dot_general(a, b, (((1,), (1,)), ((), ())), preferred_element_type=jnp.float32)


def call(kernel, out_shape, in_specs, scratch=(), limit=4, name=None, flops=None):
    cost = None
    if flops is not None:
        cost = pl.CostEstimate(flops=flops, bytes_accessed=1024, transcendentals=0)
    return pl.pallas_call(
        kernel,
        out_shape=out_shape,
        in_specs=in_specs,
        out_specs=jax.tree.map(lambda _: VMEM_SPEC, out_shape),
        scratch_shapes=list(scratch),
        compiler_params=pltpu.CompilerParams(vmem_limit_bytes=limit * MIB),
        cost_estimate=cost,
        name=name,
    )


def in_hbm(value):
    return pltpu.with_memory_space_constraint(value, pltpu.HBM)


def in_vmem(value):
    return pltpu.with_memory_space_constraint(value, pltpu.VMEM)


def attention_far_kernel(cols, *refs):
    half = cols // 2
    sources, (lengths, *outs), kept = refs[:5], refs[5 : 6 + half], refs[6 + half : 12 + half]
    sized, packed, sems = refs[12 + half :]
    copies = [
        pltpu.make_async_copy(source, target, sems.at[i])
        for i, (source, target) in enumerate(zip(sources, kept))
    ]
    copies.append(pltpu.make_async_copy(lengths, sized, sems.at[5]))
    for copy in copies:
        copy.start()
    for i in (0, 1, 2, 5, 3):
        copies[i].wait()
    row = lax.broadcasted_iota(jnp.int32, (8, HD), 0)
    limits = jnp.zeros((8, HD), jnp.int32)
    for b in range(kept[3].shape[0]):
        limits = jnp.where(row == b, sized[b], limits)
    kept[5][...] = limits
    attention(cols, 1, limits, *kept[:5], outs, packed, copies[4].wait)


def attention_near_kernel(cols, *refs):
    attention(cols, 0, refs[5][...], *refs[:5], refs[6:-1], refs[-1], lambda: None)


def attention(
    cols, far, limits, query, new_keys, new_values, keys, values, outs, packed, values_there
):
    half = cols // 2
    heads = KV_HEADS // 2
    column = lax.axis_index("col")
    chosen = jnp.bitwise_xor(column // half, far)

    def lanes(source):
        width = source.shape[2] // 2
        return source[:, :, pl.ds(pl.multiple_of(chosen * width, 128), width)].astype(jnp.float32)

    def head(source, b, g):
        return source[b, :, pl.ds(pl.multiple_of((chosen * heads + g) * HD, 128), HD)]

    rows, span, _ = keys.shape
    hb = HEADS // cols
    inv_root = 1.0 / math.sqrt(HD)
    n = TOKENS * GROUP
    pairs = [(b, g) for b in range(rows) for g in range(heads)]
    q32, nk, nv = lanes(query), lanes(new_keys), lanes(new_values)
    zeros = jnp.zeros((8 - TOKENS, HD), jnp.float32)

    def fresh(block, b, g):
        lanes = slice(g * HD, (g + 1) * HD)
        return jnp.concatenate([block[t, b : b + 1, lanes] for t in range(TOKENS)] + [zeros], axis=0)

    scores, fresh_scores = [], []
    for b, g in pairs:
        q = jnp.concatenate(
            [
                q32[t, b : b + 1, (g * GROUP + h) * HD : (g * GROUP + h + 1) * HD]
                for t in range(TOKENS)
                for h in range(GROUP)
            ],
            axis=0,
        ).astype(jnp.bfloat16)
        s = dot_t(q, head(keys, b, g)) * inv_root
        position = column * span + lax.broadcasted_iota(jnp.int32, (n, span), 1)
        scores.append(jnp.where(position < limits[b : b + 1, :1], s, very_low))
        f = dot_t(q, fresh(nk, b, g).astype(jnp.bfloat16)) * inv_root
        token = lax.broadcasted_iota(jnp.int32, (n, 8), 0) // GROUP
        slot = lax.broadcasted_iota(jnp.int32, (n, 8), 1)
        seen = jnp.logical_and(slot <= token, column == 0)
        fresh_scores.append(jnp.where(seen, f, very_low))
    scores = jnp.concatenate(scores, axis=0)
    fresh_scores = jnp.concatenate(fresh_scores, axis=0)
    peak = jnp.maximum(
        jnp.max(scores, axis=1, keepdims=True), jnp.max(fresh_scores, axis=1, keepdims=True)
    )
    weights = jnp.where(scores > 0.5 * very_low, jnp.exp(scores - peak), 0.0)
    fresh_weights = jnp.where(fresh_scores > 0.5 * very_low, jnp.exp(fresh_scores - peak), 0.0)
    total = jnp.sum(weights, axis=1, keepdims=True) + jnp.sum(fresh_weights, axis=1, keepdims=True)

    def halves(w):
        high = w.astype(jnp.bfloat16)
        low = (w - high.astype(jnp.float32)).astype(jnp.bfloat16)
        return jnp.concatenate([high, low], axis=0)

    lane = lax.broadcasted_iota(jnp.int32, (GROUP, HD), 1)
    stats = [jnp.zeros((GROUP, HD), jnp.float32) for _ in range(heads)]
    values_there()
    for i, (b, g) in enumerate(pairs):
        here = slice(i * n, (i + 1) * n)
        s = dot(halves(weights[here]), head(values, b, g))
        s = s + dot(halves(fresh_weights[here]), fresh(nv, b, g).astype(jnp.bfloat16))
        s = s[:n] + s[n:]
        for t in range(TOKENS):
            tb = t * rows + b
            part = slice(i * n + t * GROUP, i * n + (t + 1) * GROUP)
            stats[g] = jnp.where(lane == 2 * tb, peak[part], stats[g])
            stats[g] = jnp.where(lane == 2 * tb + 1, total[part], stats[g])
            block = s[t * GROUP : (t + 1) * GROUP]
            if hb >= GROUP:
                at = g * GROUP
                packed[at // hb, tb, at % hb : at % hb + GROUP] = block
            else:
                for j in range(GROUP // hb):
                    packed[g * (GROUP // hb) + j, tb] = block[j * hb : (j + 1) * hb]
    for g in range(heads):
        if hb >= GROUP:
            at = g * GROUP
            packed[at // hb, TOKENS * rows, at % hb : at % hb + GROUP] = stats[g]
        else:
            for j in range(GROUP // hb):
                packed[g * (GROUP // hb) + j, TOKENS * rows] = stats[g][j * hb : (j + 1) * hb]
    for k in range(half):
        outs[k][...] = packed[jnp.bitwise_xor(column % half, k)]


def combine_kernel(cols, *refs):
    parts, out = refs[:cols], refs[cols]
    cells = parts[0].shape[0] - 1
    hb = parts[0].shape[1]
    stats = [p[cells] for p in parts]
    attended = []
    for tb in range(cells):
        peaks = [s[:, 2 * tb : 2 * tb + 1] for s in stats]
        totals = [s[:, 2 * tb + 1 : 2 * tb + 2] for s in stats]
        top = functools.reduce(jnp.maximum, peaks)
        scales = [jnp.exp(p - top) for p in peaks]
        total = tree_sum([t * s for t, s in zip(totals, scales)])
        summed = tree_sum([p[tb] * s for p, s in zip(parts, scales)])
        attended.append(summed / total)
    rows = [
        jnp.concatenate([attended[tb][h : h + 1] for tb in range(cells)], axis=0) for h in range(hb)
    ]
    out[...] = jnp.concatenate(rows, axis=1).astype(out.dtype)


def group_order(value, groups):
    here = value.shape[1] // groups
    return jnp.concatenate(
        [value[t, r * here : (r + 1) * here] for r in range(groups) for t in range(TOKENS)], axis=0
    )


def canonical(parts, canon, me):
    cells = parts[0].shape[0]
    for k, part in enumerate(parts):
        canon[jnp.bitwise_xor(me, k), :cells] = part[...].astype(jnp.float32)
    rows = [canon[r, :cells] for r in range(len(parts))]
    return jnp.concatenate(rows, axis=0).astype(jnp.bfloat16)


def over_columns(width, body):
    size = width

    def step(j, carry):
        body(pl.multiple_of(j * size, 128), size)
        return carry

    lax.fori_loop(0, width // size, step, 0)


def across(count):
    return [0, *range(count - 1, 0, -1)]


def by_distance(refs):
    order = across(len(refs))
    return [refs[order.index(k)] for k in range(len(refs))]


def out_kernel(groups, *refs):
    parts, (weight, *outs) = refs[:groups], refs[groups:-3]
    canon, attended, packed = refs[-3:]
    half = packed.shape[2]
    attended[...] = canonical(parts, canon, lax.axis_index("row"))
    for i in range(2):
        packed[i] = dot(attended[...], weight[:, i * half : (i + 1) * half])
    bit = lax.axis_index("col") & 1
    for k, out in enumerate(outs):
        out[...] = packed[jnp.bitwise_xor(bit, k & 1)].astype(out.dtype)


def in_pieces(squares):
    first = squares.astype(WIRE).astype(jnp.float32)
    second = (squares - first).astype(WIRE).astype(jnp.float32)
    third = squares - first - second
    lane = lax.broadcasted_iota(jnp.int32, (squares.shape[0], HD), 1)
    return jnp.where(
        lane == 0, first, jnp.where(lane == 1, second, jnp.where(lane == 2, third, 0.0))
    )


def lanes_of(bit, half):
    return pl.ds(pl.multiple_of(bit * half, 128), half)


def mid_kernel(groups, residual, gains, *refs):
    parts, (mid, lifted) = by_distance(refs[:-2]), refs[-2:]
    half = mid.shape[1]
    here = lanes_of(lax.axis_index("col") & 1, half)
    own = residual[:, :, here].astype(jnp.float32)
    value = group_order(own, groups) + tree_sum([p[...].astype(jnp.float32) for p in parts])
    mid[...] = value
    lifted[...] = (value * gains[here].astype(jnp.float32).reshape(1, half)).astype(jnp.bfloat16)


def products(lifted, bit, gate_weight, up_weight, out_hidden):
    half = lifted.shape[1]
    start = 0
    if gate_weight.shape[1] > out_hidden:
        start = pl.multiple_of(lax.axis_index("side") * out_hidden, 128)
    rows, columns = lanes_of(bit, half), pl.ds(start, out_hidden)
    return dot(lifted, gate_weight[rows, columns]), dot(lifted, up_weight[rows, columns])


def lift_first_kernel(lifted, gate_weight, up_weight, gate, up):
    bit = lax.axis_index("col") & 1
    gate[...], up[...] = products(lifted[...], bit, gate_weight, up_weight, gate.shape[1])


def lift_second_kernel(
    own, received, gains, gate_weight, up_weight, gate_first, up_first, mid, keep, send, packed
):
    rows, hidden = gate_first.shape
    half, bit = rows // 2, lax.axis_index("col") & 1
    width = own.shape[1]
    mid[:, lanes_of(bit, width)] = own[...]
    mid[:, lanes_of(1 - bit, width)] = received[...]
    value = received[...]
    squares = own[...] * own[...] + value * value
    sent = in_pieces(jnp.sum(squares, axis=1, keepdims=True))
    gain = gains[lanes_of(1 - bit, width)].astype(jnp.float32).reshape(1, width)
    lifted = (value * gain).astype(jnp.bfloat16)
    gate, up = products(lifted, 1 - bit, gate_weight, up_weight, hidden)
    gate, up = gate + gate_first[...], up + up_first[...]
    for i in range(2):
        part = slice(i * half, (i + 1) * half)
        packed[i, :, hidden:] = jnp.concatenate([sent[part], sent[part]], axis=0)
        packed[i, :, :hidden] = jnp.concatenate([gate[part], up[part]], axis=0)
    bit = lax.axis_index("row") & 1
    keep[...] = packed[bit].astype(keep.dtype)
    send[...] = packed[1 - bit].astype(send.dtype)


def act_kernel(model, *refs):
    parts, out = refs[:-1], refs[-1]
    hidden = parts[0].shape[1] - HD
    cells = parts[0].shape[0] // 2
    values = [p[...].astype(jnp.float32) for p in parts]
    total = tree_sum(values[0::2]) + tree_sum(values[1::2])
    squares = jnp.sum(total[:cells, hidden:], axis=1, keepdims=True)
    inv = lax.rsqrt(squares / model + 1e-05)
    gate = total[:cells, :hidden] * inv
    up = total[cells:, :hidden] * inv
    out[...] = (gate / (1.0 + jnp.exp(-gate)) * up).astype(out.dtype)


def gather_kernel(own, received, out, packed):
    bit = lax.axis_index("row") & 1
    packed[bit] = own[...].astype(jnp.float32)
    packed[1 - bit] = received[...].astype(jnp.float32)
    out[...] = jnp.concatenate([packed[0], packed[1]], axis=0).astype(out.dtype)


def down_kernel(other, act, weight, *refs):
    out = refs[-1]
    hidden = act.shape[1]
    start = 0
    if weight.shape[0] > hidden:
        start = pl.multiple_of(jnp.bitwise_xor(lax.axis_index("side"), other) * hidden, 128)

    def body(at, size):
        product = dot(act[...], weight[pl.ds(start, hidden), pl.ds(at, size)])
        if len(refs) > 1:
            product = product + refs[0][:, pl.ds(at, size)]
        out[:, pl.ds(at, size)] = product.astype(out.dtype)

    over_columns(out.shape[1], body)


def down_half_kernel(other, flip, act, weight, *refs):
    first, out = refs[:-1], refs[-1]
    hidden, half = act.shape[1], out.shape[1]
    start = 0
    if weight.shape[0] > hidden:
        start = pl.multiple_of(jnp.bitwise_xor(lax.axis_index("side"), other) * hidden, 128)
    lanes = lanes_of(jnp.bitwise_xor(lax.axis_index("col") & 1, flip), half)
    product = dot(act[...], weight[pl.ds(start, hidden), lanes])
    for ref in first:
        product = product + ref[:, lanes]
    out[...] = product.astype(out.dtype)


def add_kernel(first, second, out):
    out[...] = (first[...].astype(jnp.float32) + second[...].astype(jnp.float32)).astype(out.dtype)


def final_kernel(groups, mid, *refs):
    parts, out = refs[:-1], refs[-1]
    half = parts[0].shape[1]
    bit = lax.axis_index("col") & 1
    here = out.shape[1] // groups
    parts = [p[...].astype(jnp.float32) for p in parts]
    for i in range(2):
        lanes = lanes_of(jnp.bitwise_xor(bit, i), half)
        total = mid[:, lanes] + tree_sum(parts[i::2])
        for t in range(TOKENS):
            block = [
                total[(r * TOKENS + t) * here : (r * TOKENS + t + 1) * here] for r in range(groups)
            ]
            out[t, :, lanes] = jnp.concatenate(block, axis=0).astype(out.dtype)


def shards(
    query,
    new_keys,
    new_values,
    key_cache,
    value_cache,
    lengths,
    residual,
    out_weight,
    norm_gain,
    gate_weight,
    up_weight,
    down_weight,
):
    sides, groups, cols = (lax.axis_size(a) for a in ("side", "row", "col"))
    rows_here = key_cache.shape[0]
    total_rows = residual.shape[1]
    width_share = residual.shape[2]
    hidden_share = gate_weight.shape[1]
    features = out_weight.shape[0]
    model = width_share * groups
    m = TOKENS * total_rows
    cells = TOKENS * rows_here
    hb = HEADS // cols
    split = 2 if sides == 2 and (hidden_share // 2) % 128 == 0 else 1
    hidden = hidden_share // split
    f32, bf16 = jnp.float32, jnp.bfloat16
    shape = jax.ShapeDtypeStruct
    pad = -(-cells // 8) * 8

    sources = [query, new_keys, new_values, key_cache, value_cache]
    message = shape((cells + 1, hb, HD), f32)
    sources = [query, new_keys, new_values, key_cache, value_cache]

    inputs = [pltpu.VMEM(a.shape, a.dtype) for a in sources]
    packed = pltpu.VMEM((cols // 2, *message.shape), f32)
    result = call(
        functools.partial(attention_far_kernel, cols),
        [message] * (cols // 2) + inputs + [pltpu.VMEM((8, HD), jnp.int32)],
        [ANY_SPEC] * 6,
        [pltpu.SMEM(lengths.shape, lengths.dtype), packed, pltpu.SemaphoreType.DMA((6,))],
        name="attention_far",
    )(*[in_hbm(a) for a in [*sources, lengths]])
    far, inputs = result[: cols // 2], result[cols // 2 :]
    far = [partner(far[k], "col", cols // 2 + k) for k in range(cols // 2)]
    near = call(
        functools.partial(attention_near_kernel, cols),
        [message] * (cols // 2),
        [VMEM_SPEC] * 6,
        [packed],
        name="attention_near",
    )(*[in_vmem(a) for a in inputs])
    parts = far + [near[0]] + [partner(near[k], "col", k) for k in range(1, cols // 2)]
    attended = call(
        functools.partial(combine_kernel, cols),
        shape((cells, features), bf16),
        [VMEM_SPEC] * cols,
        flops=40 * 10**9,
        name="combine",
    )(*parts)
    gathered = spread(attended, "row")
    half = width_share // 2
    partials = call(
        functools.partial(out_kernel, groups),
        [shape((m, half), WIRE)] * cols,
        [VMEM_SPEC] * (groups + 1),
        [
            pltpu.VMEM((groups, pad, features), f32),
            pltpu.VMEM((m, features), bf16),
            pltpu.VMEM((2, m, half), f32),
        ],
        name="out_projection",
    )(*gathered, in_vmem(out_weight))
    partials = [partials[0]] + [partner(partials[k], "col", k) for k in range(1, cols)]
    norm_gain = in_vmem(norm_gain)
    own, own_lifted = call(
        functools.partial(mid_kernel, groups),
        [shape((m, half), f32), shape((m, half), bf16)],
        [VMEM_SPEC] * (cols + 2),
        name="mid",
    )(in_vmem(residual), norm_gain, *[partials[k] for k in across(cols)])
    received = partner(own, "col", 1)
    weights = [in_vmem(gate_weight), in_vmem(up_weight)]
    first = call(
        lift_first_kernel,
        [shape((m, hidden), f32)] * 2,
        [VMEM_SPEC] * 3,
        name="gate_up_first",
    )(own_lifted, *weights)
    mid, keep, send = call(
        lift_second_kernel,
        [shape((m, width_share), f32)] + [shape((m, hidden + HD), WIRE)] * 2,
        [VMEM_SPEC] * 7,
        [pltpu.VMEM((2, m, hidden + HD), f32)],
        flops=40 * 10**9,
        name="gate_up_second",
    )(own, received, norm_gain, *weights, *first)
    sums = [keep] + [partner((keep, send)[k % 2], "row", k) for k in range(1, groups)]
    act = call(
        functools.partial(act_kernel, model),
        shape((m // 2, hidden), bf16),
        [VMEM_SPEC] * groups,
        name="activation",
    )(*sums)
    down_weight = in_vmem(down_weight)

    def gather_act(own_rows, other_rows):
        return call(
            gather_kernel,
            shape((m, hidden), bf16),
            [VMEM_SPEC] * 2,
            [pltpu.VMEM((2, m // 2, hidden), f32)],
            name="gather_act",
        )(own_rows, other_rows)

    rows, first, other = gather_act(act, partner(act, "row", 1)), [], 0
    if split > 1:
        first, other = [
            call(
                functools.partial(down_kernel, 0),
                shape((m, width_share), f32),
                [VMEM_SPEC] * 2,
                name="down_first",
            )(rows, down_weight)
        ], 1
        far = partner(act, ("side", "row"), groups + 1)
        rows = gather_act(partner(act, "side", 1), far)

    def down_half(flip, result):
        return call(
            functools.partial(down_half_kernel, other, flip),
            shape((m, half), result),
            [VMEM_SPEC] * (2 + len(first)),
            name="down_theirs" if flip else "down_mine",
        )(rows, down_weight, *first)

    theirs = partner(down_half(1, WIRE), "col", 1)
    down = call(add_kernel, shape((m, half), WIRE), [VMEM_SPEC] * 2, name="down_add")(
        down_half(0, f32), theirs
    )
    return call(
        functools.partial(final_kernel, groups),
        shape((TOKENS, total_rows, width_share), bf16),
        [VMEM_SPEC] * (cols + 1),
        name="final",
    )(mid, *spread(down, "col"))


def solution(mesh):
    in_specs = (
        P(None, "row", None),
        P(None, "row", None),
        P(None, "row", None),
        P("row", "col", None),
        P("row", "col", None),
        P("row"),
        P(None, None, "row"),
        P("col", "row"),
        P("row"),
        P("row", "col"),
        P("row", "col"),
        P("col", "row"),
    )
    out_specs = P(None, None, "row")
    return jax.shard_map(shards, mesh=mesh, in_specs=in_specs, out_specs=out_specs, check_vma=False)
```

```python
import functools
import math

import jax
import jax.numpy as jnp
from jax import lax
from jax.experimental import pallas as pl
from jax.experimental.pallas import tpu as pltpu
from jax.sharding import PartitionSpec as P

HEADS = 32
KV_HEADS = 4
HD = 128
GROUP = HEADS // KV_HEADS
TOKENS = 2
very_low = -1e30
MIB = 1024 * 1024
WIRE = jnp.bfloat16
VMEM_SPEC = pl.BlockSpec(memory_space=pltpu.VMEM)
ANY_SPEC = pl.BlockSpec(memory_space=pl.ANY)


def partner(value, axis, k):
    return lax.ppermute(value, axis, [(i, i ^ k) for i in range(lax.axis_size(axis))])


def spread(piece, axis):
    return [piece] + [partner(piece, axis, k) for k in range(1, lax.axis_size(axis))]


def tree_sum(values):
    while len(values) > 1:
        values = [values[i] + values[i + 1] for i in range(0, len(values), 2)]
    return values[0]


def dot(a, b):
    return jnp.dot(a, b, preferred_element_type=jnp.float32)


def dot_t(a, b):
    return lax.dot_general(a, b, (((1,), (1,)), ((), ())), preferred_element_type=jnp.float32)


def pieces(value):
    first = value.astype(WIRE).astype(jnp.float32)
    second = (value - first).astype(WIRE).astype(jnp.float32)
    return first, second, value - first - second


def call(kernel, out_shape, in_specs, scratch=(), limit=4, name=None, flops=None, out_specs=None):
    cost = None
    if flops is not None:
        cost = pl.CostEstimate(flops=flops, bytes_accessed=1024, transcendentals=0)
    return pl.pallas_call(
        kernel,
        out_shape=out_shape,
        in_specs=in_specs,
        out_specs=out_specs or jax.tree.map(lambda _: VMEM_SPEC, out_shape),
        scratch_shapes=list(scratch),
        compiler_params=pltpu.CompilerParams(vmem_limit_bytes=limit * MIB),
        cost_estimate=cost,
        name=name,
    )


def in_hbm(value):
    return pltpu.with_memory_space_constraint(value, pltpu.HBM)


def in_vmem(value):
    return pltpu.with_memory_space_constraint(value, pltpu.VMEM)


def attention_far_kernel(cols, *refs):
    half = cols // 2
    sources, (lengths, *outs), kept = refs[:5], refs[5 : 6 + half], refs[6 + half : 12 + half]
    sized, packed, sems = refs[12 + half :]
    keys, values, small = [], [], [pltpu.make_async_copy(lengths, sized, sems.at[0])]
    for i, (source, target) in enumerate(zip(sources, kept)):
        if i < 3:
            small.append(pltpu.make_async_copy(source, target, sems.at[i + 1]))
            continue
        for b in range(source.shape[0]):
            sem = sems.at[4 + (i - 3) * source.shape[0] + b]
            copy = pltpu.make_async_copy(source.at[b], target.at[b], sem)
            (keys, values)[i - 3].append(copy)
    for copy in small[:2] + keys + small[2:] + values:
        copy.start()
    for copy in small + keys:
        copy.wait()

    def values_there():
        for copy in values:
            copy.wait()

    row = lax.broadcasted_iota(jnp.int32, (8, HD), 0)
    limits = jnp.zeros((8, HD), jnp.int32)
    for b in range(kept[3].shape[0]):
        limits = jnp.where(row == b, sized[b], limits)
    kept[5][...] = limits
    attention(cols, 1, limits, *kept[:5], outs, packed, values_there)


def attention_near_kernel(cols, *refs):
    attention(cols, 0, refs[5][...], *refs[:5], refs[6:-1], refs[-1], lambda: None)


def attention(
    cols, far, limits, query, new_keys, new_values, keys, values, outs, packed, values_there
):
    half = cols // 2
    heads = KV_HEADS // 2
    column = lax.axis_index("col")
    chosen = jnp.bitwise_xor(column // half, far)

    def lanes(source):
        width = source.shape[2] // 2
        return source[:, :, pl.ds(pl.multiple_of(chosen * width, 128), width)].astype(jnp.float32)

    def head(source, b, g):
        return source[b, :, pl.ds(pl.multiple_of((chosen * heads + g) * HD, 128), HD)]

    rows, span, _ = keys.shape
    hb = HEADS // cols
    inv_root = 1.0 / math.sqrt(HD)
    n = TOKENS * GROUP
    pairs = [(b, g) for b in range(rows) for g in range(heads)]
    q32, nk, nv = lanes(query), lanes(new_keys), lanes(new_values)
    zeros = jnp.zeros((8 - TOKENS, HD), jnp.float32)

    def fresh(block, b, g):
        lanes = slice(g * HD, (g + 1) * HD)
        return jnp.concatenate([block[t, b : b + 1, lanes] for t in range(TOKENS)] + [zeros], axis=0)

    scores, fresh_scores = [], []
    for b, g in pairs:
        q = jnp.concatenate(
            [
                q32[t, b : b + 1, (g * GROUP + h) * HD : (g * GROUP + h + 1) * HD]
                for t in range(TOKENS)
                for h in range(GROUP)
            ],
            axis=0,
        ).astype(jnp.bfloat16)
        s = dot_t(q, head(keys, b, g)) * inv_root
        position = column * span + lax.broadcasted_iota(jnp.int32, (n, span), 1)
        scores.append(jnp.where(position < limits[b : b + 1, :1], s, very_low))
        f = dot_t(q, fresh(nk, b, g).astype(jnp.bfloat16)) * inv_root
        token = lax.broadcasted_iota(jnp.int32, (n, 8), 0) // GROUP
        slot = lax.broadcasted_iota(jnp.int32, (n, 8), 1)
        seen = jnp.logical_and(slot <= token, column == 0)
        fresh_scores.append(jnp.where(seen, f, very_low))
    scores = jnp.concatenate(scores, axis=0)
    fresh_scores = jnp.concatenate(fresh_scores, axis=0)
    peak = jnp.maximum(
        jnp.max(scores, axis=1, keepdims=True), jnp.max(fresh_scores, axis=1, keepdims=True)
    )
    weights = jnp.where(scores > 0.5 * very_low, jnp.exp(scores - peak), 0.0)
    fresh_weights = jnp.where(fresh_scores > 0.5 * very_low, jnp.exp(fresh_scores - peak), 0.0)
    total = jnp.sum(weights, axis=1, keepdims=True) + jnp.sum(fresh_weights, axis=1, keepdims=True)

    def halves(w):
        high = w.astype(jnp.bfloat16)
        low = (w - high.astype(jnp.float32)).astype(jnp.bfloat16)
        return jnp.concatenate([high, low], axis=0)

    lane = lax.broadcasted_iota(jnp.int32, (GROUP, HD), 1)
    stats = [jnp.zeros((GROUP, HD), jnp.float32) for _ in range(heads)]
    values_there()
    for i, (b, g) in enumerate(pairs):
        here = slice(i * n, (i + 1) * n)
        s = dot(halves(weights[here]), head(values, b, g))
        s = s + dot(halves(fresh_weights[here]), fresh(nv, b, g).astype(jnp.bfloat16))
        s = s[:n] + s[n:]
        for t in range(TOKENS):
            tb = t * rows + b
            part = slice(i * n + t * GROUP, i * n + (t + 1) * GROUP)
            for k, pair in enumerate(zip(pieces(peak[part]), pieces(total[part]))):
                at = 2 * (TOKENS * rows * k + tb)
                stats[g] = jnp.where(lane == at, pair[0], stats[g])
                stats[g] = jnp.where(lane == at + 1, pair[1], stats[g])
            block = s[t * GROUP : (t + 1) * GROUP].astype(WIRE)
            if hb >= GROUP:
                at = g * GROUP
                packed[at // hb, tb, at % hb : at % hb + GROUP] = block
            else:
                for j in range(GROUP // hb):
                    packed[g * (GROUP // hb) + j, tb] = block[j * hb : (j + 1) * hb]
    stats = [block.astype(WIRE) for block in stats]
    for g in range(heads):
        if hb >= GROUP:
            at = g * GROUP
            packed[at // hb, TOKENS * rows, at % hb : at % hb + GROUP] = stats[g]
        else:
            for j in range(GROUP // hb):
                packed[g * (GROUP // hb) + j, TOKENS * rows] = stats[g][j * hb : (j + 1) * hb]
    for k in range(half):
        outs[k][...] = packed[jnp.bitwise_xor(column % half, k)]


def combine_kernel(cols, *refs):
    parts, out = refs[:cols], refs[cols]
    cells = parts[0].shape[0] - 1
    hb = parts[0].shape[1]
    n = 2 * cells
    stats = [p[cells].astype(jnp.float32) for p in parts]
    stats = [s[:, :n] + s[:, n : 2 * n] + s[:, 2 * n : 3 * n] for s in stats]
    attended = []
    for tb in range(cells):
        peaks = [s[:, 2 * tb : 2 * tb + 1] for s in stats]
        totals = [s[:, 2 * tb + 1 : 2 * tb + 2] for s in stats]
        top = functools.reduce(jnp.maximum, peaks)
        scales = [jnp.exp(p - top) for p in peaks]
        total = tree_sum([t * s for t, s in zip(totals, scales)])
        summed = tree_sum([p[tb].astype(jnp.float32) * s for p, s in zip(parts, scales)])
        attended.append(summed / total)
    rows = [
        jnp.concatenate([attended[tb][h : h + 1] for tb in range(cells)], axis=0) for h in range(hb)
    ]
    out[...] = jnp.concatenate(rows, axis=1).astype(out.dtype)


def group_order(value, groups):
    here = value.shape[1] // groups
    return jnp.concatenate(
        [value[t, r * here : (r + 1) * here] for r in range(groups) for t in range(TOKENS)], axis=0
    )


def canonical(parts, canon, me):
    cells = parts[0].shape[0]
    for k, part in enumerate(parts):
        canon[jnp.bitwise_xor(me, k), :cells] = part[...].astype(jnp.float32)
    rows = [canon[r, :cells] for r in range(len(parts))]
    return jnp.concatenate(rows, axis=0).astype(jnp.bfloat16)


def over_columns(width, body):
    size = width

    def step(j, carry):
        body(pl.multiple_of(j * size, 128), size)
        return carry

    lax.fori_loop(0, width // size, step, 0)


def across(count):
    return [0, *range(count - 1, 0, -1)]


def by_distance(refs):
    order = across(len(refs))
    return [refs[order.index(k)] for k in range(len(refs))]


def out_kernel(groups, *refs):
    parts, (weight, *outs) = refs[:groups], refs[groups:-3]
    canon, attended, packed = refs[-3:]
    half = packed.shape[2]
    attended[...] = canonical(parts, canon, lax.axis_index("row"))
    for i in range(2):
        packed[i] = dot(attended[...], weight[:, i * half : (i + 1) * half])
    bit = lax.axis_index("col") & 1
    for k, out in enumerate(outs):
        out[...] = packed[jnp.bitwise_xor(bit, k & 1)].astype(out.dtype)


def in_pieces(squares):
    lane = lax.broadcasted_iota(jnp.int32, (squares.shape[0], HD), 1)
    result = jnp.zeros(lane.shape, jnp.float32)
    for i, piece in enumerate(pieces(squares)):
        result = jnp.where(lane == i, piece, result)
    return result


def lanes_of(bit, half):
    return pl.ds(pl.multiple_of(bit * half, 128), half)


def mid_kernel(groups, residual, gains, *refs):
    parts, (mid, lifted) = by_distance(refs[:-2]), refs[-2:]
    half = mid.shape[1]
    here = lanes_of(lax.axis_index("col") & 1, half)
    own = residual[:, :, here].astype(jnp.float32)
    value = group_order(own, groups) + tree_sum([p[...].astype(jnp.float32) for p in parts])
    mid[...] = value
    lifted[...] = (value * gains[here].astype(jnp.float32).reshape(1, half)).astype(jnp.bfloat16)


def products(lifted, bit, gate_weight, up_weight, out_hidden):
    half = lifted.shape[1]
    start = 0
    if gate_weight.shape[1] > out_hidden:
        start = pl.multiple_of(lax.axis_index("side") * out_hidden, 128)
    rows, columns = lanes_of(bit, half), pl.ds(start, out_hidden)
    return dot(lifted, gate_weight[rows, columns]), dot(lifted, up_weight[rows, columns])


def lift_first_kernel(lifted, gate_weight, up_weight, gate, up):
    bit = lax.axis_index("col") & 1
    gate[...], up[...] = products(lifted[...], bit, gate_weight, up_weight, gate.shape[1])


def lift_second_kernel(
    own, received, gains, gate_weight, up_weight, gate_first, up_first, mid, keep, send, packed
):
    rows, hidden = gate_first.shape
    half, bit = rows // 2, lax.axis_index("col") & 1
    width = own.shape[1]
    mid[:, lanes_of(bit, width)] = own[...]
    mid[:, lanes_of(1 - bit, width)] = received[...]
    value = received[...]
    squares = own[...] * own[...] + value * value
    sent = in_pieces(jnp.sum(squares, axis=1, keepdims=True))
    gain = gains[lanes_of(1 - bit, width)].astype(jnp.float32).reshape(1, width)
    lifted = (value * gain).astype(jnp.bfloat16)
    gate, up = products(lifted, 1 - bit, gate_weight, up_weight, hidden)
    gate, up = gate + gate_first[...], up + up_first[...]
    for i in range(2):
        part = slice(i * half, (i + 1) * half)
        packed[i, :, hidden:] = jnp.concatenate([sent[part], sent[part]], axis=0)
        packed[i, :, :hidden] = jnp.concatenate([gate[part], up[part]], axis=0)
    bit = lax.axis_index("row") & 1
    keep[...] = packed[bit].astype(keep.dtype)
    send[...] = packed[1 - bit].astype(send.dtype)


def act_kernel(model, *refs):
    parts, out = refs[:-1], refs[-1]
    hidden = parts[0].shape[1] - HD
    cells = parts[0].shape[0] // 2
    values = [p[...].astype(jnp.float32) for p in parts]
    total = tree_sum(values[0::2]) + tree_sum(values[1::2])
    squares = jnp.sum(total[:cells, hidden:], axis=1, keepdims=True)
    inv = lax.rsqrt(squares / model + 1e-05)
    gate = total[:cells, :hidden] * inv
    up = total[cells:, :hidden] * inv
    out[...] = (gate / (1.0 + jnp.exp(-gate)) * up).astype(out.dtype)


def gather_kernel(own, received, out, packed):
    bit = lax.axis_index("row") & 1
    packed[bit] = own[...].astype(jnp.float32)
    packed[1 - bit] = received[...].astype(jnp.float32)
    out[...] = jnp.concatenate([packed[0], packed[1]], axis=0).astype(out.dtype)


def down_kernel(other, act, weight, *refs):
    out = refs[-1]
    hidden = act.shape[1]
    start = 0
    if weight.shape[0] > hidden:
        start = pl.multiple_of(jnp.bitwise_xor(lax.axis_index("side"), other) * hidden, 128)

    def body(at, size):
        product = dot(act[...], weight[pl.ds(start, hidden), pl.ds(at, size)])
        if len(refs) > 1:
            product = product + refs[0][:, pl.ds(at, size)]
        out[:, pl.ds(at, size)] = product.astype(out.dtype)

    over_columns(out.shape[1], body)


def final_kernel(groups, mid, *refs):
    parts, (out, held, sems) = refs[:-3], refs[-3:]
    total = mid[...] + tree_sum([p[...].astype(jnp.float32) for p in parts])
    here = out.shape[1] // groups
    copies = []
    for t in range(TOKENS):
        block = [
            total[(r * TOKENS + t) * here : (r * TOKENS + t + 1) * here] for r in range(groups)
        ]
        held[t] = jnp.concatenate(block, axis=0).astype(out.dtype)
        copies.append(pltpu.make_async_copy(held.at[t], out.at[t], sems.at[t]))
        copies[t].start()
    for copy in copies:
        copy.wait()


def shards(
    query,
    new_keys,
    new_values,
    key_cache,
    value_cache,
    lengths,
    residual,
    out_weight,
    norm_gain,
    gate_weight,
    up_weight,
    down_weight,
):
    sides, groups, cols = (lax.axis_size(a) for a in ("side", "row", "col"))
    rows_here = key_cache.shape[0]
    total_rows = residual.shape[1]
    width_share = residual.shape[2]
    hidden_share = gate_weight.shape[1]
    features = out_weight.shape[0]
    model = width_share * groups
    m = TOKENS * total_rows
    cells = TOKENS * rows_here
    hb = HEADS // cols
    split = 2 if sides == 2 and (hidden_share // 2) % 128 == 0 else 1
    hidden = hidden_share // split
    f32, bf16 = jnp.float32, jnp.bfloat16
    shape = jax.ShapeDtypeStruct
    pad = -(-cells // 8) * 8

    sources = [query, new_keys, new_values, key_cache, value_cache]
    message = shape((cells + 1, hb, HD), WIRE)
    sources = [query, new_keys, new_values, key_cache, value_cache]

    inputs = [pltpu.VMEM(a.shape, a.dtype) for a in sources]
    packed = pltpu.VMEM((cols // 2, *message.shape), WIRE)
    result = call(
        functools.partial(attention_far_kernel, cols),
        [message] * (cols // 2) + inputs + [pltpu.VMEM((8, HD), jnp.int32)],
        [ANY_SPEC] * 6,
        [
            pltpu.SMEM(lengths.shape, lengths.dtype),
            packed,
            pltpu.SemaphoreType.DMA((4 + 2 * rows_here,)),
        ],
        name="attention_far",
    )(*[in_hbm(a) for a in [*sources, lengths]])
    far, inputs = result[: cols // 2], result[cols // 2 :]
    far = [partner(far[k], "col", cols // 2 + k) for k in range(cols // 2)]
    near = call(
        functools.partial(attention_near_kernel, cols),
        [message] * (cols // 2),
        [VMEM_SPEC] * 6,
        [packed],
        name="attention_near",
    )(*[in_vmem(a) for a in inputs])
    parts = far + [near[0]] + [partner(near[k], "col", k) for k in range(1, cols // 2)]
    attended = call(
        functools.partial(combine_kernel, cols),
        shape((cells, features), bf16),
        [VMEM_SPEC] * cols,
        flops=40 * 10**9,
        name="combine",
    )(*parts)
    gathered = spread(attended, "row")
    half = width_share // 2
    partials = call(
        functools.partial(out_kernel, groups),
        [shape((m, half), WIRE)] * cols,
        [VMEM_SPEC] * (groups + 1),
        [
            pltpu.VMEM((groups, pad, features), f32),
            pltpu.VMEM((m, features), bf16),
            pltpu.VMEM((2, m, half), f32),
        ],
        name="out_projection",
    )(*gathered, in_vmem(out_weight))
    partials = [partials[0]] + [partner(partials[k], "col", k) for k in range(1, cols)]
    norm_gain = in_vmem(norm_gain)
    own, own_lifted = call(
        functools.partial(mid_kernel, groups),
        [shape((m, half), f32), shape((m, half), bf16)],
        [VMEM_SPEC] * (cols + 2),
        name="mid",
    )(in_vmem(residual), norm_gain, *[partials[k] for k in across(cols)])
    received = partner(own, "col", 1)
    weights = [in_vmem(gate_weight), in_vmem(up_weight)]
    first = call(
        lift_first_kernel,
        [shape((m, hidden), f32)] * 2,
        [VMEM_SPEC] * 3,
        name="gate_up_first",
    )(own_lifted, *weights)
    mid, keep, send = call(
        lift_second_kernel,
        [shape((m, width_share), f32)] + [shape((m, hidden + HD), WIRE)] * 2,
        [VMEM_SPEC] * 7,
        [pltpu.VMEM((2, m, hidden + HD), f32)],
        flops=40 * 10**9,
        name="gate_up_second",
    )(own, received, norm_gain, *weights, *first)
    sums = [keep] + [partner((keep, send)[k % 2], "row", k) for k in range(1, groups)]
    act = call(
        functools.partial(act_kernel, model),
        shape((m // 2, hidden), bf16),
        [VMEM_SPEC] * groups,
        name="activation",
    )(*sums)
    down_weight = in_vmem(down_weight)

    def down_part(same, from_row, other, before, result):
        rows = call(
            gather_kernel,
            shape((m, hidden), bf16),
            [VMEM_SPEC] * 2,
            [pltpu.VMEM((2, m // 2, hidden), f32)],
            name="gather_act",
        )(same, from_row)
        return call(
            functools.partial(down_kernel, other),
            shape((m, width_share), result),
            [VMEM_SPEC] * (2 + len(before)),
            name="down",
        )(rows, down_weight, *before)

    near = partner(act, "row", 1)
    if split > 1:
        first = down_part(act, near, 0, [], f32)
        far = partner(act, ("side", "row"), groups + 1)
        down = down_part(partner(act, "side", 1), far, 1, [first], WIRE)
    else:
        down = down_part(act, near, 0, [], WIRE)
    result = shape((TOKENS, total_rows, width_share), bf16)
    return call(
        functools.partial(final_kernel, groups),
        result,
        [VMEM_SPEC] * (cols + 1),
        [pltpu.VMEM(result.shape, bf16), pltpu.SemaphoreType.DMA((TOKENS,))],
        name="final",
        out_specs=ANY_SPEC,
    )(mid, *spread(down, "col"))


def solution(mesh):
    in_specs = (
        P(None, "row", None),
        P(None, "row", None),
        P(None, "row", None),
        P("row", "col", None),
        P("row", "col", None),
        P("row"),
        P(None, None, "row"),
        P("col", "row"),
        P("row"),
        P("row", "col"),
        P("row", "col"),
        P("col", "row"),
    )
    out_specs = P(None, None, "row")
    return jax.shard_map(shards, mesh=mesh, in_specs=in_specs, out_specs=out_specs, check_vma=False)
```
